32 devices in a mesh: clip: 4 (over y, x), row: 8 (over z, core).
Axes of the slice: x: 2, y: 2, z: 4, core: 2. Of those that a mesh axis runs over, the one named last changes fastest.
Arguments:
- frames: bfloat16 [16, 17, 3, 32, 64], P('clip', None, None, 'row'), may hold values from 0 to 1
- valid: int32 [16, 16, 32, 64], P('clip', None, 'row'), may hold values from 0 to 1
- flags: int32 [16, 16, 2], P('clip'), may hold values 0 or 1
- actions: float32 [16, 16, 4], P('clip'), may hold values from -4 to 4
- states: float32 [16, 16, 3], P('clip'), may hold values from -4 to 4
- latent: float32 [16, 8], P('clip'), may hold values from -4 to 4
- w_enc: float32 [75, 32], replicated, may hold values from -0.75 to 0.75
- w_lstm: float32 [1600, 128], replicated, may hold values from -0.15625 to 0.15625
- w_fc: float32 [16, 250, 1024], P('row'), may hold values from -0.1875 to 0.1875
- w_cond: float32 [15, 250], replicated, may hold values from -1.5 to 1.5
- w_deconv: float32 [32, 128], replicated, may hold values from -1 to 1
- w_mask: float32 [32, 11], replicated, may hold values from -2 to 2
- vector: float32 [517], replicated, may hold values from -1 to 2
- m_enc: float32 [75, 32], replicated, may hold values from -2.9802322e-07 to 2.9802322e-07
- m_lstm: float32 [1600, 128], replicated, may hold values from -2.9802322e-07 to 2.9802322e-07
- m_fc: float32 [16, 250, 1024], P('row'), may hold values from -2.9802322e-07 to 2.9802322e-07
- m_cond: float32 [15, 250], replicated, may hold values from -2.9802322e-07 to 2.9802322e-07
- m_deconv: float32 [32, 128], replicated, may hold values from -2.9802322e-07 to 2.9802322e-07
- m_mask: float32 [32, 11], replicated, may hold values from -2.9802322e-07 to 2.9802322e-07
- m_vector: float32 [517], replicated, may hold values from -1.1920929e-06 to 1.1920929e-06
- v_enc: float32 [75, 32], replicated, may hold values from 2.3191553e-16 to 9.276621e-16
- v_lstm: float32 [1600, 128], replicated, may hold values from 2.3191553e-16 to 9.276621e-16
- v_fc: float32 [16, 250, 1024], P('row'), may hold values from 2.3191553e-16 to 9.276621e-16
- v_cond: float32 [15, 250], replicated, may hold values from 2.3191553e-16 to 9.276621e-16
- v_deconv: float32 [32, 128], replicated, may hold values from 2.3191553e-16 to 9.276621e-16
- v_mask: float32 [32, 11], replicated, may hold values from 2.3191553e-16 to 9.276621e-16
- v_vector: float32 [517], replicated, may hold values from 3.7106485e-15 to 1.4842594e-14
Outputs:
- loss_sum: float32 [], replicated
- valid_count: float32 [], replicated
- grad_norm: float32 [], replicated
- new_enc: float32 [75, 32], replicated
- new_lstm: float32 [1600, 128], replicated
- new_fc: float32 [16, 250, 1024], P('row')
- new_cond: float32 [15, 250], replicated
- new_deconv: float32 [32, 128], replicated
- new_mask: float32 [32, 11], replicated
- new_vector: float32 [517], replicated
- first_enc: float32 [75, 32], replicated
- first_lstm: float32 [1600, 128], replicated
- first_fc: float32 [16, 250, 1024], P('row')
- first_cond: float32 [15, 250], replicated
- first_deconv: float32 [32, 128], replicated
- first_mask: float32 [32, 11], replicated
- first_vector: float32 [517], replicated
- second_enc: float32 [75, 32], replicated
- second_lstm: float32 [1600, 128], replicated
- second_fc: float32 [16, 250, 1024], P('row')
- second_cond: float32 [15, 250], replicated
- second_deconv: float32 [32, 128], replicated
- second_mask: float32 [32, 11], replicated
- second_vector: float32 [517], replicated
The draws below stay inside these ranges and needn't reach their ends.
All inputs are finite; a program needn't handle non-finite values. No bound on the sum of `flags` on one device may be relied on, other than what follows from the above.
Results may differ from the reference program's by a relative error of at most 0.0096.
Values may be sent and summed in bfloat16 or wider, within the bound.
No kernel may reach another device: no remote copies, remote signals or barrier semaphores. Data moves between devices by JAX's collectives and lax.ppermute only.
A program may use at most 128 MiB of HBM per device.

```python
import math
import jax
import jax.numpy as jnp
from jax import lax

C = 32
W = 64
KS = 5
NK = 10
ACT = 4
ST = 3
LAT = 8
STEPS = 16
STEP_NO = 10
KK = 25
NM = 11
COND = 15
CLIPS = 16
HB = 16
H = 32
WB = 32
NV = 517
PARAMS = 4311915


def draw_valid(key, part):
    key = jax.random.fold_in(key, 11)
    shape = (CLIPS, STEPS, H, W)
    numbers = jax.random.randint(key, shape, 0, 3000)
    height = lax.broadcasted_iota(jnp.int32, shape, 2)
    member = lax.broadcasted_iota(jnp.int32, shape, 0)
    limit = (250 + 500 * height // H) * (CLIPS + 2 * member) // CLIPS
    return (numbers < limit).astype(jnp.int32)


def draw_vector(key, part):
    key = jax.random.fold_in(key, 23)
    base = 0.3 * jax.random.truncated_normal(key, -3.0, 3.0, (NV,), jnp.float32)
    index = lax.broadcasted_iota(jnp.int32, (NV,), 0)
    gains = (index >= C) & (index < 2 * C)
    return jnp.where(gains, 1.0 + base, base)


def touch_ends(values, rng, least, top_value):
    shape = values.shape
    place = [jax.random.randint(jax.random.fold_in(rng, axis), (), 0, shape[axis]) for axis in range(len(shape))]
    values = values.at[tuple(place)].set(least)
    longest = shape.index(max(shape))
    place[longest] = (place[longest] + 1) % shape[longest]
    return values.at[tuple(place)].set(top_value)


def block_scale(own_key, extent, cuts, smallest, high):
    loudness, own = 1.0, jax.random.fold_in(own_key, 6)
    for axis_at, shards_of in cuts:
        heights = jnp.exp(jax.random.uniform(jax.random.fold_in(own, axis_at), (shards_of,), jnp.float32, smallest / len(cuts), high / len(cuts)))
        loudness = loudness * jnp.repeat(heights, extent[axis_at] // shards_of).reshape([-1 if axis == axis_at else 1 for axis in range(len(extent))])
    return loudness


def centred(own_key, shape, scale, most, cuts=(), kind=jnp.bfloat16):
    factor_of = block_scale(own_key, shape, cuts, -0.22, 0.18) if cuts else 1.0
    array = jax.random.normal(own_key, shape, jnp.float32) * scale * factor_of
    return jnp.minimum(jnp.maximum(array, -most), most).astype(kind)


def setup_inputs(seed: int = 0) -> dict:
    seeds = jax.random.split(jax.random.key(seed), 28)
    frames = jnp.clip(1.0 * jax.random.uniform(seeds[0], (CLIPS, STEPS + 1, 3, H, W), jnp.float32) ** block_scale(seeds[0], (CLIPS, STEPS + 1, 3, H, W), ((0, 4), (3, 8)), -0.2, 0.2), 0.0, 1.0).astype(jnp.bfloat16)
    valid = draw_valid(jax.random.fold_in(seeds[27], 71), 0)
    flags = touch_ends((jax.random.randint(seeds[2], (CLIPS, STEPS, 2), 0, 4) < 3).astype(jnp.int32), jax.random.fold_in(seeds[2], 1), 0, 1)
    actions = centred(seeds[3], (CLIPS, STEPS, ACT), 1.0, 4.0, ((0, 4),), jnp.float32)
    states = centred(seeds[4], (CLIPS, STEPS, ST), 1.0, 4.0, ((0, 4),), jnp.float32)
    latent = centred(seeds[5], (CLIPS, LAT), 1.0, 4.0, ((0, 4),), jnp.float32)
    w_enc = centred(seeds[6], (KK * 3, C), (KK * 3) ** -0.5, 0.75, (), jnp.float32)
    w_lstm = centred(seeds[7], (KK * 2 * C, 4 * C), (KK * 2 * C) ** -0.5, 0.15625, (), jnp.float32)
    w_fc = centred(seeds[8], (HB, NK * KK, WB * C), (HB * WB * C // 16) ** -0.5, 0.1875, ((0, 8),), jnp.float32)
    w_cond = centred(seeds[9], (COND, NK * KK), COND ** -0.5, 1.5, (), jnp.float32)
    w_deconv = centred(seeds[10], (C, 4 * C), C ** -0.5, 1.0, (), jnp.float32)
    w_mask = centred(seeds[11], (C, NM), (C // 4) ** -0.5, 2.0, (), jnp.float32)
    vector = draw_vector(jax.random.fold_in(seeds[27], 71), 0)
    m_enc = centred(seeds[13], (KK * 3, C), (0.000111 / PARAMS ** 0.5), 2.980232238769531e-07, (), jnp.float32)
    m_lstm = centred(seeds[14], (KK * 2 * C, 4 * C), (0.000111 / PARAMS ** 0.5), 2.980232238769531e-07, (), jnp.float32)
    m_fc = centred(seeds[15], (HB, NK * KK, WB * C), (0.000111 / PARAMS ** 0.5), 2.980232238769531e-07, ((0, 8),), jnp.float32)
    m_cond = centred(seeds[16], (COND, NK * KK), (0.000111 / PARAMS ** 0.5), 2.980232238769531e-07, (), jnp.float32)
    m_deconv = centred(seeds[17], (C, 4 * C), (0.000111 / PARAMS ** 0.5), 2.980232238769531e-07, (), jnp.float32)
    m_mask = centred(seeds[18], (C, NM), (0.000111 / PARAMS ** 0.5), 2.980232238769531e-07, (), jnp.float32)
    m_vector = centred(seeds[19], (NV,), (0.000444 / PARAMS ** 0.5), 1.1920928955078125e-06, (), jnp.float32)
    v_enc = jnp.clip(jnp.exp(jax.random.uniform(seeds[20], (KK * 3, C), jnp.float32, math.log(2.319155298456389e-16), math.log(9.276621193825556e-16))), 2.319155298456389e-16, 9.276621193825556e-16)
    v_lstm = jnp.clip(jnp.exp(jax.random.uniform(seeds[21], (KK * 2 * C, 4 * C), jnp.float32, math.log(2.319155298456389e-16), math.log(9.276621193825556e-16))), 2.319155298456389e-16, 9.276621193825556e-16)
    v_fc = jnp.clip(jnp.exp(math.log(9.276621193825556e-16) - 1.3862944 * jax.random.uniform(seeds[22], (HB, NK * KK, WB * C), jnp.float32) ** block_scale(seeds[22], (HB, NK * KK, WB * C), ((0, 8),), -0.2, 0.2)), 2.319155298456389e-16, 9.276621193825556e-16)
    v_cond = jnp.clip(jnp.exp(jax.random.uniform(seeds[23], (COND, NK * KK), jnp.float32, math.log(2.319155298456389e-16), math.log(9.276621193825556e-16))), 2.319155298456389e-16, 9.276621193825556e-16)
    v_deconv = jnp.clip(jnp.exp(jax.random.uniform(seeds[24], (C, 4 * C), jnp.float32, math.log(2.319155298456389e-16), math.log(9.276621193825556e-16))), 2.319155298456389e-16, 9.276621193825556e-16)
    v_mask = jnp.clip(jnp.exp(jax.random.uniform(seeds[25], (C, NM), jnp.float32, math.log(2.319155298456389e-16), math.log(9.276621193825556e-16))), 2.319155298456389e-16, 9.276621193825556e-16)
    v_vector = jnp.clip(jnp.exp(jax.random.uniform(seeds[26], (NV,), jnp.float32, math.log(3.710648477530222e-15), math.log(1.484259391012089e-14))), 3.710648477530222e-15, 1.484259391012089e-14)
    return dict(frames=frames, valid=valid, flags=flags, actions=actions, states=states, latent=latent, w_enc=w_enc, w_lstm=w_lstm, w_fc=w_fc, w_cond=w_cond, w_deconv=w_deconv, w_mask=w_mask, vector=vector, m_enc=m_enc, m_lstm=m_lstm, m_fc=m_fc, m_cond=m_cond, m_deconv=m_deconv, m_mask=m_mask, m_vector=m_vector, v_enc=v_enc, v_lstm=v_lstm, v_fc=v_fc, v_cond=v_cond, v_deconv=v_deconv, v_mask=v_mask, v_vector=v_vector)


NORM_EPS = 1e-05
CLIP_NORM = 0.001
BETA_ONE = 0.9
BETA_TWO = 0.999
ADAM_EPS = 1e-12
DECAY = 0.01
HIGH = lax.Precision.HIGHEST

@jax.custom_vjp
def low(v):
    return lax.optimization_barrier(v.astype(jnp.bfloat16)).astype(jnp.float32)

@jax.custom_vjp
def low_back(v):
    return v

def low_keep(v):
    return (low(v), None)

def low_pass(kept, grad):
    return (grad,)

def back_keep(v):
    return (v, None)

def back_low(kept, grad):
    return (low(grad),)
low.defvjp(low_keep, low_pass)
low_back.defvjp(back_keep, back_low)

def split_vector(vector):
    counts = [C, C, C, 4 * C, NK * KK, C, NM]
    pieces = []
    start = 0
    for count in counts:
        pieces.append(vector[start:start + count])
        start += count
    return pieces

def norm_act(pre, gain, shift):
    centered = pre - lax.optimization_barrier(jnp.mean(pre, -1, keepdims=True))
    scale = lax.rsqrt(lax.optimization_barrier(jnp.mean(centered * centered, -1, keepdims=True)) + NORM_EPS)
    return jax.nn.silu(centered * scale * gain + shift)

def cell_step(gates, cell):
    gate_in, gate_keep, gate_out, gate_new = jnp.split(gates, 4, axis=-1)
    new_cell = jax.nn.sigmoid(gate_keep + 1.0) * cell + jax.nn.sigmoid(gate_in) * jnp.tanh(gate_new)
    return (jax.nn.sigmoid(gate_out) * jnp.tanh(new_cell), new_cell)

def upsample(values):
    clips, rows_in, cols_in, depth = values.shape
    grid = values.reshape(clips, rows_in, cols_in, 2, 2, depth // 4)
    return jnp.transpose(grid, (0, 1, 3, 2, 4, 5)).reshape(clips, 2 * rows_in, 2 * cols_in, depth // 4)

def predict(logits, upper, w_mask, b_mask, prev_pad):
    clips = logits.shape[0]
    kernels = jax.nn.softmax(logits.reshape(clips, NK, KK), axis=-1)
    activated = jax.nn.silu(upper)
    blend = jax.nn.softmax(jnp.einsum('byxc,cm->byxm', activated, w_mask, precision=HIGH) + b_mask, axis=-1)
    mixing = jnp.einsum('byxk,bko->byxo', blend[..., 1:], kernels, precision=HIGH)
    height = prev_pad.shape[1] - 4
    breadth = prev_pad.shape[2] - 4
    result = blend[..., :1] * prev_pad[:, 2:2 + height, 2:2 + breadth, :]
    for offset in range(KK):
        top = offset // KS
        left = offset % KS
        result = result + mixing[..., offset:offset + 1] * prev_pad[:, top:top + height, left:left + breadth, :]
    return result

def convolve(image, kernel, stride):
    return lax.conv_general_dilated(image, kernel, (stride, stride), ((2, 2), (2, 2)), dimension_numbers=('NHWC', 'HWIO', 'NHWC'), precision=HIGH)

def learning_rates(rows_total):
    return [0.5 * (KK * 3) ** (-0.5), 0.5 * (KK * 2 * C) ** (-0.5), 0.5 * (rows_total * WB * C // 16) ** (-0.5), 0.5 * COND ** (-0.5), 0.5 * C ** (-0.5), 0.5 * (C // 4) ** (-0.5), 0.1]

def adam(weight, grad, first, second, rate):
    first = BETA_ONE * first + (1.0 - BETA_ONE) * grad
    second = BETA_TWO * second + (1.0 - BETA_TWO) * grad * grad
    update = first / (1.0 - BETA_ONE ** STEP_NO) / (jnp.sqrt(second / (1.0 - BETA_TWO ** STEP_NO)) + ADAM_EPS)
    return (weight - rate * (update + DECAY * weight), first, second)

def forward(weights, images, padded, valid_steps, conditions):
    w_enc, w_lstm, w_fc, w_cond, w_deconv, w_mask, vector = weights
    b_enc, g_enc, s_enc, b_lstm, b_fc, b_dec, b_mask = split_vector(vector)
    clips = images.shape[1]
    k_enc = low(w_enc).reshape(KS, KS, 3, C)
    k_lstm = low(w_lstm).reshape(KS, KS, 2 * C, 4 * C)
    k_fc = low(w_fc)
    k_dec = low(w_deconv)

    @jax.checkpoint
    def advance(carry, item):
        hidden, cell = carry
        image, image_pad, target, mask, cond = item
        pre = low_back(convolve(image, k_enc, 2)) + b_enc
        encoded = low(norm_act(pre, g_enc, s_enc))
        gates = low_back(convolve(jnp.concatenate([encoded, hidden], -1), k_lstm, 1)) + b_lstm
        new_hidden, cell = cell_step(gates, cell)
        hidden = low(new_hidden)
        summed = jnp.einsum('bjk,jnk->bn', hidden.reshape(clips, HB, WB * C), k_fc, precision=HIGH)
        logits = low_back(summed) + jnp.dot(cond, w_cond, precision=HIGH) + b_fc
        upper = low_back(jnp.einsum('byxc,cd->byxd', hidden, k_dec, precision=HIGH))
        upper = upsample(upper) + b_dec
        result = predict(logits, upper, w_mask, b_mask, image_pad)
        error = jnp.sum(mask * lax.optimization_barrier(jnp.sum((result - target) ** 2, -1)))
        return ((hidden, cell), error)
    zeros_state = jnp.zeros((clips, HB, WB, C), jnp.float32)
    _, errors = lax.scan(advance, (zeros_state, zeros_state), (images[:-1], padded[:-1], images[1:], valid_steps, conditions))
    return jnp.sum(errors)

def reference(frames, valid, flags, actions, states, latent, w_enc, w_lstm, w_fc, w_cond, w_deconv, w_mask, vector, m_enc, m_lstm, m_fc, m_cond, m_deconv, m_mask, m_vector, v_enc, v_lstm, v_fc, v_cond, v_deconv, v_mask, v_vector):
    images = jnp.transpose(frames.astype(jnp.float32), (1, 0, 3, 4, 2))
    padded = jnp.pad(images, ((0, 0), (0, 0), (2, 2), (2, 2), (0, 0)))
    valid_steps = jnp.transpose(valid.astype(jnp.float32), (1, 0, 2, 3))
    presence = flags.astype(jnp.float32)
    conditions = jnp.concatenate([actions * presence[..., :1], states * presence[..., 1:], jnp.broadcast_to(latent[:, None, :], (latent.shape[0], STEPS, LAT))], -1)
    conditions = jnp.transpose(conditions, (1, 0, 2))
    valid_count = jnp.sum(valid_steps)
    weights = (w_enc, w_lstm, w_fc, w_cond, w_deconv, w_mask, vector)

    def objective(params):
        total = forward(params, images, padded, valid_steps, conditions)
        return (total / valid_count, total)
    _, pullback, loss_sum = jax.vjp(objective, weights, has_aux=True)
    grads = pullback(jnp.float32(1.0))[0]
    squares = jnp.float32(0.0)
    for grad in grads:
        squares = squares + jnp.sum(grad * grad)
    grad_norm = jnp.sqrt(squares)
    factor = CLIP_NORM / jnp.maximum(grad_norm, CLIP_NORM)
    rates = learning_rates(HB)
    firsts = (m_enc, m_lstm, m_fc, m_cond, m_deconv, m_mask, m_vector)
    seconds = (v_enc, v_lstm, v_fc, v_cond, v_deconv, v_mask, v_vector)
    new = [adam(weights[index], grads[index] * factor, firsts[index], seconds[index], rates[index]) for index in range(7)]
    return (loss_sum, valid_count, grad_norm, new[0][0], new[1][0], new[2][0], new[3][0], new[4][0], new[5][0], new[6][0], new[0][1], new[1][1], new[2][1], new[3][1], new[4][1], new[5][1], new[6][1], new[0][2], new[1][2], new[2][2], new[3][2], new[4][2], new[5][2], new[6][2])
```

```python
import functools

import jax
import jax.numpy as jnp
import numpy as np
from jax import lax
from jax.experimental import pallas as pl
from jax.experimental.pallas import tpu as pltpu
from jax.sharding import PartitionSpec as P

C = 32
KS = 5
NK = 10
STEP_NO = 10
KK = 25
NM = 11
COND = 15
WB = 32


NORM_EPS = 1e-05
CLIP_NORM = 0.001
BETA_ONE = 0.9
BETA_TWO = 0.999
ADAM_EPS = 1e-12
DECAY = 0.01
HIGH = lax.Precision.HIGHEST


def padded_2(cells, sides, width):
    for axis, dim in sides:
        count = lax.axis_size(axis)
        ends = count - 1
        head = lax.slice_in_dim(cells, 0, width, axis=dim)
        tail = lax.slice_in_dim(cells, cells.shape[dim] - width, cells.shape[dim], axis=dim)
        cells = jnp.concatenate(
            [
                lax.ppermute(tail, axis, [(i, (i + 1) % count) for i in range(ends)]),
                cells,
                lax.ppermute(head, axis, [((i + 1) % count, i) for i in range(ends)]),
            ],
            axis=dim,
        )
    return cells


def passed_along(block, axis, distance):
    devices = range(lax.axis_size(axis))
    route = [(i - distance, i) for i in devices if i - distance in devices]
    return lax.ppermute(block, axis, route)


def split_vector(vector):
    counts = [C, C, C, 4 * C, NK * KK, C, NM]
    pieces = []
    start = 0
    for count in counts:
        pieces.append(vector[start : start + count])
        start += count
    return pieces


def norm_act(pre, gain, shift):
    centered = pre - jnp.mean(pre, -1, keepdims=True)
    scale = lax.rsqrt(jnp.mean(centered * centered, -1, keepdims=True) + NORM_EPS)
    return jax.nn.silu(centered * scale * gain + shift)


def cell_step(gates, cell):
    gate_in, gate_keep, gate_out, gate_new = jnp.split(gates, 4, axis=-1)
    new_cell = jax.nn.sigmoid(gate_keep + 1.0) * cell + jax.nn.sigmoid(gate_in) * jnp.tanh(gate_new)
    return (jax.nn.sigmoid(gate_out) * jnp.tanh(new_cell), new_cell)


def upsample(values):
    clips, rows_in, cols_in, depth = values.shape
    grid = values.reshape(clips, rows_in, cols_in, 2, 2, depth // 4)
    return jnp.transpose(grid, (0, 1, 3, 2, 4, 5)).reshape(
        clips, 2 * rows_in, 2 * cols_in, depth // 4
    )


def predict(logits, upper, w_mask, b_mask, prev_pad):
    clips = logits.shape[0]
    kernels = jax.nn.softmax(logits.reshape(clips, NK, KK), axis=-1)
    activated = jax.nn.silu(upper)
    blend = jax.nn.softmax(
        jnp.einsum("byxc,cm->byxm", activated, w_mask, precision=HIGH) + b_mask, axis=-1
    )
    mixing = jnp.einsum("byxk,bko->byxo", blend[..., 1:], kernels, precision=HIGH)
    height = prev_pad.shape[1] - 4
    breadth = prev_pad.shape[2] - 4
    result = blend[..., :1] * prev_pad[:, 2 : 2 + height, 2 : 2 + breadth, :]
    for offset in range(KK):
        top = offset // KS
        left = offset % KS
        result = (
            result
            + mixing[..., offset : offset + 1]
            * prev_pad[:, top : top + height, left : left + breadth, :]
        )
    return result


def patches(padded, stride, out_rows, out_cols):
    pieces = []
    for offset in range(KK):
        top = offset // KS
        left = offset % KS
        pieces.append(
            padded[
                :,
                top : top + stride * (out_rows - 1) + 1 : stride,
                left : left + stride * (out_cols - 1) + 1 : stride,
                :,
            ]
        )
    return jnp.concatenate(pieces, -1)


def unpatch(grads, shape, stride):

    def extract(padded):
        return patches(padded, stride, grads.shape[1], grads.shape[2])

    _, pullback = jax.vjp(extract, jnp.zeros(shape, jnp.float32))
    return pullback(grads)[0]


def product(left, right, form):
    return jnp.einsum(form, left, right, preferred_element_type=jnp.float32)


def learning_rates(rows_total):
    return [
        0.5 * (KK * 3) ** (-0.5),
        0.5 * (KK * 2 * C) ** (-0.5),
        0.5 * (rows_total * WB * C // 16) ** (-0.5),
        0.5 * COND ** (-0.5),
        0.5 * C ** (-0.5),
        0.5 * (C // 4) ** (-0.5),
        0.1,
    ]


def adam(weight, grad, first, second, rate):
    first = BETA_ONE * first + (1.0 - BETA_ONE) * grad
    second = BETA_TWO * second + (1.0 - BETA_TWO) * grad * grad
    update = (
        first
        / (1.0 - BETA_ONE**STEP_NO)
        / (jnp.sqrt(second / (1.0 - BETA_TWO**STEP_NO)) + ADAM_EPS)
    )
    return (weight - rate * (update + DECAY * weight), first, second)


def strips(
    frames,
    valid,
    flags,
    actions,
    states,
    latent,
    w_enc,
    w_lstm,
    w_fc,
    w_cond,
    w_deconv,
    w_mask,
    vector,
    m_enc,
    m_lstm,
    m_fc,
    m_cond,
    m_deconv,
    m_mask,
    m_vector,
    v_enc,
    v_lstm,
    v_fc,
    v_cond,
    v_deconv,
    v_mask,
    v_vector,
):
    clips = frames.shape[0]
    out_rows = frames.shape[3] // 2
    out_cols = frames.shape[4] // 2
    b_enc, g_enc, s_enc, b_lstm, b_fc, b_dec, b_mask = split_vector(vector)
    k_enc = w_enc.astype(jnp.bfloat16)
    k_lstm = w_lstm.astype(jnp.bfloat16)
    k_fc = w_fc.astype(jnp.bfloat16)
    k_dec = w_deconv.astype(jnp.bfloat16)
    images = jnp.transpose(frames, (1, 0, 3, 4, 2))
    padded = padded_2(images, (("row", 2),), 2)
    padded = jnp.pad(padded, ((0, 0), (0, 0), (0, 0), (2, 2), (0, 0)))
    valid_steps = jnp.transpose(valid.astype(jnp.float32), (1, 0, 2, 3))
    presence = flags.astype(jnp.float32)
    conditions = jnp.concatenate(
        [
            actions * presence[..., :1],
            states * presence[..., 1:],
            jnp.broadcast_to(latent[:, None, :], (clips, actions.shape[1], latent.shape[1])),
        ],
        -1,
    )
    conditions = jnp.transpose(conditions, (1, 0, 2))
    valid_count = lax.psum(jnp.sum(valid_steps), ("clip", "row"))
    inv_count = 1.0 / valid_count

    def advance(carry, image_pad):
        hidden, cell = carry
        pre = product(patches(image_pad, 2, out_rows, out_cols), k_enc, "byxk,kc->byxc") + b_enc
        encoded = norm_act(pre, g_enc, s_enc).astype(jnp.bfloat16)
        joined = jnp.concatenate([encoded, hidden], -1)
        joined_pad = padded_2(joined, (("row", 1),), 2)
        joined_pad = jnp.pad(joined_pad, ((0, 0), (0, 0), (2, 2), (0, 0)))
        gates = (
            product(patches(joined_pad, 1, out_rows, out_cols), k_lstm, "byxk,kg->byxg") + b_lstm
        )
        new_hidden, new_cell = cell_step(gates, cell)
        hidden_low = new_hidden.astype(jnp.bfloat16)
        part = product(hidden_low.reshape(clips, out_rows, -1), k_fc, "bjk,jnk->bn")
        part = lax.psum(part, "row")
        upper = product(hidden_low, k_dec, "byxc,cd->byxd")
        return ((hidden_low, new_cell), (pre, joined_pad, gates, cell, hidden_low, part, upper))

    start = (
        jnp.zeros((clips, out_rows, out_cols, C), jnp.bfloat16),
        jnp.zeros((clips, out_rows, out_cols, C), jnp.float32),
    )
    _, saved = lax.scan(advance, start, padded[:-1])
    pre_all, joined_all, gates_all, cells_all, hidden_all, summed_all, uppers = saved
    targets = images[1:].astype(jnp.float32)

    def local_head(item):
        summed_t, upper_t, image_pad, target, mask, cond = item

        def error_of(summed_t, upper_t, w_cond, w_mask, b_fc, b_dec, b_mask):
            logits = summed_t + jnp.dot(cond, w_cond, precision=HIGH) + b_fc
            upper_full = upsample(upper_t) + b_dec
            result = predict(logits, upper_full, w_mask, b_mask, image_pad.astype(jnp.float32))
            return jnp.sum(mask * jnp.sum((result - target) ** 2, -1))

        error, pullback = jax.vjp(error_of, summed_t, upper_t, w_cond, w_mask, b_fc, b_dec, b_mask)
        return (error, pullback(inv_count))

    head_inputs = (summed_all, uppers, padded[:-1], targets, valid_steps, conditions)

    def retreat(carry, item):
        (
            back_hidden,
            back_cell,
            acc_enc,
            acc_lstm,
            acc_dec,
            acc_benc,
            acc_genc,
            acc_senc,
            acc_blstm,
        ) = carry
        saved_t, head_t = item
        pre, joined_pad, gates, cell_prev, hidden_low, image_pad = saved_t
        error, pulled_t = local_head(head_t)
        d_sum = lax.psum(pulled_t[0], "row")
        d_upper = pulled_t[1]
        extra = (error, pulled_t[2:])
        d_sum_low = d_sum.astype(jnp.bfloat16)
        d_upper_low = d_upper.astype(jnp.bfloat16)
        acc_dec = acc_dec + product(hidden_low, d_upper_low, "byxc,byxd->cd")
        back = back_hidden + product(d_upper_low, k_dec, "byxd,cd->byxc")
        back = back + product(d_sum_low, k_fc, "bn,jnk->bjk").reshape(back_hidden.shape)
        _, cell_pull = jax.vjp(cell_step, gates, cell_prev)
        d_gates, back_cell = cell_pull((back, back_cell))
        d_gates_low = d_gates.astype(jnp.bfloat16)
        acc_blstm = acc_blstm + jnp.sum(d_gates, (0, 1, 2))
        acc_lstm = acc_lstm + product(
            patches(joined_pad, 1, out_rows, out_cols), d_gates_low, "byxk,byxg->kg"
        )
        d_pad = unpatch(product(d_gates_low, k_lstm, "byxg,kg->byxk"), joined_pad.shape, 1)[
            :, :, 2:-2, :
        ]
        from_below = passed_along(d_pad[:, :2], "row", -1)
        from_above = passed_along(d_pad[:, -2:], "row", 1)
        d_joined = d_pad[:, 2:-2].at[:, -2:].add(from_below).at[:, :2].add(from_above)
        _, norm_pull = jax.vjp(norm_act, pre, g_enc, s_enc)
        d_pre, d_gain, d_shift = norm_pull(d_joined[..., :C])
        acc_benc = acc_benc + jnp.sum(d_pre, (0, 1, 2))
        acc_genc = acc_genc + d_gain
        acc_senc = acc_senc + d_shift
        acc_enc = acc_enc + product(
            patches(image_pad, 2, out_rows, out_cols), d_pre.astype(jnp.bfloat16), "byxk,byxc->kc"
        )
        new_carry = (
            d_joined[..., C:],
            back_cell,
            acc_enc,
            acc_lstm,
            acc_dec,
            acc_benc,
            acc_genc,
            acc_senc,
            acc_blstm,
        )
        return (new_carry, (d_sum_low, extra))

    zeros_state = jnp.zeros((clips, out_rows, out_cols, C), jnp.float32)
    zeros_small = jnp.zeros((C,), jnp.float32)
    init = (
        zeros_state,
        zeros_state,
        jnp.zeros(w_enc.shape, jnp.float32),
        jnp.zeros(w_lstm.shape, jnp.float32),
        jnp.zeros(w_deconv.shape, jnp.float32),
        zeros_small,
        zeros_small,
        zeros_small,
        jnp.zeros((4 * C,), jnp.float32),
    )
    final, (d_sums_low, extra) = lax.scan(
        retreat,
        init,
        ((pre_all, joined_all, gates_all, cells_all, hidden_all, padded[:-1]), head_inputs),
        reverse=True,
    )
    error_sum = jnp.sum(extra[0])
    head_sums = [jnp.sum(grad, 0) for grad in extra[1]]
    acc_enc, acc_lstm, acc_dec, acc_benc, acc_genc, acc_senc, acc_blstm = final[2:]
    flat_hidden = hidden_all.reshape(hidden_all.shape[0], clips, out_rows, -1)
    d_fc = lax.psum(
        product(flat_hidden, d_sums_low, "tbjk,tbn->jnk").astype(jnp.bfloat16), "clip"
    ).astype(jnp.float32)
    fc_squares = jnp.sum(d_fc * d_fc) / lax.axis_size("clip")
    d_vector = jnp.concatenate(
        [acc_benc, acc_genc, acc_senc, acc_blstm, head_sums[2], head_sums[3], head_sums[4]]
    )
    d_enc, d_lstm, d_cond, d_dec, d_mask, d_vector, loss_sum, squares = lax.psum(
        (acc_enc, acc_lstm, head_sums[0], acc_dec, head_sums[1], d_vector, error_sum, fc_squares),
        ("clip", "row"),
    )
    grads = (d_enc, d_lstm, d_fc, d_cond, d_dec, d_mask, d_vector)
    for index in (0, 1, 3, 4, 5, 6):
        squares = squares + jnp.sum(grads[index] * grads[index])
    grad_norm = jnp.sqrt(squares)
    factor = CLIP_NORM / jnp.maximum(grad_norm, CLIP_NORM)
    rates = learning_rates(w_fc.shape[0] * lax.axis_size("row"))
    weights = (w_enc, w_lstm, w_fc, w_cond, w_deconv, w_mask, vector)
    firsts = (m_enc, m_lstm, m_fc, m_cond, m_deconv, m_mask, m_vector)
    seconds = (v_enc, v_lstm, v_fc, v_cond, v_deconv, v_mask, v_vector)
    new = [
        adam(weights[index], grads[index] * factor, firsts[index], seconds[index], rates[index])
        for index in range(7)
    ]
    return (
        loss_sum,
        valid_count,
        grad_norm,
        new[0][0],
        new[1][0],
        new[2][0],
        new[3][0],
        new[4][0],
        new[5][0],
        new[6][0],
        new[0][1],
        new[1][1],
        new[2][1],
        new[3][1],
        new[4][1],
        new[5][1],
        new[6][1],
        new[0][2],
        new[1][2],
        new[2][2],
        new[3][2],
        new[4][2],
        new[5][2],
        new[6][2],
    )


LANES = 128
TILES = 4
BANDS = 4
HALVES = 2
FAR = 1
WIN = 9 * 16
BF = jnp.bfloat16
F32 = jnp.float32
VMEM_BYTES = 56 * 1024 * 1024


def window_places():
    places = np.zeros((4, WIN, 32), np.float32)
    encoder = np.zeros((WIN, KK * 3), np.float32)
    for sub in range(4):
        for tap in range(KK):
            off_y = tap // KS - 2 + sub // 2
            off_x = tap % KS - 2 + sub % 2
            block = (off_y // 2 + 1) * 3 + off_x // 2 + 1
            base = block * 16 + (off_y % 2) * 8 + (off_x % 2) * 4
            for channel in range(3):
                places[sub, base + channel, tap] = 1.0
                if sub == 0:
                    encoder[base + channel, tap * 3 + channel] = 1.0
    return places, encoder


def lane_places():
    lane = lax.broadcasted_iota(jnp.int32, (8, LANES), 1)
    return lane % WB, lane // WB


def moved(tile, lanes, d_col, d_band):
    if d_col == 0 and d_band == 0:
        return tile
    col, band = lanes
    rows = tile.shape[0]
    shift = (-(WB * d_band + d_col)) % LANES
    rolled = pltpu.roll(tile.reshape(rows // 8, 8, LANES), shift, 2)
    keep = None
    for place, delta, count in ((col, d_col, WB), (band, d_band, BANDS)):
        if delta > 0:
            inside = place < count - delta
        elif delta < 0:
            inside = place >= -delta
        else:
            continue
        keep = inside if keep is None else keep & inside
    return jnp.where(keep[None], rolled, 0.0).reshape(rows, LANES)


def spread(tiles, lanes, reach, target, width, start):
    rows = tiles[0].shape[0]
    for index in range(TILES + 2 * reach):
        tile = index - reach
        for shift in range(2 * reach + 1):
            place = shift * width + start
            target[index, place : place + rows, :] = moved(
                tiles[tile % TILES], lanes, shift - reach, tile // TILES
            ).astype(target.dtype)


def stacked(ref, tile, count):
    rows = count * ref.shape[1]
    return jnp.concatenate(
        [ref[tile : tile + count].reshape(rows, LANES), ref[tile + 1 : tile + 1 + count].reshape(rows, LANES)],
        axis=1,
    )


def nn(left, right):
    return lax.dot_general(left, right, (((1,), (0,)), ((), ())), preferred_element_type=F32)


def nt(left, right):
    return lax.dot_general(left, right, (((1,), (1,)), ((), ())), preferred_element_type=F32)


def logistic(v):
    return 0.5 * jnp.tanh(0.5 * v) + 0.5


def image_tiles(x_ref, t):
    return [x_ref[t, tile].astype(F32) for tile in range(TILES)]


def block_swap(parts, band):
    swapped = []
    for out in range(BANDS):
        total = None
        for part in range(BANDS):
            shift = (WB * (part - out)) % LANES
            value = parts[part] if shift == 0 else pltpu.roll(parts[part], shift, 1)
            total = value if total is None else jnp.where(band == part, value, total)
        swapped.append(total)
    return swapped


def twice(tile):
    return jnp.concatenate([tile, tile], axis=1)


def forward_kernel(
    half_ref, x_ref, we_ref, wx_ref, wh_ref, bias_ref,
    enc_ref, hid_ref, act_ref, cell_ref, strip_ref,
    win_s, enc_s, hid_s, state_s,
):
    steps = enc_ref.shape[0]
    lanes = lane_places()

    def encode(t, _):
        spread(image_tiles(x_ref, t), lanes, 1, win_s, 16, 0)
        tiles = []
        for two in range(0, TILES, 2):
            pre = nn(we_ref[...], stacked(win_s, two, 3)) + twice(bias_ref[0:C])
            centered = pre - jnp.mean(pre, 0, keepdims=True)
            scale = lax.rsqrt(jnp.mean(centered * centered, 0, keepdims=True) + NORM_EPS)
            value = centered * scale * twice(bias_ref[C : 2 * C]) + twice(bias_ref[2 * C : 3 * C])
            value = (value * logistic(value)).astype(BF)
            for one in range(2):
                part = value[:, one * LANES : (one + 1) * LANES]
                enc_ref[t, two + one] = part
                tiles.append(part.astype(F32))
        spread(tiles, lanes, 2, enc_s, C, 0)
        for two in range(0, TILES, 2):
            gates = nn(wx_ref[...], stacked(enc_s, two, KS)) + twice(bias_ref[3 * C : 7 * C])
            for one in range(2):
                act_ref[t, two + one] = gates[:, one * LANES : (one + 1) * LANES]
        return 0

    lax.fori_loop(0, steps, encode, 0)
    hid_s[...] = jnp.zeros_like(hid_s)
    state_s[...] = jnp.zeros_like(state_s)

    def advance(t, _):
        hidden = []
        for two in range(0, TILES, 2):
            sums = nn(wh_ref[...], stacked(hid_s, two, KS))
            for one in range(2):
                tile = two + one
                gates = act_ref[t, tile] + sums[:, one * LANES : (one + 1) * LANES]
                gate_in = logistic(gates[0:C])
                gate_keep = logistic(gates[C : 2 * C] + 1.0)
                gate_out = logistic(gates[2 * C : 3 * C])
                gate_new = jnp.tanh(gates[3 * C : 4 * C])
                cell = gate_keep * state_s[tile] + gate_in * gate_new
                act_ref[t, tile, 0:C] = gate_in
                act_ref[t, tile, C : 2 * C] = gate_keep
                act_ref[t, tile, 2 * C : 3 * C] = gate_out
                act_ref[t, tile, 3 * C : 4 * C] = gate_new
                state_s[tile] = cell
                cell_ref[t, tile] = cell
                low = (gate_out * jnp.tanh(cell)).astype(BF)
                hid_ref[t, tile] = low
                hidden.append(low.astype(F32))
        spread(hidden, lanes, 2, hid_s, C, 0)
        return 0

    lax.fori_loop(0, steps, advance, 0)
    own = steps // HALVES
    base = half_ref[0] * own

    def to_strips(i, _):
        for pair in range(2):
            rows = []
            for low_row in range(2):
                tile = hid_ref[base + i, 2 * pair + low_row].astype(F32)
                rows.append(block_swap([tile[8 * q : 8 * q + 8] for q in range(4)], lanes[1]))
            for band in range(BANDS):
                strip_ref[2 * band + pair, i] = jnp.concatenate(
                    [rows[0][band], rows[1][band]], axis=0
                ).astype(BF)
        return 0

    lax.fori_loop(0, own, to_strips, 0)


def head_kernel(
    half_ref, x_ref, hid_ref, logit_ref, wd_ref, wdt_ref, wm_ref, wmt_ref, bias_ref, place_ref, placet_ref,
    back_ref, dlog_ref, dwd_ref, dwm_ref, sums_ref,
    win_s, dk_s,
):
    own = logit_ref.shape[0]
    base = half_ref[0] * own
    lanes = lane_places()
    dwd_ref[...] = jnp.zeros_like(dwd_ref)
    dwm_ref[...] = jnp.zeros_like(dwm_ref)
    sums_ref[...] = jnp.zeros_like(sums_ref)
    row8 = lax.broadcasted_iota(jnp.int32, (8, 2 * LANES), 0)
    color = (row8 % 4) != 3
    row16 = lax.broadcasted_iota(jnp.int32, (16, 32), 0)
    lane16 = lax.broadcasted_iota(jnp.int32, (16, 32), 1)

    def frame(i, _):
        t = base + i
        spread(image_tiles(x_ref, t), lanes, 1, win_s, 16, 0)
        logits = logit_ref[i]
        powers = jnp.exp(logits - jnp.max(logits, -1, keepdims=True))
        kernels = powers / jnp.sum(powers, -1, keepdims=True)
        kernels = jnp.where(row16 == 0, (lane16 == KK // 2).astype(F32), jnp.where(row16 <= NK, kernels, 0.0))
        kernels_low = kernels.astype(BF)
        dk_s[...] = jnp.zeros_like(dk_s)
        for two in range(0, TILES, 2):
            hidden = jnp.concatenate([hid_ref[t, two], hid_ref[t, two + 1]], axis=1)
            window = stacked(win_s, two, 3)
            upper = nn(wdt_ref[...], hidden) + twice(bias_ref[0 : 4 * C])
            gate = logistic(upper)
            active = (upper * gate).astype(BF)
            scores = nn(wm_ref[...], active) + twice(bias_ref[4 * C : 4 * C + 64])
            scores = scores.reshape(4, 16, 2 * LANES)
            powers = jnp.exp(scores - jnp.max(scores, 1, keepdims=True))
            masks = powers / jnp.sum(powers, 1, keepdims=True)
            after = jnp.concatenate([x_ref[t + 1, two], x_ref[t + 1, two + 1]], axis=1).astype(F32)
            d_scores = []
            for sub in range(4):
                mask_low = masks[sub].astype(BF)
                spots = nt(place_ref[sub], kernels_low).astype(BF)
                mixing = nn(spots, mask_low)
                both = jnp.sum((mixing * window).reshape(18, 8, 2 * LANES), 0)
                result = both + pltpu.roll(both, 4, 0)
                goal = after[(sub // 2) * 8 : (sub // 2) * 8 + 8]
                turned = pltpu.roll(goal, 4, 0)
                goal = jnp.where((row8 < 4) == (sub % 2 == 0), goal, turned)
                counted = goal[3:4]
                diff = jnp.where(color, result - goal, 0.0)
                weighted = diff * counted
                lost = weighted * diff
                sums_ref[192:200] += lost[:, :LANES] + lost[:, LANES:]
                d_result = 2.0 * weighted
                d_mix = (window.reshape(18, 8, 2 * LANES) * d_result[None]).reshape(WIN, 2 * LANES).astype(BF)
                spots_t = nn(kernels_low, placet_ref[sub]).astype(BF)
                d_mask = nn(spots_t, d_mix)
                d_spots = nt(mask_low, d_mix)
                dk_s[...] += lax.dot_general(
                    d_spots, place_ref[sub].astype(F32), (((1,), (0,)), ((), ())),
                    preferred_element_type=F32, precision=HIGH,
                )
                inner = jnp.sum(masks[sub] * d_mask, 0, keepdims=True)
                d_scores.append(masks[sub] * (d_mask - inner))
            d_score = jnp.concatenate(d_scores, axis=0)
            sums_ref[128:192] += d_score[:, :LANES] + d_score[:, LANES:]
            d_score_low = d_score.astype(BF)
            d_active = nn(wmt_ref[...], d_score_low)
            dwm_ref[...] += nt(active, d_score_low)
            d_upper = d_active * (gate * (1.0 + upper * (1.0 - gate)))
            sums_ref[0:128] += d_upper[:, :LANES] + d_upper[:, LANES:]
            d_upper_low = d_upper.astype(BF)
            dwd_ref[...] += nt(hidden, d_upper_low)
            back = nn(wd_ref[...], d_upper_low).astype(BF)
            for one in range(2):
                back_ref[i, two + one] = back[:, one * LANES : (one + 1) * LANES]
        d_kernels = dk_s[...]
        inner = jnp.sum(d_kernels * kernels, -1, keepdims=True)
        dlog_ref[i] = kernels * (d_kernels - inner)
        return 0

    lax.fori_loop(0, own, frame, 0)


def backward_kernel(
    half_ref, x_ref, enc_ref, hid_ref, act_ref, cell_ref, dec_ref, fc_ref, wb_ref, we_ref, bias_ref,
    dw_ref, dwe_ref, sums_ref,
    gate_s, keep_s, denc_s, back_s, state_s, win_s, join_s,
):
    steps = enc_ref.shape[0]
    own = steps // HALVES
    base = half_ref[0] * own
    lanes = lane_places()
    back_s[...] = jnp.zeros_like(back_s)
    state_s[...] = jnp.zeros_like(state_s)
    dw_ref[...] = jnp.zeros_like(dw_ref)
    dwe_ref[...] = jnp.zeros_like(dwe_ref)
    sums_ref[...] = jnp.zeros_like(sums_ref)

    def retreat(step, _):
        t = steps - 1 - step
        half = t // own
        inside = t % own
        mine = jnp.where(half == half_ref[0], 1.0, 0.0)
        earlier = jnp.maximum(t - 1, 0)
        started = jnp.where(t > 0, 1.0, 0.0)
        tiles = []
        for tile in range(TILES):
            pair = tile // 2
            low_row = tile % 2
            parts = [
                fc_ref[half, 2 * band + pair, inside].astype(F32)[8 * low_row : 8 * low_row + 8]
                for band in range(BANDS)
            ]
            from_fc = jnp.concatenate(block_swap(parts, lanes[1]), axis=0)
            back = back_s[tile] + from_fc + dec_ref[half, inside, tile].astype(F32)
            gate_in = act_ref[t, tile, 0:C]
            gate_keep = act_ref[t, tile, C : 2 * C]
            gate_out = act_ref[t, tile, 2 * C : 3 * C]
            gate_new = act_ref[t, tile, 3 * C : 4 * C]
            bent = jnp.tanh(cell_ref[t, tile])
            d_cell = state_s[tile] + back * gate_out * (1.0 - bent * bent)
            state_s[tile] = d_cell * gate_keep
            d_gates = jnp.concatenate(
                [
                    d_cell * gate_new * gate_in * (1.0 - gate_in),
                    d_cell * (cell_ref[earlier, tile] * started) * gate_keep * (1.0 - gate_keep),
                    back * bent * gate_out * (1.0 - gate_out),
                    d_cell * gate_in * (1.0 - gate_new * gate_new),
                ],
                axis=0,
            )
            sums_ref[3 * C : 7 * C] += d_gates * mine
            low = d_gates.astype(BF)
            keep_s[t, tile] = low
            tiles.append(low.astype(F32))
        for index in range(TILES + 4):
            tile = index - 2
            gate_s[index] = moved(tiles[tile % TILES], lanes, 0, tile // TILES).astype(BF)
        for two in range(0, TILES, 2):
            sums = nn(wb_ref[...], stacked(gate_s, two, KS))
            for one in range(2):
                part = sums[:, one * LANES : (one + 1) * LANES]
                total = None
                for shift in range(KS):
                    value = moved(part[shift * 2 * C : (shift + 1) * 2 * C], lanes, 2 - shift, 0)
                    total = value if total is None else total + value
                denc_s[t, two + one] = total[:C]
                back_s[two + one] = total[C:]
        return 0

    lax.fori_loop(0, steps, retreat, 0)

    def gather(i, _):
        t = base + i
        earlier = jnp.maximum(t - 1, 0)
        started = jnp.where(t > 0, 1.0, 0.0)
        spread([enc_ref[t, tile].astype(F32) for tile in range(TILES)], lanes, 2, join_s, 2 * C, 0)
        spread(
            [hid_ref[earlier, tile].astype(F32) * started for tile in range(TILES)], lanes, 2, join_s, 2 * C, C
        )
        spread(image_tiles(x_ref, t), lanes, 1, win_s, 16, 0)
        for two in range(0, TILES, 2):
            d_gates = jnp.concatenate([keep_s[t, two], keep_s[t, two + 1]], axis=1)
            dw_ref[...] += nt(stacked(join_s, two, KS), d_gates)
            window = stacked(win_s, two, 3)
            pre = nn(we_ref[...], window) + twice(bias_ref[0:C])
            centered = pre - jnp.mean(pre, 0, keepdims=True)
            scale = lax.rsqrt(jnp.mean(centered * centered, 0, keepdims=True) + NORM_EPS)
            normal = centered * scale
            gain = twice(bias_ref[C : 2 * C])
            value = normal * gain + twice(bias_ref[2 * C : 3 * C])
            gate = logistic(value)
            d_out = jnp.concatenate([denc_s[t, two], denc_s[t, two + 1]], axis=1)
            d_value = d_out * (gate * (1.0 + value * (1.0 - gate)))
            d_gain = d_value * normal
            d_normal = d_value * gain
            d_pre = scale * (
                d_normal
                - jnp.mean(d_normal, 0, keepdims=True)
                - normal * jnp.mean(d_normal * normal, 0, keepdims=True)
            )
            sums_ref[0:C] += d_pre[:, :LANES] + d_pre[:, LANES:]
            sums_ref[C : 2 * C] += d_gain[:, :LANES] + d_gain[:, LANES:]
            sums_ref[2 * C : 3 * C] += d_value[:, :LANES] + d_value[:, LANES:]
            dwe_ref[...] += nt(d_pre.astype(BF), window)
        return 0

    lax.fori_loop(0, own, gather, 0)


SMEM_SPEC = pl.BlockSpec(memory_space=pltpu.SMEM)
VMEM_SPEC = pl.BlockSpec(memory_space=pltpu.VMEM)


def call(kernel, outs, scratch, half, *operands):
    return pl.pallas_call(
        kernel,
        out_shape=[jax.ShapeDtypeStruct(shape, kind) for shape, kind in outs],
        in_specs=[SMEM_SPEC] + [VMEM_SPEC] * len(operands),
        out_specs=[VMEM_SPEC] * len(outs),
        scratch_shapes=[pltpu.VMEM(shape, kind) for shape, kind in scratch],
        compiler_params=pltpu.CompilerParams(vmem_limit_bytes=VMEM_BYTES),
    )(half, *operands)


def columns(values):
    return jnp.broadcast_to(values[:, None], (values.shape[0], LANES))


def pieces_to_clips(block):
    return lax.all_to_all(block, "row", 0, 0, tiled=True)


def whole_clips(
    frames, valid, flags, actions, states, latent,
    w_enc, w_lstm, w_fc, w_cond, w_deconv, w_mask, vector,
    m_enc, m_lstm, m_fc, m_cond, m_deconv, m_mask, m_vector,
    v_enc, v_lstm, v_fc, v_cond, v_deconv, v_mask, v_vector,
):
    clips, shots, _, strip_rows, width = frames.shape
    steps = shots - 1
    own = steps // HALVES
    count = lax.axis_size("row")
    place = lax.axis_index("row")
    clip = place // HALVES
    half = place % HALVES
    half_1 = half.reshape(1).astype(jnp.int32)
    b_enc, g_enc, s_enc, b_lstm, b_fc, b_dec, b_mask = split_vector(vector)
    k_enc = w_enc.astype(BF)
    k_lstm = w_lstm.astype(BF)
    k_dec = w_deconv.astype(BF)
    k_mask = w_mask.astype(BF)
    places, encoder = window_places()
    flagged = jnp.pad(valid.astype(BF), ((0, 0), (1, 0), (0, 0), (0, 0)))
    pieces = jnp.concatenate([frames, flagged[:, :, None]], axis=2)
    pieces = jnp.repeat(pieces, HALVES, axis=0)
    pieces = pieces_to_clips(pieces)
    grid = pieces.reshape(BANDS, 2, shots, 4, 2, 2, width // 2, 2)
    grid = jnp.transpose(grid, (2, 1, 4, 5, 7, 3, 0, 6))
    x = grid.reshape(shots, TILES, 16, LANES)

    wide_enc = jnp.einsum("rk,ko->or", jnp.asarray(encoder, BF), k_enc, preferred_element_type=F32).astype(BF)
    taps = k_lstm.reshape(KS, KS, 2, C, 4 * C)
    wx = taps[:, :, 0].reshape(KK * C, 4 * C).T
    wh = taps[:, :, 1].reshape(KK * C, 4 * C).T
    bias = columns(jnp.concatenate([b_enc, g_enc, s_enc, b_lstm]))
    cells = (steps, TILES, C, LANES)
    enc, hid, act, cell, strips_out = call(
        forward_kernel,
        [(cells, BF), (cells, BF), ((steps, TILES, 4 * C, LANES), F32), (cells, F32), ((count, own, 16, LANES), BF)],
        [((6, 48, LANES), BF), ((8, KS * C, LANES), BF), ((8, KS * C, LANES), BF), ((TILES, C, LANES), F32)],
        half_1, x, wide_enc, wx, wh, bias,
    )
    items = clips * steps
    strip_hid = pieces_to_clips(strips_out).reshape(items, 2, WB * C)
    k_fc = w_fc.astype(BF).reshape(2, NK * KK, WB, 4, 8)
    k_fc = jnp.transpose(k_fc, (0, 1, 4, 3, 2)).reshape(2, NK * KK, WB * C)
    parts = jnp.einsum("mjk,jnk->mn", strip_hid, k_fc, preferred_element_type=F32)
    summed = jnp.sum(pieces_to_clips(parts.reshape(count, own, NK * KK)), 0)
    presence = flags.astype(F32)
    conditions = jnp.concatenate(
        [
            actions * presence[..., :1],
            states * presence[..., 1:],
            jnp.broadcast_to(latent[:, None, :], (clips, steps, latent.shape[1])),
        ],
        -1,
    )
    cond = lax.dynamic_slice(conditions, (clip, half * own, 0), (1, own, COND))[0]
    logits = summed + (jnp.dot(cond, w_cond, precision=HIGH) + b_fc)
    logits = jnp.pad(
        logits.reshape(own, NK, KK), ((0, 0), (1, 5), (0, 32 - KK)), constant_values=-1e30
    )
    wdt = k_dec.T
    eye = jnp.eye(4, dtype=BF)
    pad_mask = jnp.pad(k_mask, ((0, 0), (0, 16 - NM)))
    wmt = jnp.einsum("ab,cm->acbm", eye, pad_mask).reshape(4 * C, 64)
    head_bias = columns(
        jnp.concatenate([jnp.tile(b_dec, 4), jnp.tile(jnp.pad(b_mask, (0, 16 - NM), constant_values=-1e30), 4)])
    )
    dec, d_logit, d_dec, d_mask_wide, head_sums = call(
        head_kernel,
        [
            ((own, TILES, C, LANES), BF), ((own, 16, 32), F32), ((C, 4 * C), F32), ((4 * C, 64), F32),
            ((200, LANES), F32),
        ],
        [((6, 48, LANES), F32), ((16, 32), F32)],
        half_1, x, hid, logits, k_dec, wdt, wmt.T, wmt, head_bias,
        jnp.asarray(places, BF), jnp.asarray(places.transpose(0, 2, 1), BF),
    )
    d_logit = d_logit[:, 1 : NK + 1, :KK].reshape(own, NK * KK)
    d_sum = lax.all_gather(d_logit.astype(BF), "row").reshape(items, NK * KK)
    back_fc = jnp.einsum("mn,jnk->mjk", d_sum, k_fc, preferred_element_type=F32).astype(BF)
    back_fc = pieces_to_clips(back_fc.reshape(count, own, 16, LANES))
    swap = [(index, index ^ 1) for index in range(count)]

    def in_order(block):
        other = lax.ppermute(block, "row", swap)
        return jnp.stack([jnp.where(half == 0, block, other), jnp.where(half == 0, other, block)])

    wb = jnp.transpose(k_lstm.reshape(KS, KS, 2 * C, 4 * C)[::-1], (1, 2, 0, 3)).reshape(KS * 2 * C, KS * 4 * C)
    d_lstm, d_enc_wide, sums = call(
        backward_kernel,
        [((KK * 2 * C, 4 * C), F32), ((C, WIN), F32), ((7 * C, LANES), F32)],
        [
            ((8, 4 * C, LANES), BF), ((steps, TILES, 4 * C, LANES), BF), (cells, F32), ((TILES, C, LANES), F32),
            ((TILES, C, LANES), F32), ((6, 48, LANES), BF), ((8, KS * 2 * C, LANES), BF),
        ],
        half_1, x, enc, hid, act, cell, in_order(dec), in_order(back_fc), wb, wide_enc, bias,
    )
    d_fc = jnp.einsum("mjk,mn->jnk", strip_hid, d_sum, preferred_element_type=F32).astype(BF)
    d_fc = jnp.transpose(d_fc.reshape(2, NK * KK, 8, 4, WB), (0, 1, 4, 3, 2)).reshape(2, NK * KK, WB * C)
    d_fc = lax.psum(d_fc, "clip").astype(F32)
    fc_squares = jnp.sum(d_fc * d_fc) / lax.axis_size("clip")

    d_enc = jnp.einsum("rk,or->ko", jnp.asarray(encoder, F32), d_enc_wide, precision=HIGH)
    d_cond = jnp.dot(cond.T, d_logit, precision=HIGH)
    d_mask = jnp.sum(jnp.stack([d_mask_wide[s * C : (s + 1) * C, s * 16 : s * 16 + NM] for s in range(4)]), 0)
    line_sums = jnp.sum(sums, 1)
    head_lines = jnp.sum(head_sums, 1)
    d_vector = jnp.concatenate(
        [
            line_sums,
            jnp.sum(d_logit, 0),
            jnp.sum(head_lines[:128].reshape(4, C), 0),
            jnp.sum(head_lines[128:192].reshape(4, 16), 0)[:NM],
        ]
    )
    loss_part = jnp.sum(head_lines[192:196])
    count_part = jnp.sum(valid.astype(F32))
    d_enc, d_lstm, d_cond, d_dec, d_mask, d_vector, loss_sum, squares, valid_count = lax.psum(
        (d_enc, d_lstm, d_cond, d_dec, d_mask, d_vector, loss_part, fc_squares, count_part), ("clip", "row")
    )
    inv_count = 1.0 / valid_count
    grads = (d_enc, d_lstm, d_fc, d_cond, d_dec, d_mask, d_vector)
    for index in (0, 1, 3, 4, 5, 6):
        squares = squares + jnp.sum(grads[index] * grads[index])
    grad_norm = jnp.sqrt(squares) * inv_count
    factor = inv_count * (CLIP_NORM / jnp.maximum(grad_norm, CLIP_NORM))
    rates = learning_rates(w_fc.shape[0] * count)
    weights = (w_enc, w_lstm, w_fc, w_cond, w_deconv, w_mask, vector)
    firsts = (m_enc, m_lstm, m_fc, m_cond, m_deconv, m_mask, m_vector)
    seconds = (v_enc, v_lstm, v_fc, v_cond, v_deconv, v_mask, v_vector)
    new = [
        adam(weights[index], grads[index] * factor, firsts[index], seconds[index], rates[index])
        for index in range(7)
    ]
    outs = [loss_sum, valid_count, grad_norm]
    for kind in range(3):
        outs.extend(new[index][kind] for index in range(7))
    return tuple(outs)


def shards(frames, *rest):
    clips, _, _, strip_rows, width = frames.shape
    count = lax.axis_size("row")
    one_clip = strip_rows * count // 2 == TILES * BANDS and width // 2 == WB
    if one_clip and clips * HALVES == count:
        return whole_clips(frames, *rest)
    return strips(frames, *rest)


def solution(mesh):
    placed = (
        P("clip", None, None, "row", None),
        P("clip", None, "row", None),
        P("clip", None, None),
        P("clip", None, None),
        P("clip", None, None),
        P("clip", None),
        P(),
        P(),
        P("row", None, None),
        P(),
        P(),
        P(),
        P(),
        P(),
        P(),
        P("row", None, None),
        P(),
        P(),
        P(),
        P(),
        P(),
        P(),
        P("row", None, None),
        P(),
        P(),
        P(),
        P(),
    )
    return jax.shard_map(
        shards,
        mesh=mesh,
        in_specs=placed,
        out_specs=(
            P(),
            P(),
            P(),
            P(),
            P(),
            P("row", None, None),
            P(),
            P(),
            P(),
            P(),
            P(),
            P(),
            P("row", None, None),
            P(),
            P(),
            P(),
            P(),
            P(),
            P(),
            P("row", None, None),
            P(),
            P(),
            P(),
            P(),
        ),
        check_vma=False,
    )
```

```python
import functools

import jax
import jax.numpy as jnp
import numpy as np
from jax import lax
from jax.experimental import pallas as pl
from jax.experimental.pallas import tpu as pltpu
from jax.sharding import PartitionSpec as P

C = 32
KS = 5
NK = 10
STEP_NO = 10
KK = 25
NM = 11
COND = 15
WB = 32


NORM_EPS = 1e-05
CLIP_NORM = 0.001
BETA_ONE = 0.9
BETA_TWO = 0.999
ADAM_EPS = 1e-12
DECAY = 0.01
HIGH = lax.Precision.HIGHEST


def padded_2(cells, sides, width):
    for axis, dim in sides:
        count = lax.axis_size(axis)
        ends = count - 1
        head = lax.slice_in_dim(cells, 0, width, axis=dim)
        tail = lax.slice_in_dim(cells, cells.shape[dim] - width, cells.shape[dim], axis=dim)
        cells = jnp.concatenate(
            [
                lax.ppermute(tail, axis, [(i, (i + 1) % count) for i in range(ends)]),
                cells,
                lax.ppermute(head, axis, [((i + 1) % count, i) for i in range(ends)]),
            ],
            axis=dim,
        )
    return cells


def passed_along(block, axis, distance):
    devices = range(lax.axis_size(axis))
    route = [(i - distance, i) for i in devices if i - distance in devices]
    return lax.ppermute(block, axis, route)


def split_vector(vector):
    counts = [C, C, C, 4 * C, NK * KK, C, NM]
    pieces = []
    start = 0
    for count in counts:
        pieces.append(vector[start : start + count])
        start += count
    return pieces


def norm_act(pre, gain, shift):
    centered = pre - jnp.mean(pre, -1, keepdims=True)
    scale = lax.rsqrt(jnp.mean(centered * centered, -1, keepdims=True) + NORM_EPS)
    return jax.nn.silu(centered * scale * gain + shift)


def cell_step(gates, cell):
    gate_in, gate_keep, gate_out, gate_new = jnp.split(gates, 4, axis=-1)
    new_cell = jax.nn.sigmoid(gate_keep + 1.0) * cell + jax.nn.sigmoid(gate_in) * jnp.tanh(gate_new)
    return (jax.nn.sigmoid(gate_out) * jnp.tanh(new_cell), new_cell)


def upsample(values):
    clips, rows_in, cols_in, depth = values.shape
    grid = values.reshape(clips, rows_in, cols_in, 2, 2, depth // 4)
    return jnp.transpose(grid, (0, 1, 3, 2, 4, 5)).reshape(
        clips, 2 * rows_in, 2 * cols_in, depth // 4
    )


def predict(logits, upper, w_mask, b_mask, prev_pad):
    clips = logits.shape[0]
    kernels = jax.nn.softmax(logits.reshape(clips, NK, KK), axis=-1)
    activated = jax.nn.silu(upper)
    blend = jax.nn.softmax(
        jnp.einsum("byxc,cm->byxm", activated, w_mask, precision=HIGH) + b_mask, axis=-1
    )
    mixing = jnp.einsum("byxk,bko->byxo", blend[..., 1:], kernels, precision=HIGH)
    height = prev_pad.shape[1] - 4
    breadth = prev_pad.shape[2] - 4
    result = blend[..., :1] * prev_pad[:, 2 : 2 + height, 2 : 2 + breadth, :]
    for offset in range(KK):
        top = offset // KS
        left = offset % KS
        result = (
            result
            + mixing[..., offset : offset + 1]
            * prev_pad[:, top : top + height, left : left + breadth, :]
        )
    return result


def patches(padded, stride, out_rows, out_cols):
    pieces = []
    for offset in range(KK):
        top = offset // KS
        left = offset % KS
        pieces.append(
            padded[
                :,
                top : top + stride * (out_rows - 1) + 1 : stride,
                left : left + stride * (out_cols - 1) + 1 : stride,
                :,
            ]
        )
    return jnp.concatenate(pieces, -1)


def unpatch(grads, shape, stride):

    def extract(padded):
        return patches(padded, stride, grads.shape[1], grads.shape[2])

    _, pullback = jax.vjp(extract, jnp.zeros(shape, jnp.float32))
    return pullback(grads)[0]


def product(left, right, form):
    return jnp.einsum(form, left, right, preferred_element_type=jnp.float32)


def learning_rates(rows_total):
    return [
        0.5 * (KK * 3) ** (-0.5),
        0.5 * (KK * 2 * C) ** (-0.5),
        0.5 * (rows_total * WB * C // 16) ** (-0.5),
        0.5 * COND ** (-0.5),
        0.5 * C ** (-0.5),
        0.5 * (C // 4) ** (-0.5),
        0.1,
    ]


def adam(weight, grad, first, second, rate):
    first = BETA_ONE * first + (1.0 - BETA_ONE) * grad
    second = BETA_TWO * second + (1.0 - BETA_TWO) * grad * grad
    update = (
        first
        / (1.0 - BETA_ONE**STEP_NO)
        / (jnp.sqrt(second / (1.0 - BETA_TWO**STEP_NO)) + ADAM_EPS)
    )
    return (weight - rate * (update + DECAY * weight), first, second)


def strips(
    frames,
    valid,
    flags,
    actions,
    states,
    latent,
    w_enc,
    w_lstm,
    w_fc,
    w_cond,
    w_deconv,
    w_mask,
    vector,
    m_enc,
    m_lstm,
    m_fc,
    m_cond,
    m_deconv,
    m_mask,
    m_vector,
    v_enc,
    v_lstm,
    v_fc,
    v_cond,
    v_deconv,
    v_mask,
    v_vector,
):
    clips = frames.shape[0]
    out_rows = frames.shape[3] // 2
    out_cols = frames.shape[4] // 2
    b_enc, g_enc, s_enc, b_lstm, b_fc, b_dec, b_mask = split_vector(vector)
    k_enc = w_enc.astype(jnp.bfloat16)
    k_lstm = w_lstm.astype(jnp.bfloat16)
    k_fc = w_fc.astype(jnp.bfloat16)
    k_dec = w_deconv.astype(jnp.bfloat16)
    images = jnp.transpose(frames, (1, 0, 3, 4, 2))
    padded = padded_2(images, (("row", 2),), 2)
    padded = jnp.pad(padded, ((0, 0), (0, 0), (0, 0), (2, 2), (0, 0)))
    valid_steps = jnp.transpose(valid.astype(jnp.float32), (1, 0, 2, 3))
    presence = flags.astype(jnp.float32)
    conditions = jnp.concatenate(
        [
            actions * presence[..., :1],
            states * presence[..., 1:],
            jnp.broadcast_to(latent[:, None, :], (clips, actions.shape[1], latent.shape[1])),
        ],
        -1,
    )
    conditions = jnp.transpose(conditions, (1, 0, 2))
    valid_count = lax.psum(jnp.sum(valid_steps), ("clip", "row"))
    inv_count = 1.0 / valid_count

    def advance(carry, image_pad):
        hidden, cell = carry
        pre = product(patches(image_pad, 2, out_rows, out_cols), k_enc, "byxk,kc->byxc") + b_enc
        encoded = norm_act(pre, g_enc, s_enc).astype(jnp.bfloat16)
        joined = jnp.concatenate([encoded, hidden], -1)
        joined_pad = padded_2(joined, (("row", 1),), 2)
        joined_pad = jnp.pad(joined_pad, ((0, 0), (0, 0), (2, 2), (0, 0)))
        gates = (
            product(patches(joined_pad, 1, out_rows, out_cols), k_lstm, "byxk,kg->byxg") + b_lstm
        )
        new_hidden, new_cell = cell_step(gates, cell)
        hidden_low = new_hidden.astype(jnp.bfloat16)
        part = product(hidden_low.reshape(clips, out_rows, -1), k_fc, "bjk,jnk->bn")
        part = lax.psum(part, "row")
        upper = product(hidden_low, k_dec, "byxc,cd->byxd")
        return ((hidden_low, new_cell), (pre, joined_pad, gates, cell, hidden_low, part, upper))

    start = (
        jnp.zeros((clips, out_rows, out_cols, C), jnp.bfloat16),
        jnp.zeros((clips, out_rows, out_cols, C), jnp.float32),
    )
    _, saved = lax.scan(advance, start, padded[:-1])
    pre_all, joined_all, gates_all, cells_all, hidden_all, summed_all, uppers = saved
    targets = images[1:].astype(jnp.float32)

    def local_head(item):
        summed_t, upper_t, image_pad, target, mask, cond = item

        def error_of(summed_t, upper_t, w_cond, w_mask, b_fc, b_dec, b_mask):
            logits = summed_t + jnp.dot(cond, w_cond, precision=HIGH) + b_fc
            upper_full = upsample(upper_t) + b_dec
            result = predict(logits, upper_full, w_mask, b_mask, image_pad.astype(jnp.float32))
            return jnp.sum(mask * jnp.sum((result - target) ** 2, -1))

        error, pullback = jax.vjp(error_of, summed_t, upper_t, w_cond, w_mask, b_fc, b_dec, b_mask)
        return (error, pullback(inv_count))

    head_inputs = (summed_all, uppers, padded[:-1], targets, valid_steps, conditions)

    def retreat(carry, item):
        (
            back_hidden,
            back_cell,
            acc_enc,
            acc_lstm,
            acc_dec,
            acc_benc,
            acc_genc,
            acc_senc,
            acc_blstm,
        ) = carry
        saved_t, head_t = item
        pre, joined_pad, gates, cell_prev, hidden_low, image_pad = saved_t
        error, pulled_t = local_head(head_t)
        d_sum = lax.psum(pulled_t[0], "row")
        d_upper = pulled_t[1]
        extra = (error, pulled_t[2:])
        d_sum_low = d_sum.astype(jnp.bfloat16)
        d_upper_low = d_upper.astype(jnp.bfloat16)
        acc_dec = acc_dec + product(hidden_low, d_upper_low, "byxc,byxd->cd")
        back = back_hidden + product(d_upper_low, k_dec, "byxd,cd->byxc")
        back = back + product(d_sum_low, k_fc, "bn,jnk->bjk").reshape(back_hidden.shape)
        _, cell_pull = jax.vjp(cell_step, gates, cell_prev)
        d_gates, back_cell = cell_pull((back, back_cell))
        d_gates_low = d_gates.astype(jnp.bfloat16)
        acc_blstm = acc_blstm + jnp.sum(d_gates, (0, 1, 2))
        acc_lstm = acc_lstm + product(
            patches(joined_pad, 1, out_rows, out_cols), d_gates_low, "byxk,byxg->kg"
        )
        d_pad = unpatch(product(d_gates_low, k_lstm, "byxg,kg->byxk"), joined_pad.shape, 1)[
            :, :, 2:-2, :
        ]
        from_below = passed_along(d_pad[:, :2], "row", -1)
        from_above = passed_along(d_pad[:, -2:], "row", 1)
        d_joined = d_pad[:, 2:-2].at[:, -2:].add(from_below).at[:, :2].add(from_above)
        _, norm_pull = jax.vjp(norm_act, pre, g_enc, s_enc)
        d_pre, d_gain, d_shift = norm_pull(d_joined[..., :C])
        acc_benc = acc_benc + jnp.sum(d_pre, (0, 1, 2))
        acc_genc = acc_genc + d_gain
        acc_senc = acc_senc + d_shift
        acc_enc = acc_enc + product(
            patches(image_pad, 2, out_rows, out_cols), d_pre.astype(jnp.bfloat16), "byxk,byxc->kc"
        )
        new_carry = (
            d_joined[..., C:],
            back_cell,
            acc_enc,
            acc_lstm,
            acc_dec,
            acc_benc,
            acc_genc,
            acc_senc,
            acc_blstm,
        )
        return (new_carry, (d_sum_low, extra))

    zeros_state = jnp.zeros((clips, out_rows, out_cols, C), jnp.float32)
    zeros_small = jnp.zeros((C,), jnp.float32)
    init = (
        zeros_state,
        zeros_state,
        jnp.zeros(w_enc.shape, jnp.float32),
        jnp.zeros(w_lstm.shape, jnp.float32),
        jnp.zeros(w_deconv.shape, jnp.float32),
        zeros_small,
        zeros_small,
        zeros_small,
        jnp.zeros((4 * C,), jnp.float32),
    )
    final, (d_sums_low, extra) = lax.scan(
        retreat,
        init,
        ((pre_all, joined_all, gates_all, cells_all, hidden_all, padded[:-1]), head_inputs),
        reverse=True,
    )
    error_sum = jnp.sum(extra[0])
    head_sums = [jnp.sum(grad, 0) for grad in extra[1]]
    acc_enc, acc_lstm, acc_dec, acc_benc, acc_genc, acc_senc, acc_blstm = final[2:]
    flat_hidden = hidden_all.reshape(hidden_all.shape[0], clips, out_rows, -1)
    d_fc = lax.psum(
        product(flat_hidden, d_sums_low, "tbjk,tbn->jnk").astype(jnp.bfloat16), "clip"
    ).astype(jnp.float32)
    fc_squares = jnp.sum(d_fc * d_fc) / lax.axis_size("clip")
    d_vector = jnp.concatenate(
        [acc_benc, acc_genc, acc_senc, acc_blstm, head_sums[2], head_sums[3], head_sums[4]]
    )
    d_enc, d_lstm, d_cond, d_dec, d_mask, d_vector, loss_sum, squares = lax.psum(
        (acc_enc, acc_lstm, head_sums[0], acc_dec, head_sums[1], d_vector, error_sum, fc_squares),
        ("clip", "row"),
    )
    grads = (d_enc, d_lstm, d_fc, d_cond, d_dec, d_mask, d_vector)
    for index in (0, 1, 3, 4, 5, 6):
        squares = squares + jnp.sum(grads[index] * grads[index])
    grad_norm = jnp.sqrt(squares)
    factor = CLIP_NORM / jnp.maximum(grad_norm, CLIP_NORM)
    rates = learning_rates(w_fc.shape[0] * lax.axis_size("row"))
    weights = (w_enc, w_lstm, w_fc, w_cond, w_deconv, w_mask, vector)
    firsts = (m_enc, m_lstm, m_fc, m_cond, m_deconv, m_mask, m_vector)
    seconds = (v_enc, v_lstm, v_fc, v_cond, v_deconv, v_mask, v_vector)
    new = [
        adam(weights[index], grads[index] * factor, firsts[index], seconds[index], rates[index])
        for index in range(7)
    ]
    return (
        loss_sum,
        valid_count,
        grad_norm,
        new[0][0],
        new[1][0],
        new[2][0],
        new[3][0],
        new[4][0],
        new[5][0],
        new[6][0],
        new[0][1],
        new[1][1],
        new[2][1],
        new[3][1],
        new[4][1],
        new[5][1],
        new[6][1],
        new[0][2],
        new[1][2],
        new[2][2],
        new[3][2],
        new[4][2],
        new[5][2],
        new[6][2],
    )


LANES = 128
TILES = 4
BANDS = 4
HALVES = 2
FAR = 1
WIN = 9 * 16
BF = jnp.bfloat16
F32 = jnp.float32
VMEM_BYTES = 56 * 1024 * 1024


def window_places():
    places = np.zeros((4, WIN, 32), np.float32)
    encoder = np.zeros((WIN, KK * 3), np.float32)
    for sub in range(4):
        for tap in range(KK):
            off_y = tap // KS - 2 + sub // 2
            off_x = tap % KS - 2 + sub % 2
            block = (off_y // 2 + 1) * 3 + off_x // 2 + 1
            base = block * 16 + (off_x % 2) * 8 + (off_y % 2) * 4
            for channel in range(3):
                places[sub, base + channel, tap] = 1.0
                if sub == 0:
                    encoder[base + channel, tap * 3 + channel] = 1.0
    return places, encoder


def lane_places():
    lane = lax.broadcasted_iota(jnp.int32, (8, LANES), 1)
    return lane % WB, lane // WB


def moved(tile, lanes, d_col, d_band):
    if d_col == 0 and d_band == 0:
        return tile
    col, band = lanes
    rows = tile.shape[0]
    shift = (-(WB * d_band + d_col)) % LANES
    rolled = pltpu.roll(tile.reshape(rows // 8, 8, LANES), shift, 2)
    keep = None
    for place, delta, count in ((col, d_col, WB), (band, d_band, BANDS)):
        if delta > 0:
            inside = place < count - delta
        elif delta < 0:
            inside = place >= -delta
        else:
            continue
        keep = inside if keep is None else keep & inside
    return jnp.where(keep[None], rolled, 0.0).reshape(rows, LANES)


def spread(tiles, lanes, reach, target, width, start):
    rows = tiles[0].shape[0]
    for index in range(TILES + 2 * reach):
        tile = index - reach
        for shift in range(2 * reach + 1):
            place = shift * width + start
            target[index, place : place + rows, :] = moved(
                tiles[tile % TILES], lanes, shift - reach, tile // TILES
            ).astype(target.dtype)


def stacked(ref, tile, count):
    rows = count * ref.shape[1]
    return jnp.concatenate(
        [ref[tile : tile + count].reshape(rows, LANES), ref[tile + 1 : tile + 1 + count].reshape(rows, LANES)],
        axis=1,
    )


def nn(left, right):
    return lax.dot_general(left, right, (((1,), (0,)), ((), ())), preferred_element_type=F32)


def nt(left, right):
    return lax.dot_general(left, right, (((1,), (1,)), ((), ())), preferred_element_type=F32)


def logistic(v):
    return 0.5 * jnp.tanh(0.5 * v) + 0.5


def one_hot_eye(size):
    row = lax.broadcasted_iota(jnp.int32, (size, size), 0)
    return (row == lax.broadcasted_iota(jnp.int32, (size, size), 1)).astype(BF)


def one_hot_mod(shape, period, axis):
    folded = lax.broadcasted_iota(jnp.int32, shape, axis) % period
    return (folded == lax.broadcasted_iota(jnp.int32, shape, 1 - axis)).astype(BF)


def unpack_images(raw_ref, x_ref):
    source = lax.broadcasted_iota(jnp.int32, (LANES, 4 * LANES), 0)
    goal = lax.broadcasted_iota(jnp.int32, (LANES, 4 * LANES), 1)
    same = (source // 64 == goal // 256) & (source % 2 == goal // LANES % 2) & (source // 2 % WB == goal % WB)
    picks = [(same & (goal // WB % BANDS == band)).astype(BF) for band in range(BANDS)]
    for pair in range(2):
        total = nn(raw_ref[pair], picks[0])
        for band in range(1, BANDS):
            total = total + nn(raw_ref[2 * band + pair], picks[band])
        for t in range(x_ref.shape[0]):
            rows = total[8 * t : 8 * t + 8]
            for low_row in range(2):
                start = 2 * LANES * low_row
                x_ref[t, 2 * pair + low_row] = jnp.concatenate(
                    [rows[:, start : start + LANES], rows[:, start + LANES : start + 2 * LANES]], axis=0
                ).astype(BF)


def image_tiles(x_ref, t):
    return [x_ref[t, tile].astype(F32) for tile in range(TILES)]


def block_swap(parts, band):
    swapped = []
    for out in range(BANDS):
        total = None
        for part in range(BANDS):
            shift = (WB * (part - out)) % LANES
            value = parts[part] if shift == 0 else pltpu.roll(parts[part], shift, 1)
            total = value if total is None else jnp.where(band == part, value, total)
        swapped.append(total)
    return swapped


def twice(tile):
    return jnp.concatenate([tile, tile], axis=1)


def forward_kernel(
    half_ref, raw_ref, we_ref, w_ref, bias_ref,
    x_ref, enc_ref, hid_ref, act_ref, cell_ref, strip_ref,
    win_s, enc_s, hid_s, state_s, rows_s, wx_s, wh_s,
):
    steps = enc_ref.shape[0]
    lanes = lane_places()
    for kind, target in ((0, wx_s), (1, wh_s)):
        for tap in range(KK):
            start = tap * 2 * C + kind * C
            rows_s[tap * C : (tap + 1) * C, :] = w_ref[start : start + C, :].astype(BF)
        target[...] = nt(one_hot_eye(4 * C), rows_s[...]).astype(BF)
    unpack_images(raw_ref, x_ref)

    def encode(t, _):
        spread(image_tiles(x_ref, t), lanes, 1, win_s, 16, 0)
        tiles = []
        for two in range(0, TILES, 2):
            pre = nn(we_ref[...], stacked(win_s, two, 3)) + twice(bias_ref[0:C])
            centered = pre - jnp.mean(pre, 0, keepdims=True)
            scale = lax.rsqrt(jnp.mean(centered * centered, 0, keepdims=True) + NORM_EPS)
            value = centered * scale * twice(bias_ref[C : 2 * C]) + twice(bias_ref[2 * C : 3 * C])
            value = (value * logistic(value)).astype(BF)
            for one in range(2):
                part = value[:, one * LANES : (one + 1) * LANES]
                enc_ref[t, two + one] = part
                tiles.append(part.astype(F32))
        spread(tiles, lanes, 2, enc_s, C, 0)
        for two in range(0, TILES, 2):
            gates = nn(wx_s[...], stacked(enc_s, two, KS)) + twice(bias_ref[3 * C : 7 * C])
            for one in range(2):
                act_ref[t, two + one] = gates[:, one * LANES : (one + 1) * LANES]
        return 0

    lax.fori_loop(0, steps, encode, 0)
    hid_s[...] = jnp.zeros_like(hid_s)
    state_s[...] = jnp.zeros_like(state_s)

    def advance(t, _):
        hidden = []
        for two in range(0, TILES, 2):
            sums = nn(wh_s[...], stacked(hid_s, two, KS))
            for one in range(2):
                tile = two + one
                gates = act_ref[t, tile] + sums[:, one * LANES : (one + 1) * LANES]
                gate_in = logistic(gates[0:C])
                gate_keep = logistic(gates[C : 2 * C] + 1.0)
                gate_out = logistic(gates[2 * C : 3 * C])
                gate_new = jnp.tanh(gates[3 * C : 4 * C])
                cell = gate_keep * state_s[tile] + gate_in * gate_new
                act_ref[t, tile, 0:C] = gate_in
                act_ref[t, tile, C : 2 * C] = gate_keep
                act_ref[t, tile, 2 * C : 3 * C] = gate_out
                act_ref[t, tile, 3 * C : 4 * C] = gate_new
                state_s[tile] = cell
                cell_ref[t, tile] = cell
                low = (gate_out * jnp.tanh(cell)).astype(BF)
                hid_ref[t, tile] = low
                hidden.append(low.astype(F32))
        spread(hidden, lanes, 2, hid_s, C, 0)
        return 0

    lax.fori_loop(0, steps, advance, 0)
    own = steps // HALVES
    base = half_ref[0] * own

    def to_strips(i, _):
        for pair in range(2):
            rows = []
            for low_row in range(2):
                tile = hid_ref[base + i, 2 * pair + low_row].astype(F32)
                rows.append(block_swap([tile[8 * q : 8 * q + 8] for q in range(4)], lanes[1]))
            for band in range(BANDS):
                strip_ref[2 * band + pair, i] = jnp.concatenate(
                    [rows[0][band], rows[1][band]], axis=0
                ).astype(BF)
        return 0

    lax.fori_loop(0, own, to_strips, 0)


def head_kernel(
    half_ref, x_ref, hid_ref, logit_ref, w_ref, mask_ref, bias_ref, place_ref, placet_ref,
    back_ref, dlog_ref, dwd_ref, dwm_ref, sums_ref,
    win_s, dk_s, wd_ref, wdt_ref, wm_ref, wmt_ref, over_ref,
):
    wd_ref[...] = w_ref[...].astype(BF)
    wdt_ref[...] = nt(one_hot_eye(4 * C), wd_ref[...]).astype(BF)
    copies = one_hot_mod((4 * C, C), C, 0)
    fourfold = nn(copies, mask_ref[...].astype(BF)).astype(BF)
    row = lax.broadcasted_iota(jnp.int32, (4 * C, 64), 0)
    wmt_ref[...] = jnp.where(
        row // C == lax.broadcasted_iota(jnp.int32, (4 * C, 64), 1) // 16,
        nn(fourfold, one_hot_mod((NM, 64), 16, 1)), 0.0,
    ).astype(BF)
    row = lax.broadcasted_iota(jnp.int32, (64, 4 * C), 0)
    wm_ref[...] = jnp.where(
        row // 16 == lax.broadcasted_iota(jnp.int32, (64, 4 * C), 1) // C,
        nt(one_hot_mod((64, NM), 16, 0), fourfold), 0.0,
    ).astype(BF)
    for sub in range(4):
        over_ref[sub * C : (sub + 1) * C, :] = bias_ref[7 * C : 8 * C]
        over_ref[4 * C + sub * 16 : 4 * C + (sub + 1) * 16, :] = bias_ref[8 * C : 8 * C + 16]
    own = logit_ref.shape[0]
    base = half_ref[0] * own
    lanes = lane_places()
    dwd_ref[...] = jnp.zeros_like(dwd_ref)
    dwm_ref[...] = jnp.zeros_like(dwm_ref)
    sums_ref[...] = jnp.zeros_like(sums_ref)
    row8 = lax.broadcasted_iota(jnp.int32, (8, 2 * LANES), 0)
    color = (row8 % 4) != 3
    row16 = lax.broadcasted_iota(jnp.int32, (16, 32), 0)
    lane16 = lax.broadcasted_iota(jnp.int32, (16, 32), 1)

    def frame(i, _):
        t = base + i
        spread(image_tiles(x_ref, t), lanes, 1, win_s, 16, 0)
        logits = logit_ref[i]
        powers = jnp.exp(logits - jnp.max(logits, -1, keepdims=True))
        kernels = powers / jnp.sum(powers, -1, keepdims=True)
        kernels = jnp.where(row16 == 0, (lane16 == KK // 2).astype(F32), jnp.where(row16 <= NK, kernels, 0.0))
        kernels_low = kernels.astype(BF)
        dk_s[...] = jnp.zeros_like(dk_s)
        for two in range(0, TILES, 2):
            hidden = jnp.concatenate([hid_ref[t, two], hid_ref[t, two + 1]], axis=1)
            window = stacked(win_s, two, 3)
            upper = nn(wdt_ref[...], hidden) + twice(over_ref[0 : 4 * C])
            gate = logistic(upper)
            active = (upper * gate).astype(BF)
            scores = nn(wm_ref[...], active) + twice(over_ref[4 * C : 4 * C + 64])
            scores = scores.reshape(4, 16, 2 * LANES)
            powers = jnp.exp(scores - jnp.max(scores, 1, keepdims=True))
            masks = powers / jnp.sum(powers, 1, keepdims=True)
            after = jnp.concatenate([x_ref[t + 1, two], x_ref[t + 1, two + 1]], axis=1).astype(F32)
            d_scores = []
            for sub in range(4):
                mask_low = masks[sub].astype(BF)
                spots = nt(place_ref[sub], kernels_low).astype(BF)
                mixing = nn(spots, mask_low)
                both = jnp.sum((mixing * window).reshape(18, 8, 2 * LANES), 0)
                result = both + pltpu.roll(both, 4, 0)
                goal = after[(sub % 2) * 8 : (sub % 2) * 8 + 8]
                turned = pltpu.roll(goal, 4, 0)
                goal = jnp.where((row8 < 4) == (sub // 2 == 0), goal, turned)
                counted = goal[3:4]
                diff = jnp.where(color, result - goal, 0.0)
                weighted = diff * counted
                lost = weighted * diff
                sums_ref[192:200] += lost[:, :LANES] + lost[:, LANES:]
                d_result = 2.0 * weighted
                d_mix = (window.reshape(18, 8, 2 * LANES) * d_result[None]).reshape(WIN, 2 * LANES).astype(BF)
                spots_t = nn(kernels_low, placet_ref[sub]).astype(BF)
                d_mask = nn(spots_t, d_mix)
                d_spots = nt(mask_low, d_mix)
                dk_s[...] += lax.dot_general(
                    d_spots, place_ref[sub].astype(F32), (((1,), (0,)), ((), ())),
                    preferred_element_type=F32, precision=HIGH,
                )
                inner = jnp.sum(masks[sub] * d_mask, 0, keepdims=True)
                d_scores.append(masks[sub] * (d_mask - inner))
            d_score = jnp.concatenate(d_scores, axis=0)
            sums_ref[128:192] += d_score[:, :LANES] + d_score[:, LANES:]
            d_score_low = d_score.astype(BF)
            d_active = nn(wmt_ref[...], d_score_low)
            dwm_ref[...] += nt(active, d_score_low)
            d_upper = d_active * (gate * (1.0 + upper * (1.0 - gate)))
            sums_ref[0:128] += d_upper[:, :LANES] + d_upper[:, LANES:]
            d_upper_low = d_upper.astype(BF)
            dwd_ref[...] += nt(hidden, d_upper_low)
            back = nn(wd_ref[...], d_upper_low).astype(BF)
            for one in range(2):
                back_ref[i, two + one] = back[:, one * LANES : (one + 1) * LANES]
        d_kernels = dk_s[...]
        inner = jnp.sum(d_kernels * kernels, -1, keepdims=True)
        dlog_ref[i] = kernels * (d_kernels - inner)
        return 0

    lax.fori_loop(0, own, frame, 0)


def backward_kernel(
    half_ref, x_ref, enc_ref, hid_ref, act_ref, cell_ref, dec_ref, fc_ref, w_ref, we_ref, bias_ref,
    dw_ref, dwe_ref, sums_ref,
    gate_s, keep_s, denc_s, back_s, state_s, win_s, join_s, wb_ref,
):
    for tap in range(KK):
        place = tap % KS * 2 * C
        turn = (KS - 1 - tap // KS) * 4 * C
        wb_ref[place : place + 2 * C, turn : turn + 4 * C] = w_ref[tap * 2 * C : (tap + 1) * 2 * C, :].astype(BF)
    steps = enc_ref.shape[0]
    own = steps // HALVES
    base = half_ref[0] * own
    lanes = lane_places()
    back_s[...] = jnp.zeros_like(back_s)
    state_s[...] = jnp.zeros_like(state_s)
    dw_ref[...] = jnp.zeros_like(dw_ref)
    dwe_ref[...] = jnp.zeros_like(dwe_ref)
    sums_ref[...] = jnp.zeros_like(sums_ref)

    def retreat(step, _):
        t = steps - 1 - step
        half = t // own
        inside = t % own
        mine = jnp.where(half == half_ref[0], 1.0, 0.0)
        earlier = jnp.maximum(t - 1, 0)
        started = jnp.where(t > 0, 1.0, 0.0)
        tiles = []
        for tile in range(TILES):
            pair = tile // 2
            low_row = tile % 2
            parts = [
                fc_ref[half, 2 * band + pair, inside].astype(F32)[8 * low_row : 8 * low_row + 8]
                for band in range(BANDS)
            ]
            from_fc = jnp.concatenate(block_swap(parts, lanes[1]), axis=0)
            back = back_s[tile] + from_fc + dec_ref[half, inside, tile].astype(F32)
            gate_in = act_ref[t, tile, 0:C]
            gate_keep = act_ref[t, tile, C : 2 * C]
            gate_out = act_ref[t, tile, 2 * C : 3 * C]
            gate_new = act_ref[t, tile, 3 * C : 4 * C]
            bent = jnp.tanh(cell_ref[t, tile])
            d_cell = state_s[tile] + back * gate_out * (1.0 - bent * bent)
            state_s[tile] = d_cell * gate_keep
            d_gates = jnp.concatenate(
                [
                    d_cell * gate_new * gate_in * (1.0 - gate_in),
                    d_cell * (cell_ref[earlier, tile] * started) * gate_keep * (1.0 - gate_keep),
                    back * bent * gate_out * (1.0 - gate_out),
                    d_cell * gate_in * (1.0 - gate_new * gate_new),
                ],
                axis=0,
            )
            sums_ref[3 * C : 7 * C] += d_gates * mine
            low = d_gates.astype(BF)
            keep_s[t, tile] = low
            tiles.append(low.astype(F32))
        for index in range(TILES + 4):
            tile = index - 2
            gate_s[index] = moved(tiles[tile % TILES], lanes, 0, tile // TILES).astype(BF)
        for two in range(0, TILES, 2):
            sums = nn(wb_ref[...], stacked(gate_s, two, KS))
            for one in range(2):
                part = sums[:, one * LANES : (one + 1) * LANES]
                total = None
                for shift in range(KS):
                    value = moved(part[shift * 2 * C : (shift + 1) * 2 * C], lanes, 2 - shift, 0)
                    total = value if total is None else total + value
                denc_s[t, two + one] = total[:C]
                back_s[two + one] = total[C:]
        return 0

    lax.fori_loop(0, steps, retreat, 0)

    def gather(i, _):
        t = base + i
        earlier = jnp.maximum(t - 1, 0)
        started = jnp.where(t > 0, 1.0, 0.0)
        spread([enc_ref[t, tile].astype(F32) for tile in range(TILES)], lanes, 2, join_s, 2 * C, 0)
        spread(
            [hid_ref[earlier, tile].astype(F32) * started for tile in range(TILES)], lanes, 2, join_s, 2 * C, C
        )
        spread(image_tiles(x_ref, t), lanes, 1, win_s, 16, 0)
        for two in range(0, TILES, 2):
            d_gates = jnp.concatenate([keep_s[t, two], keep_s[t, two + 1]], axis=1)
            dw_ref[...] += nt(stacked(join_s, two, KS), d_gates)
            window = stacked(win_s, two, 3)
            pre = nn(we_ref[...], window) + twice(bias_ref[0:C])
            centered = pre - jnp.mean(pre, 0, keepdims=True)
            scale = lax.rsqrt(jnp.mean(centered * centered, 0, keepdims=True) + NORM_EPS)
            normal = centered * scale
            gain = twice(bias_ref[C : 2 * C])
            value = normal * gain + twice(bias_ref[2 * C : 3 * C])
            gate = logistic(value)
            d_out = jnp.concatenate([denc_s[t, two], denc_s[t, two + 1]], axis=1)
            d_value = d_out * (gate * (1.0 + value * (1.0 - gate)))
            d_gain = d_value * normal
            d_normal = d_value * gain
            d_pre = scale * (
                d_normal
                - jnp.mean(d_normal, 0, keepdims=True)
                - normal * jnp.mean(d_normal * normal, 0, keepdims=True)
            )
            sums_ref[0:C] += d_pre[:, :LANES] + d_pre[:, LANES:]
            sums_ref[C : 2 * C] += d_gain[:, :LANES] + d_gain[:, LANES:]
            sums_ref[2 * C : 3 * C] += d_value[:, :LANES] + d_value[:, LANES:]
            dwe_ref[...] += nt(d_pre.astype(BF), window)
        return 0

    lax.fori_loop(0, own, gather, 0)


SMEM_SPEC = pl.BlockSpec(memory_space=pltpu.SMEM)
VMEM_SPEC = pl.BlockSpec(memory_space=pltpu.VMEM)


def call(kernel, outs, scratch, half, *operands):
    return pl.pallas_call(
        kernel,
        out_shape=[jax.ShapeDtypeStruct(shape, kind) for shape, kind in outs],
        in_specs=[SMEM_SPEC] + [VMEM_SPEC] * len(operands),
        out_specs=[VMEM_SPEC] * len(outs),
        scratch_shapes=[pltpu.VMEM(shape, kind) for shape, kind in scratch],
        compiler_params=pltpu.CompilerParams(vmem_limit_bytes=VMEM_BYTES),
    )(half, *operands)


def columns(values):
    return jnp.broadcast_to(values[:, None], (values.shape[0], LANES))


def exchange(block, axes):
    return lax.all_to_all(block, axes, 0, 0, tiled=True)


def to_all(block, axes):
    count = lax.axis_size(axes)
    return exchange(jnp.broadcast_to(block[None], (count,) + block.shape), axes)


def strip_order():
    sent = np.arange(WB * C)
    natural = sent % WB * C + sent // WB % 4 * 8 + sent // LANES
    order = np.zeros((WB * C, WB * C), np.float32)
    order[sent, natural] = 1.0
    return order


def in_three(values):
    terms = []
    for _ in range(3):
        low = lax.optimization_barrier(values.astype(BF))
        terms.append(low)
        values = values - low.astype(F32)
    return jnp.concatenate(terms)


def in_rows(values):
    flat = values.reshape(-1)
    rows = -(-flat.shape[0] // LANES)
    return jnp.pad(flat, (0, rows * LANES - flat.shape[0])).reshape(rows, LANES)


def whole_clips(
    frames, valid, flags, actions, states, latent,
    w_enc, w_lstm, w_fc, w_cond, w_deconv, w_mask, vector,
    m_enc, m_lstm, m_fc, m_cond, m_deconv, m_mask, m_vector,
    v_enc, v_lstm, v_fc, v_cond, v_deconv, v_mask, v_vector,
):
    clips, shots, _, strip_rows, width = frames.shape
    steps = shots - 1
    own = steps // HALVES
    count = lax.axis_size("row")
    place = lax.axis_index("row")
    clip = place // HALVES
    half = place % HALVES
    half_1 = half.reshape(1).astype(jnp.int32)
    b_enc, g_enc, s_enc, b_lstm, b_fc, b_dec, b_mask = split_vector(vector)
    places, encoder = window_places()
    flagged = jnp.pad(valid.astype(BF), ((0, 0), (1, 0), (0, 0), (0, 0)))
    pieces = jnp.concatenate([frames, flagged[:, :, None]], axis=2).reshape(clips, shots, 4, 2, 2, width)
    pieces = jnp.transpose(pieces, (0, 1, 4, 2, 3, 5)).reshape(clips, shots * 8, LANES)
    pieces = jnp.pad(pieces, ((0, 0), (0, 8), (0, 0)))
    raw = exchange(jnp.repeat(pieces, HALVES, axis=0), "row")

    wide_enc = jnp.einsum(
        "rk,ko->or", jnp.asarray(encoder, BF), w_enc.astype(BF), preferred_element_type=F32
    ).astype(BF)
    bias = columns(
        jnp.concatenate([vector[: 7 * C], b_dec, jnp.pad(b_mask, (0, 16 - NM), constant_values=-1e30)])
    )
    cells = (steps, TILES, C, LANES)
    x, enc, hid, act, cell, strips_out = call(
        forward_kernel,
        [
            ((shots, TILES, 16, LANES), BF), (cells, BF), (cells, BF), ((steps, TILES, 4 * C, LANES), F32),
            (cells, F32), ((count, own, 16, LANES), BF),
        ],
        [
            ((6, 48, LANES), BF), ((8, KS * C, LANES), BF), ((8, KS * C, LANES), BF), ((TILES, C, LANES), F32),
            ((KK * C, LANES), BF), ((4 * C, KK * C), BF), ((4 * C, KK * C), BF),
        ],
        half_1, raw, wide_enc, w_lstm, bias,
    )
    items = clips * steps
    order = jnp.asarray(strip_order(), BF)
    k_fc = w_fc.astype(BF)
    strip_hid = exchange(strips_out, "row").reshape(items * 2, WB * C)
    strip_hid = jnp.dot(strip_hid, order, preferred_element_type=F32).astype(BF).reshape(items, 2, WB * C)
    parts = jnp.einsum("mjk,jnk->mn", strip_hid, k_fc, preferred_element_type=F32)
    summed = jnp.sum(exchange(parts.reshape(count, own, NK * KK), "row"), 0)
    presence = flags.astype(F32)
    conditions = jnp.concatenate(
        [
            actions * presence[..., :1],
            states * presence[..., 1:],
            jnp.broadcast_to(latent[:, None, :], (clips, steps, latent.shape[1])),
        ],
        -1,
    )
    cond = lax.dynamic_slice(conditions, (clip, half * own, 0), (1, own, COND))[0]
    logits = summed + (jnp.dot(cond, w_cond, precision=HIGH) + b_fc)
    logits = jnp.pad(
        logits.reshape(own, NK, KK), ((0, 0), (1, 5), (0, 32 - KK)), constant_values=-1e30
    )
    dec, d_logit, d_dec, d_mask_wide, head_sums = call(
        head_kernel,
        [
            ((own, TILES, C, LANES), BF), ((own, 16, 32), F32), ((C, 4 * C), F32), ((4 * C, 64), F32),
            ((200, LANES), F32),
        ],
        [
            ((6, 48, LANES), F32), ((16, 32), F32), ((C, 4 * C), BF), ((4 * C, C), BF), ((64, 4 * C), BF),
            ((4 * C, 64), BF), ((4 * C + 64, LANES), F32),
        ],
        half_1, x, hid, logits, w_deconv, w_mask, bias,
        jnp.asarray(places, BF), jnp.asarray(places.transpose(0, 2, 1), BF),
    )
    d_logit = d_logit[:, 1 : NK + 1, :KK].reshape(own, NK * KK)
    d_sum = to_all(d_logit.astype(BF), "row").reshape(items, NK * KK)
    back_fc = jnp.einsum("mn,jnk->mjk", d_sum, k_fc, preferred_element_type=F32).astype(BF)
    back_fc = lax.dot_general(
        back_fc.reshape(items * 2, WB * C), order, (((1,), (1,)), ((), ())), preferred_element_type=F32
    ).astype(BF)
    back_fc = exchange(back_fc.reshape(count, own, 16, LANES), "row")
    swap = [(index, index ^ 1) for index in range(count)]

    def in_order(block):
        other = lax.ppermute(block, "row", swap)
        return jnp.stack([jnp.where(half == 0, block, other), jnp.where(half == 0, other, block)])

    d_lstm, d_enc_wide, sums = call(
        backward_kernel,
        [((KK * 2 * C, 4 * C), F32), ((C, WIN), F32), ((7 * C, LANES), F32)],
        [
            ((8, 4 * C, LANES), BF), ((steps, TILES, 4 * C, LANES), BF), (cells, F32), ((TILES, C, LANES), F32),
            ((TILES, C, LANES), F32), ((6, 48, LANES), BF), ((8, KS * 2 * C, LANES), BF),
            ((KS * 2 * C, KS * 4 * C), BF),
        ],
        half_1, x, enc, hid, act, cell, in_order(dec), in_order(back_fc), w_lstm, wide_enc, bias,
    )
    groups = lax.axis_size("clip")
    part = WB * C // groups
    d_fc = jnp.einsum(
        "mjqk,mn->qjnk", strip_hid.reshape(items, 2, groups, part), d_sum, preferred_element_type=F32
    ).astype(BF)
    d_fc = jnp.sum(exchange(d_fc, "clip").astype(F32), 0)
    fc_squares = jnp.sum(d_fc * d_fc)
    d_fc = jnp.transpose(to_all(d_fc.astype(BF), "clip"), (1, 2, 0, 3)).reshape(w_fc.shape).astype(F32)

    d_enc = jnp.einsum("rk,or->ko", jnp.asarray(encoder, F32), d_enc_wide, precision=HIGH)
    d_cond = jnp.dot(cond.T, d_logit, precision=HIGH)
    d_mask = sum(d_mask_wide[sub * C : (sub + 1) * C, sub * 16 : sub * 16 + NM] for sub in range(4))
    head_lines = jnp.sum(head_sums, 1)
    d_vector = jnp.concatenate(
        [
            jnp.sum(sums, 1),
            jnp.sum(d_logit, 0),
            jnp.sum(head_lines[:128].reshape(4, C), 0),
            jnp.sum(head_lines[128:192].reshape(4, 16), 0)[:NM],
        ]
    )
    scalars = jnp.stack([jnp.sum(head_lines[192:196]), jnp.sum(valid.astype(F32)), fc_squares])
    both = ("clip", "row")
    devices = lax.axis_size(both)
    small = [d_enc, d_cond, d_dec, d_mask, d_vector]
    block = jnp.concatenate([in_rows(value.astype(BF)) for value in [d_lstm] + small])
    each = -(-block.shape[0] // devices)
    block = jnp.pad(block, ((0, devices * each - block.shape[0]), (0, 0))).reshape(devices, each, LANES)
    extra = jnp.pad(in_three(scalars), (0, LANES - 9))
    extra = jnp.broadcast_to(extra, (devices, 1, LANES))
    fill = jnp.zeros((devices, -(each + 1) % 16, LANES), BF)
    got = jnp.sum(exchange(jnp.concatenate([block, extra, fill], axis=1), both).astype(F32), 0)
    loss_sum, valid_count, squares = got[each, 0:3] + got[each, 3:6] + got[each, 6:9]
    got = to_all(got.astype(BF), both)[:, :each].reshape(devices * each, LANES).astype(F32)
    summed = []
    start = 0
    for value in [d_lstm] + small:
        rows = -(-value.size // LANES)
        summed.append(got[start : start + rows].reshape(-1)[: value.size].reshape(value.shape))
        start += rows
    d_lstm, d_enc, d_cond, d_dec, d_mask, d_vector = summed
    inv_count = 1.0 / valid_count
    grads = (d_enc, d_lstm, d_fc, d_cond, d_dec, d_mask, d_vector)
    squares = squares + jnp.sum(got * got)
    grad_norm = jnp.sqrt(squares) * inv_count
    factor = inv_count * (CLIP_NORM / jnp.maximum(grad_norm, CLIP_NORM))
    rates = learning_rates(w_fc.shape[0] * count)
    weights = (w_enc, w_lstm, w_fc, w_cond, w_deconv, w_mask, vector)
    firsts = (m_enc, m_lstm, m_fc, m_cond, m_deconv, m_mask, m_vector)
    seconds = (v_enc, v_lstm, v_fc, v_cond, v_deconv, v_mask, v_vector)
    new = [
        adam(weights[index], grads[index] * factor, firsts[index], seconds[index], rates[index])
        for index in range(7)
    ]
    outs = [loss_sum, valid_count, grad_norm]
    for kind in range(3):
        outs.extend(new[index][kind] for index in range(7))
    return tuple(outs)


def shards(frames, *rest):
    clips, _, _, strip_rows, width = frames.shape
    count = lax.axis_size("row")
    one_clip = strip_rows * count // 2 == TILES * BANDS and width // 2 == WB
    if one_clip and clips * HALVES == count:
        return whole_clips(frames, *rest)
    return strips(frames, *rest)


def solution(mesh):
    placed = (
        P("clip", None, None, "row", None),
        P("clip", None, "row", None),
        P("clip", None, None),
        P("clip", None, None),
        P("clip", None, None),
        P("clip", None),
        P(),
        P(),
        P("row", None, None),
        P(),
        P(),
        P(),
        P(),
        P(),
        P(),
        P("row", None, None),
        P(),
        P(),
        P(),
        P(),
        P(),
        P(),
        P("row", None, None),
        P(),
        P(),
        P(),
        P(),
    )
    return jax.shard_map(
        shards,
        mesh=mesh,
        in_specs=placed,
        out_specs=(
            P(),
            P(),
            P(),
            P(),
            P(),
            P("row", None, None),
            P(),
            P(),
            P(),
            P(),
            P(),
            P(),
            P("row", None, None),
            P(),
            P(),
            P(),
            P(),
            P(),
            P(),
            P("row", None, None),
            P(),
            P(),
            P(),
            P(),
        ),
        check_vma=False,
    )
```

```python
import functools

import jax
import jax.numpy as jnp
import numpy as np
from jax import lax
from jax.experimental import pallas as pl
from jax.experimental.pallas import tpu as pltpu
from jax.sharding import PartitionSpec as P

C = 32
KS = 5
NK = 10
STEP_NO = 10
KK = 25
NM = 11
COND = 15
WB = 32


NORM_EPS = 1e-05
CLIP_NORM = 0.001
BETA_ONE = 0.9
BETA_TWO = 0.999
ADAM_EPS = 1e-12
DECAY = 0.01
HIGH = lax.Precision.HIGHEST


def padded_2(cells, sides, width):
    for axis, dim in sides:
        count = lax.axis_size(axis)
        ends = count - 1
        head = lax.slice_in_dim(cells, 0, width, axis=dim)
        tail = lax.slice_in_dim(cells, cells.shape[dim] - width, cells.shape[dim], axis=dim)
        cells = jnp.concatenate(
            [
                lax.ppermute(tail, axis, [(i, (i + 1) % count) for i in range(ends)]),
                cells,
                lax.ppermute(head, axis, [((i + 1) % count, i) for i in range(ends)]),
            ],
            axis=dim,
        )
    return cells


def passed_along(block, axis, distance):
    devices = range(lax.axis_size(axis))
    route = [(i - distance, i) for i in devices if i - distance in devices]
    return lax.ppermute(block, axis, route)


def split_vector(vector):
    counts = [C, C, C, 4 * C, NK * KK, C, NM]
    pieces = []
    start = 0
    for count in counts:
        pieces.append(vector[start : start + count])
        start += count
    return pieces


def norm_act(pre, gain, shift):
    centered = pre - jnp.mean(pre, -1, keepdims=True)
    scale = lax.rsqrt(jnp.mean(centered * centered, -1, keepdims=True) + NORM_EPS)
    return jax.nn.silu(centered * scale * gain + shift)


def cell_step(gates, cell):
    gate_in, gate_keep, gate_out, gate_new = jnp.split(gates, 4, axis=-1)
    new_cell = jax.nn.sigmoid(gate_keep + 1.0) * cell + jax.nn.sigmoid(gate_in) * jnp.tanh(gate_new)
    return (jax.nn.sigmoid(gate_out) * jnp.tanh(new_cell), new_cell)


def upsample(values):
    clips, rows_in, cols_in, depth = values.shape
    grid = values.reshape(clips, rows_in, cols_in, 2, 2, depth // 4)
    return jnp.transpose(grid, (0, 1, 3, 2, 4, 5)).reshape(
        clips, 2 * rows_in, 2 * cols_in, depth // 4
    )


def predict(logits, upper, w_mask, b_mask, prev_pad):
    clips = logits.shape[0]
    kernels = jax.nn.softmax(logits.reshape(clips, NK, KK), axis=-1)
    activated = jax.nn.silu(upper)
    blend = jax.nn.softmax(
        jnp.einsum("byxc,cm->byxm", activated, w_mask, precision=HIGH) + b_mask, axis=-1
    )
    mixing = jnp.einsum("byxk,bko->byxo", blend[..., 1:], kernels, precision=HIGH)
    height = prev_pad.shape[1] - 4
    breadth = prev_pad.shape[2] - 4
    result = blend[..., :1] * prev_pad[:, 2 : 2 + height, 2 : 2 + breadth, :]
    for offset in range(KK):
        top = offset // KS
        left = offset % KS
        result = (
            result
            + mixing[..., offset : offset + 1]
            * prev_pad[:, top : top + height, left : left + breadth, :]
        )
    return result


def patches(padded, stride, out_rows, out_cols):
    pieces = []
    for offset in range(KK):
        top = offset // KS
        left = offset % KS
        pieces.append(
            padded[
                :,
                top : top + stride * (out_rows - 1) + 1 : stride,
                left : left + stride * (out_cols - 1) + 1 : stride,
                :,
            ]
        )
    return jnp.concatenate(pieces, -1)


def unpatch(grads, shape, stride):

    def extract(padded):
        return patches(padded, stride, grads.shape[1], grads.shape[2])

    _, pullback = jax.vjp(extract, jnp.zeros(shape, jnp.float32))
    return pullback(grads)[0]


def product(left, right, form):
    return jnp.einsum(form, left, right, preferred_element_type=jnp.float32)


def learning_rates(rows_total):
    return [
        0.5 * (KK * 3) ** (-0.5),
        0.5 * (KK * 2 * C) ** (-0.5),
        0.5 * (rows_total * WB * C // 16) ** (-0.5),
        0.5 * COND ** (-0.5),
        0.5 * C ** (-0.5),
        0.5 * (C // 4) ** (-0.5),
        0.1,
    ]


def adam(weight, grad, first, second, rate):
    first = BETA_ONE * first + (1.0 - BETA_ONE) * grad
    second = BETA_TWO * second + (1.0 - BETA_TWO) * grad * grad
    update = (
        first
        / (1.0 - BETA_ONE**STEP_NO)
        / (jnp.sqrt(second / (1.0 - BETA_TWO**STEP_NO)) + ADAM_EPS)
    )
    return (weight - rate * (update + DECAY * weight), first, second)


def strips(
    frames,
    valid,
    flags,
    actions,
    states,
    latent,
    w_enc,
    w_lstm,
    w_fc,
    w_cond,
    w_deconv,
    w_mask,
    vector,
    m_enc,
    m_lstm,
    m_fc,
    m_cond,
    m_deconv,
    m_mask,
    m_vector,
    v_enc,
    v_lstm,
    v_fc,
    v_cond,
    v_deconv,
    v_mask,
    v_vector,
):
    clips = frames.shape[0]
    out_rows = frames.shape[3] // 2
    out_cols = frames.shape[4] // 2
    b_enc, g_enc, s_enc, b_lstm, b_fc, b_dec, b_mask = split_vector(vector)
    k_enc = w_enc.astype(jnp.bfloat16)
    k_lstm = w_lstm.astype(jnp.bfloat16)
    k_fc = w_fc.astype(jnp.bfloat16)
    k_dec = w_deconv.astype(jnp.bfloat16)
    images = jnp.transpose(frames, (1, 0, 3, 4, 2))
    padded = padded_2(images, (("row", 2),), 2)
    padded = jnp.pad(padded, ((0, 0), (0, 0), (0, 0), (2, 2), (0, 0)))
    valid_steps = jnp.transpose(valid.astype(jnp.float32), (1, 0, 2, 3))
    presence = flags.astype(jnp.float32)
    conditions = jnp.concatenate(
        [
            actions * presence[..., :1],
            states * presence[..., 1:],
            jnp.broadcast_to(latent[:, None, :], (clips, actions.shape[1], latent.shape[1])),
        ],
        -1,
    )
    conditions = jnp.transpose(conditions, (1, 0, 2))
    valid_count = lax.psum(jnp.sum(valid_steps), ("clip", "row"))
    inv_count = 1.0 / valid_count

    def advance(carry, image_pad):
        hidden, cell = carry
        pre = product(patches(image_pad, 2, out_rows, out_cols), k_enc, "byxk,kc->byxc") + b_enc
        encoded = norm_act(pre, g_enc, s_enc).astype(jnp.bfloat16)
        joined = jnp.concatenate([encoded, hidden], -1)
        joined_pad = padded_2(joined, (("row", 1),), 2)
        joined_pad = jnp.pad(joined_pad, ((0, 0), (0, 0), (2, 2), (0, 0)))
        gates = (
            product(patches(joined_pad, 1, out_rows, out_cols), k_lstm, "byxk,kg->byxg") + b_lstm
        )
        new_hidden, new_cell = cell_step(gates, cell)
        hidden_low = new_hidden.astype(jnp.bfloat16)
        part = product(hidden_low.reshape(clips, out_rows, -1), k_fc, "bjk,jnk->bn")
        part = lax.psum(part, "row")
        upper = product(hidden_low, k_dec, "byxc,cd->byxd")
        return ((hidden_low, new_cell), (pre, joined_pad, gates, cell, hidden_low, part, upper))

    start = (
        jnp.zeros((clips, out_rows, out_cols, C), jnp.bfloat16),
        jnp.zeros((clips, out_rows, out_cols, C), jnp.float32),
    )
    _, saved = lax.scan(advance, start, padded[:-1])
    pre_all, joined_all, gates_all, cells_all, hidden_all, summed_all, uppers = saved
    targets = images[1:].astype(jnp.float32)

    def local_head(item):
        summed_t, upper_t, image_pad, target, mask, cond = item

        def error_of(summed_t, upper_t, w_cond, w_mask, b_fc, b_dec, b_mask):
            logits = summed_t + jnp.dot(cond, w_cond, precision=HIGH) + b_fc
            upper_full = upsample(upper_t) + b_dec
            result = predict(logits, upper_full, w_mask, b_mask, image_pad.astype(jnp.float32))
            return jnp.sum(mask * jnp.sum((result - target) ** 2, -1))

        error, pullback = jax.vjp(error_of, summed_t, upper_t, w_cond, w_mask, b_fc, b_dec, b_mask)
        return (error, pullback(inv_count))

    head_inputs = (summed_all, uppers, padded[:-1], targets, valid_steps, conditions)

    def retreat(carry, item):
        (
            back_hidden,
            back_cell,
            acc_enc,
            acc_lstm,
            acc_dec,
            acc_benc,
            acc_genc,
            acc_senc,
            acc_blstm,
        ) = carry
        saved_t, head_t = item
        pre, joined_pad, gates, cell_prev, hidden_low, image_pad = saved_t
        error, pulled_t = local_head(head_t)
        d_sum = lax.psum(pulled_t[0], "row")
        d_upper = pulled_t[1]
        extra = (error, pulled_t[2:])
        d_sum_low = d_sum.astype(jnp.bfloat16)
        d_upper_low = d_upper.astype(jnp.bfloat16)
        acc_dec = acc_dec + product(hidden_low, d_upper_low, "byxc,byxd->cd")
        back = back_hidden + product(d_upper_low, k_dec, "byxd,cd->byxc")
        back = back + product(d_sum_low, k_fc, "bn,jnk->bjk").reshape(back_hidden.shape)
        _, cell_pull = jax.vjp(cell_step, gates, cell_prev)
        d_gates, back_cell = cell_pull((back, back_cell))
        d_gates_low = d_gates.astype(jnp.bfloat16)
        acc_blstm = acc_blstm + jnp.sum(d_gates, (0, 1, 2))
        acc_lstm = acc_lstm + product(
            patches(joined_pad, 1, out_rows, out_cols), d_gates_low, "byxk,byxg->kg"
        )
        d_pad = unpatch(product(d_gates_low, k_lstm, "byxg,kg->byxk"), joined_pad.shape, 1)[
            :, :, 2:-2, :
        ]
        from_below = passed_along(d_pad[:, :2], "row", -1)
        from_above = passed_along(d_pad[:, -2:], "row", 1)
        d_joined = d_pad[:, 2:-2].at[:, -2:].add(from_below).at[:, :2].add(from_above)
        _, norm_pull = jax.vjp(norm_act, pre, g_enc, s_enc)
        d_pre, d_gain, d_shift = norm_pull(d_joined[..., :C])
        acc_benc = acc_benc + jnp.sum(d_pre, (0, 1, 2))
        acc_genc = acc_genc + d_gain
        acc_senc = acc_senc + d_shift
        acc_enc = acc_enc + product(
            patches(image_pad, 2, out_rows, out_cols), d_pre.astype(jnp.bfloat16), "byxk,byxc->kc"
        )
        new_carry = (
            d_joined[..., C:],
            back_cell,
            acc_enc,
            acc_lstm,
            acc_dec,
            acc_benc,
            acc_genc,
            acc_senc,
            acc_blstm,
        )
        return (new_carry, (d_sum_low, extra))

    zeros_state = jnp.zeros((clips, out_rows, out_cols, C), jnp.float32)
    zeros_small = jnp.zeros((C,), jnp.float32)
    init = (
        zeros_state,
        zeros_state,
        jnp.zeros(w_enc.shape, jnp.float32),
        jnp.zeros(w_lstm.shape, jnp.float32),
        jnp.zeros(w_deconv.shape, jnp.float32),
        zeros_small,
        zeros_small,
        zeros_small,
        jnp.zeros((4 * C,), jnp.float32),
    )
    final, (d_sums_low, extra) = lax.scan(
        retreat,
        init,
        ((pre_all, joined_all, gates_all, cells_all, hidden_all, padded[:-1]), head_inputs),
        reverse=True,
    )
    error_sum = jnp.sum(extra[0])
    head_sums = [jnp.sum(grad, 0) for grad in extra[1]]
    acc_enc, acc_lstm, acc_dec, acc_benc, acc_genc, acc_senc, acc_blstm = final[2:]
    flat_hidden = hidden_all.reshape(hidden_all.shape[0], clips, out_rows, -1)
    d_fc = lax.psum(
        product(flat_hidden, d_sums_low, "tbjk,tbn->jnk").astype(jnp.bfloat16), "clip"
    ).astype(jnp.float32)
    fc_squares = jnp.sum(d_fc * d_fc) / lax.axis_size("clip")
    d_vector = jnp.concatenate(
        [acc_benc, acc_genc, acc_senc, acc_blstm, head_sums[2], head_sums[3], head_sums[4]]
    )
    d_enc, d_lstm, d_cond, d_dec, d_mask, d_vector, loss_sum, squares = lax.psum(
        (acc_enc, acc_lstm, head_sums[0], acc_dec, head_sums[1], d_vector, error_sum, fc_squares),
        ("clip", "row"),
    )
    grads = (d_enc, d_lstm, d_fc, d_cond, d_dec, d_mask, d_vector)
    for index in (0, 1, 3, 4, 5, 6):
        squares = squares + jnp.sum(grads[index] * grads[index])
    grad_norm = jnp.sqrt(squares)
    factor = CLIP_NORM / jnp.maximum(grad_norm, CLIP_NORM)
    rates = learning_rates(w_fc.shape[0] * lax.axis_size("row"))
    weights = (w_enc, w_lstm, w_fc, w_cond, w_deconv, w_mask, vector)
    firsts = (m_enc, m_lstm, m_fc, m_cond, m_deconv, m_mask, m_vector)
    seconds = (v_enc, v_lstm, v_fc, v_cond, v_deconv, v_mask, v_vector)
    new = [
        adam(weights[index], grads[index] * factor, firsts[index], seconds[index], rates[index])
        for index in range(7)
    ]
    return (
        loss_sum,
        valid_count,
        grad_norm,
        new[0][0],
        new[1][0],
        new[2][0],
        new[3][0],
        new[4][0],
        new[5][0],
        new[6][0],
        new[0][1],
        new[1][1],
        new[2][1],
        new[3][1],
        new[4][1],
        new[5][1],
        new[6][1],
        new[0][2],
        new[1][2],
        new[2][2],
        new[3][2],
        new[4][2],
        new[5][2],
        new[6][2],
    )


LANES = 128
TILES = 4
BANDS = 4
HALVES = 2
FAR = 1
WIN = 9 * 16
BF = jnp.bfloat16
F32 = jnp.float32
VMEM_BYTES = 56 * 1024 * 1024


def window_places():
    places = np.zeros((4, WIN, 32), np.float32)
    encoder = np.zeros((WIN, KK * 3), np.float32)
    for sub in range(4):
        for tap in range(KK):
            off_y = tap // KS - 2 + sub // 2
            off_x = tap % KS - 2 + sub % 2
            block = (off_y // 2 + 1) * 3 + off_x // 2 + 1
            base = block * 16 + (off_x % 2) * 8 + (off_y % 2) * 4
            for channel in range(3):
                places[sub, base + channel, tap] = 1.0
                if sub == 0:
                    encoder[base + channel, tap * 3 + channel] = 1.0
    return places, encoder


def lane_places():
    lane = lax.broadcasted_iota(jnp.int32, (8, LANES), 1)
    return lane % WB, lane // WB


def moved(tile, lanes, d_col, d_band):
    if d_col == 0 and d_band == 0:
        return tile
    col, band = lanes
    rows = tile.shape[0]
    shift = (-(WB * d_band + d_col)) % LANES
    rolled = pltpu.roll(tile.reshape(rows // 8, 8, LANES), shift, 2)
    keep = None
    for place, delta, count in ((col, d_col, WB), (band, d_band, BANDS)):
        if delta > 0:
            inside = place < count - delta
        elif delta < 0:
            inside = place >= -delta
        else:
            continue
        keep = inside if keep is None else keep & inside
    return jnp.where(keep[None], rolled, 0.0).reshape(rows, LANES)


def spread(tiles, lanes, reach, target, width, start):
    rows = tiles[0].shape[0]
    for index in range(TILES + 2 * reach):
        tile = index - reach
        for shift in range(2 * reach + 1):
            place = shift * width + start
            target[index, place : place + rows, :] = moved(
                tiles[tile % TILES], lanes, shift - reach, tile // TILES
            ).astype(target.dtype)


def stacked(ref, tile, count):
    rows = count * ref.shape[1]
    return jnp.concatenate(
        [ref[tile : tile + count].reshape(rows, LANES), ref[tile + 1 : tile + 1 + count].reshape(rows, LANES)],
        axis=1,
    )


def nn(left, right):
    return lax.dot_general(left, right, (((1,), (0,)), ((), ())), preferred_element_type=F32)


def nt(left, right):
    return lax.dot_general(left, right, (((1,), (1,)), ((), ())), preferred_element_type=F32)


def nn_exact(left, right):
    return lax.dot_general(left, right, (((1,), (0,)), ((), ())), preferred_element_type=F32, precision=HIGH)


def nt_exact(left, right):
    return lax.dot_general(left, right, (((1,), (1,)), ((), ())), preferred_element_type=F32, precision=HIGH)


def logistic(v):
    return 0.5 * jnp.tanh(0.5 * v) + 0.5


def one_hot_eye(size):
    row = lax.broadcasted_iota(jnp.int32, (size, size), 0)
    return (row == lax.broadcasted_iota(jnp.int32, (size, size), 1)).astype(BF)


def split(value):
    high = value.astype(BF)
    return high, (value - high.astype(F32)).astype(BF)


def one_hot_mod(shape, period, axis):
    folded = lax.broadcasted_iota(jnp.int32, shape, axis) % period
    return (folded == lax.broadcasted_iota(jnp.int32, shape, 1 - axis)).astype(BF)


def unpack_images(raw_ref, x_ref):
    source = lax.broadcasted_iota(jnp.int32, (LANES, 4 * LANES), 0)
    goal = lax.broadcasted_iota(jnp.int32, (LANES, 4 * LANES), 1)
    same = (source // 64 == goal // 256) & (source % 2 == goal // LANES % 2) & (source // 2 % WB == goal % WB)
    picks = [(same & (goal // WB % BANDS == band)).astype(BF) for band in range(BANDS)]
    for pair in range(2):
        total = nn(raw_ref[pair], picks[0])
        for band in range(1, BANDS):
            total = total + nn(raw_ref[2 * band + pair], picks[band])
        for t in range(x_ref.shape[0]):
            rows = total[8 * t : 8 * t + 8]
            for low_row in range(2):
                start = 2 * LANES * low_row
                x_ref[t, 2 * pair + low_row] = jnp.concatenate(
                    [rows[:, start : start + LANES], rows[:, start + LANES : start + 2 * LANES]], axis=0
                ).astype(BF)


def image_tiles(x_ref, t):
    return [x_ref[t, tile].astype(F32) for tile in range(TILES)]


def block_swap(parts, band):
    swapped = []
    for out in range(BANDS):
        total = None
        for part in range(BANDS):
            shift = (WB * (part - out)) % LANES
            value = parts[part] if shift == 0 else pltpu.roll(parts[part], shift, 1)
            total = value if total is None else jnp.where(band == part, value, total)
        swapped.append(total)
    return swapped


def wide(tile):
    return jnp.concatenate([tile] * TILES, axis=1)


def folded(values):
    total = values[:, :LANES]
    for tile in range(1, values.shape[1] // LANES):
        total = total + values[:, tile * LANES : (tile + 1) * LANES]
    return total


def twice(tile):
    return jnp.concatenate([tile, tile], axis=1)


def forward_kernel(
    half_ref, raw_ref, we_ref, w_ref, bias_ref,
    x_ref, enc_ref, hid_ref, act_ref, cell_ref, strip_ref,
    win_s, enc_s, hid_s, state_s, rows_s, wx_s, wh_s,
):
    steps = enc_ref.shape[0]
    lanes = lane_places()
    for kind, target in ((0, wx_s), (1, wh_s)):
        for tap in range(KK):
            start = tap * 2 * C + kind * C
            rows_s[tap * C : (tap + 1) * C, :] = w_ref[start : start + C, :].astype(BF)
        target[...] = nt(one_hot_eye(4 * C), rows_s[...]).astype(BF)
    unpack_images(raw_ref, x_ref)

    def encode(t, _):
        spread(image_tiles(x_ref, t), lanes, 1, win_s, 16, 0)
        tiles = []
        for two in range(0, TILES, 2):
            pre = nn(we_ref[...], stacked(win_s, two, 3)) + twice(bias_ref[0:C])
            centered = pre - jnp.mean(pre, 0, keepdims=True)
            scale = lax.rsqrt(jnp.mean(centered * centered, 0, keepdims=True) + NORM_EPS)
            value = centered * scale * twice(bias_ref[C : 2 * C]) + twice(bias_ref[2 * C : 3 * C])
            value = (value * logistic(value)).astype(BF)
            for one in range(2):
                part = value[:, one * LANES : (one + 1) * LANES]
                enc_ref[t, two + one] = part
                tiles.append(part.astype(F32))
        spread(tiles, lanes, 2, enc_s, C, 0)
        for two in range(0, TILES, 2):
            gates = nn(wx_s[...], stacked(enc_s, two, KS)) + twice(bias_ref[3 * C : 7 * C])
            for one in range(2):
                act_ref[t, two + one] = gates[:, one * LANES : (one + 1) * LANES]
        return 0

    lax.fori_loop(0, steps, encode, 0)
    hid_s[...] = jnp.zeros_like(hid_s)
    state_s[...] = jnp.zeros_like(state_s)

    def advance(t, _):
        hidden = []
        for two in range(0, TILES, 2):
            sums = nn(wh_s[...], stacked(hid_s, two, KS))
            for one in range(2):
                tile = two + one
                gates = act_ref[t, tile] + sums[:, one * LANES : (one + 1) * LANES]
                gate_in = logistic(gates[0:C])
                gate_keep = logistic(gates[C : 2 * C] + 1.0)
                gate_out = logistic(gates[2 * C : 3 * C])
                gate_new = jnp.tanh(gates[3 * C : 4 * C])
                cell = gate_keep * state_s[tile] + gate_in * gate_new
                act_ref[t, tile, 0:C] = gate_in
                act_ref[t, tile, C : 2 * C] = gate_keep
                act_ref[t, tile, 2 * C : 3 * C] = gate_out
                act_ref[t, tile, 3 * C : 4 * C] = gate_new
                state_s[tile] = cell
                cell_ref[t, tile] = cell
                low = (gate_out * jnp.tanh(cell)).astype(BF)
                hid_ref[t, tile] = low
                hidden.append(low.astype(F32))
        spread(hidden, lanes, 2, hid_s, C, 0)
        return 0

    lax.fori_loop(0, steps, advance, 0)
    own = steps // HALVES
    base = half_ref[0] * own

    def to_strips(i, _):
        for pair in range(2):
            rows = []
            for low_row in range(2):
                tile = hid_ref[base + i, 2 * pair + low_row].astype(F32)
                rows.append(block_swap([tile[8 * q : 8 * q + 8] for q in range(4)], lanes[1]))
            for band in range(BANDS):
                strip_ref[2 * band + pair, i] = jnp.concatenate(
                    [rows[0][band], rows[1][band]], axis=0
                ).astype(BF)
        return 0

    lax.fori_loop(0, own, to_strips, 0)


def head_kernel(
    half_ref, x_ref, hid_ref, logit_ref, w_ref, mask_ref, bias_ref, place_ref, placet_ref,
    back_ref, dlog_ref, dwd_ref, dwm_ref, sums_ref,
    win_s, wd_ref, wdt_ref, wm_ref, wmt_ref, over_ref, wide_s, everywhere_s, turned_s, d_mix_s, d_spot_s, kernel_s,
):
    wd_ref[...] = w_ref[...].astype(BF)
    wdt_ref[...] = nt(one_hot_eye(4 * C), wd_ref[...]).astype(BF)
    row = lax.broadcasted_iota(jnp.int32, (4 * C, 64), 0)
    mine_t = row // C == lax.broadcasted_iota(jnp.int32, (4 * C, 64), 1) // 16
    row = lax.broadcasted_iota(jnp.int32, (64, 4 * C), 0)
    mine = row // 16 == lax.broadcasted_iota(jnp.int32, (64, 4 * C), 1) // C
    for kind, part in enumerate(split(mask_ref[...])):
        spread_mask = nt(one_hot_mod((4 * C, C), C, 0), part).astype(BF)
        wide_t = jnp.where(mine_t, nn(spread_mask, one_hot_mod((NM, 64), 16, 1)), 0.0).astype(BF)
        wide_m = jnp.where(mine, nt(one_hot_mod((64, NM), 16, 0), spread_mask), 0.0).astype(BF)
        wmt_ref[:, kind * 64 : kind * 64 + 64] = wide_t
        wm_ref[:, kind * 4 * C : (kind + 1) * 4 * C] = wide_m
        if kind == 0:
            wmt_ref[:, 128:192] = wide_t
            wm_ref[:, 8 * C : 12 * C] = wide_m
    for sub in range(4):
        over_ref[sub * C : (sub + 1) * C, :] = bias_ref[7 * C : 8 * C]
        over_ref[4 * C + sub * 16 : 4 * C + (sub + 1) * 16, :] = bias_ref[8 * C : 8 * C + 16]
    own = logit_ref.shape[0]
    base = half_ref[0] * own
    lanes = lane_places()
    dwd_ref[...] = jnp.zeros_like(dwd_ref)
    wide_s[...] = jnp.zeros_like(wide_s)
    sums_ref[...] = jnp.zeros_like(sums_ref)
    cells = TILES * LANES
    row8 = lax.broadcasted_iota(jnp.int32, (8, cells), 0)
    color = (row8 % 4) != 3
    row16 = lax.broadcasted_iota(jnp.int32, (16, 32), 0)
    lane16 = lax.broadcasted_iota(jnp.int32, (16, 32), 1)

    for sub in range(4):
        everywhere_s[sub * WIN : (sub + 1) * WIN] = place_ref[sub]
        turned_s[:, sub * WIN : (sub + 1) * WIN] = placet_ref[sub]
    row = lax.broadcasted_iota(jnp.int32, (4 * WIN, 64), 0) // WIN
    own_spots = row == lax.broadcasted_iota(jnp.int32, (4 * WIN, 64), 1) // 16
    row = lax.broadcasted_iota(jnp.int32, (64, 4 * WIN), 0) // 16
    own_turned = row == lax.broadcasted_iota(jnp.int32, (64, 4 * WIN), 1) // WIN

    def frame(i, _):
        t = base + i
        spread(image_tiles(x_ref, t), lanes, 1, win_s, 16, 0)
        window = jnp.concatenate([win_s[tile : tile + 3].reshape(WIN, LANES) for tile in range(TILES)], axis=1)
        window = window.reshape(18, 8, cells)
        logits = logit_ref[i]
        powers = jnp.exp(logits - jnp.max(logits, -1, keepdims=True))
        kernels = powers / jnp.sum(powers, -1, keepdims=True)
        kernels = jnp.where(row16 == 0, (lane16 == KK // 2).astype(F32), jnp.where(row16 <= NK, kernels, 0.0))
        kernel_s[i] = kernels
        spots = []
        turned = []
        for part in split(kernels):
            part = jnp.concatenate([part, part, part, part], axis=0)
            spots.append(jnp.where(own_spots, nt(everywhere_s[...], part), 0.0).astype(BF))
            turned.append(jnp.where(own_turned, nn(part, turned_s[...]), 0.0).astype(BF))
        spots = jnp.concatenate([spots[0], spots[1], spots[0]], axis=1)
        turned = jnp.concatenate(turned, axis=0)
        hidden = jnp.concatenate([hid_ref[t, tile] for tile in range(TILES)], axis=1)
        upper = nn(wdt_ref[...], hidden) + wide(over_ref[0 : 4 * C])
        gate = logistic(upper)
        active, active_rest = split(upper * gate)
        scores = nn(wm_ref[...], jnp.concatenate([active, active, active_rest], axis=0)) + wide(over_ref[4 * C : 4 * C + 64])
        scores = scores.reshape(4, 16, cells)
        powers = jnp.exp(scores - jnp.max(scores, 1, keepdims=True))
        masks = powers / jnp.sum(powers, 1, keepdims=True)
        mask_low, mask_rest = split(masks.reshape(64, cells))
        mixing = nn(spots, jnp.concatenate([mask_low, mask_low, mask_rest], axis=0)).reshape(4, 18, 8, cells)
        after = jnp.concatenate([x_ref[t + 1, tile] for tile in range(TILES)], axis=1).astype(F32)
        lost = None
        for sub in range(4):
            both = jnp.sum(mixing[sub] * window, 0)
            result = both + pltpu.roll(both, 4, 0)
            goal = after[(sub % 2) * 8 : (sub % 2) * 8 + 8]
            goal = jnp.where((row8 < 4) == (sub // 2 == 0), goal, pltpu.roll(goal, 4, 0))
            diff = jnp.where(color, result - goal, 0.0)
            weighted = diff * goal[3:4]
            part = weighted * diff
            lost = part if lost is None else lost + part
            d_result = 2.0 * weighted
            d_mix_s[sub * WIN : (sub + 1) * WIN] = (window * d_result[None]).reshape(WIN, cells).astype(BF)
        sums_ref[192:200] += folded(lost)
        d_mask = nn(turned, d_mix_s[...])
        d_mask = (d_mask[:64] + d_mask[64:]).reshape(4, 16, cells)
        d_spot_s[i] = nt(mask_low, d_mix_s[...])
        inner = jnp.sum(masks * d_mask, 1, keepdims=True)
        d_score = (masks * (d_mask - inner)).reshape(64, cells)
        sums_ref[128:192] += folded(d_score)
        d_score_low, d_score_rest = split(d_score)
        d_active = nn(wmt_ref[...], jnp.concatenate([d_score_low, d_score_low, d_score_rest], axis=0))
        wide_s[...] += nt(d_score_low, active)
        d_upper = d_active * (gate * (1.0 + upper * (1.0 - gate)))
        sums_ref[0:128] += folded(d_upper)
        d_upper_low = d_upper.astype(BF)
        dwd_ref[...] += nt(hidden, d_upper_low)
        back = nn(wd_ref[...], d_upper_low).astype(BF)
        for tile in range(TILES):
            back_ref[i, tile] = back[:, tile * LANES : (tile + 1) * LANES]
        return 0

    lax.fori_loop(0, own, frame, 0)
    d_kernels = None
    for sub in range(4):
        rows = jnp.concatenate([d_spot_s[i, sub * 16 : sub * 16 + 16] for i in range(own)], axis=0)
        place = lax.broadcasted_iota(jnp.int32, rows.shape, 1) // WIN
        part = nn_exact(jnp.where(place == sub, rows, 0.0), everywhere_s[...].astype(F32))
        d_kernels = part if d_kernels is None else d_kernels + part
    for i in range(own):
        kernels = kernel_s[i]
        d_one = d_kernels[16 * i : 16 * i + 16]
        inner = jnp.sum(d_one * kernels, -1, keepdims=True)
        dlog_ref[i] = kernels * (d_one - inner)
    row = lax.broadcasted_iota(jnp.int32, (64, 4 * C), 0)
    lane = lax.broadcasted_iota(jnp.int32, (64, 4 * C), 1)
    own_block = jnp.where(row // 16 == lane // C, wide_s[...], 0.0)
    fold = lax.broadcasted_iota(jnp.int32, (4 * C, LANES), 0) % C
    fold = (fold == lax.broadcasted_iota(jnp.int32, (4 * C, LANES), 1)).astype(F32)
    dwm_ref[...] = jnp.sum(nn_exact(own_block, fold).reshape(4, 16, LANES), 0)


def backward_kernel(
    half_ref, act_ref, cell_ref, dec_ref, fc_ref, w_ref,
    keep_ref, denc_ref, lines_ref,
    gate_s, back_s, state_s, wb_s,
):
    for tap in range(KK):
        place = tap % KS * 2 * C
        turn = (KS - 1 - tap // KS) * 4 * C
        wb_s[place : place + 2 * C, turn : turn + 4 * C] = w_ref[tap * 2 * C : (tap + 1) * 2 * C, :].astype(BF)
    steps = act_ref.shape[0]
    own = steps // HALVES
    base = half_ref[0] * own
    lanes = lane_places()
    back_s[...] = jnp.zeros_like(back_s)
    state_s[...] = jnp.zeros_like(state_s)
    lines_ref[...] = jnp.zeros_like(lines_ref)

    def retreat(step, _):
        t = steps - 1 - step
        half = t // own
        inside = t % own
        mine = half == half_ref[0]
        counted = jnp.where(mine, 1.0, 0.0)
        earlier = jnp.maximum(t - 1, 0)
        started = jnp.where(t > 0, 1.0, 0.0)
        tiles = []
        for tile in range(TILES):
            pair = tile // 2
            low_row = tile % 2
            parts = [
                fc_ref[half, 2 * band + pair, inside].astype(F32)[8 * low_row : 8 * low_row + 8]
                for band in range(BANDS)
            ]
            from_fc = jnp.concatenate(block_swap(parts, lanes[1]), axis=0)
            back = back_s[tile] + from_fc + dec_ref[half, inside, tile].astype(F32)
            gate_in = act_ref[t, tile, 0:C]
            gate_keep = act_ref[t, tile, C : 2 * C]
            gate_out = act_ref[t, tile, 2 * C : 3 * C]
            gate_new = act_ref[t, tile, 3 * C : 4 * C]
            bent = jnp.tanh(cell_ref[t, tile])
            d_cell = state_s[tile] + back * gate_out * (1.0 - bent * bent)
            state_s[tile] = d_cell * gate_keep
            d_gates = jnp.concatenate(
                [
                    d_cell * gate_new * gate_in * (1.0 - gate_in),
                    d_cell * (cell_ref[earlier, tile] * started) * gate_keep * (1.0 - gate_keep),
                    back * bent * gate_out * (1.0 - gate_out),
                    d_cell * gate_in * (1.0 - gate_new * gate_new),
                ],
                axis=0,
            )
            lines_ref[...] += d_gates * counted
            tiles.append(d_gates.astype(BF))

        @pl.when(mine)
        def _():
            for tile in range(TILES):
                keep_ref[inside, tile] = tiles[tile]

        wide = [tile.astype(F32) for tile in tiles]
        for index in range(TILES + 4):
            tile = index - 2
            gate_s[index] = moved(wide[tile % TILES], lanes, 0, tile // TILES).astype(BF)
        d_enc = []
        for two in range(0, TILES, 2):
            sums = nn(wb_s[...], stacked(gate_s, two, KS))
            for one in range(2):
                part = sums[:, one * LANES : (one + 1) * LANES]
                total = None
                for shift in range(KS):
                    value = moved(part[shift * 2 * C : (shift + 1) * 2 * C], lanes, 2 - shift, 0)
                    total = value if total is None else total + value
                d_enc.append(total[:C])
                back_s[two + one] = total[C:]

        @pl.when(mine)
        def _():
            for tile in range(TILES):
                denc_ref[inside, tile] = d_enc[tile]

        return 0

    lax.fori_loop(0, steps, retreat, 0)


ROW_DEC = KK * 2 * C
ROW_COND = ROW_DEC + C
ROW_ENC = ROW_COND + 32
ROW_MASK = ROW_ENC + C
ROW_VECTOR = ROW_MASK + 16
ROWS = ROW_VECTOR + 16
PART = 64
SMALL = ROWS - ROW_DEC


def vector_places():
    place = np.zeros((7 * C + 4 * C + 64, 5 * LANES), np.float32)
    for line in range(7 * C):
        place[line, line] = 1.0
    for line in range(4 * C):
        place[7 * C + line, 7 * C + NK * KK + line % C] = 1.0
    for line in range(64):
        if line % 16 < NM:
            place[11 * C + line, 8 * C + NK * KK + line % 16] = 1.0
    return place


def pack_kernel(
    half_ref, x_ref, enc_ref, hid_ref, keep_ref, denc_ref, lines_ref, head_ref, ddec_ref, dmask_ref, dcond_ref,
    dline_ref, scalar_ref, we_ref, bias_ref, place_ref, encoder_ref,
    block_ref,
    win_s, join_s, dwe_s, sums_s, packed_s,
):
    own = keep_ref.shape[0]
    base = half_ref[0] * own
    lanes = lane_places()
    dwe_s[...] = jnp.zeros_like(dwe_s)
    sums_s[...] = jnp.zeros_like(sums_s)
    packed_s[...] = jnp.zeros_like(packed_s)

    def gather(i, _):
        t = base + i
        earlier = jnp.maximum(t - 1, 0)
        started = jnp.where(t > 0, 1.0, 0.0)
        spread([enc_ref[t, tile].astype(F32) for tile in range(TILES)], lanes, 2, join_s, 2 * C, 0)
        spread(
            [hid_ref[earlier, tile].astype(F32) * started for tile in range(TILES)], lanes, 2, join_s, 2 * C, C
        )
        spread(image_tiles(x_ref, t), lanes, 1, win_s, 16, 0)
        for two in range(0, TILES, 2):
            d_gates = jnp.concatenate([keep_ref[i, two], keep_ref[i, two + 1]], axis=1)
            packed_s[0:ROW_DEC] += nt(stacked(join_s, two, KS), d_gates)
            window = stacked(win_s, two, 3)
            pre = nn(we_ref[...], window) + twice(bias_ref[0:C])
            centered = pre - jnp.mean(pre, 0, keepdims=True)
            scale = lax.rsqrt(jnp.mean(centered * centered, 0, keepdims=True) + NORM_EPS)
            normal = centered * scale
            gain = twice(bias_ref[C : 2 * C])
            value = normal * gain + twice(bias_ref[2 * C : 3 * C])
            gate = logistic(value)
            d_out = jnp.concatenate([denc_ref[i, two], denc_ref[i, two + 1]], axis=1)
            d_value = d_out * (gate * (1.0 + value * (1.0 - gate)))
            d_gain = d_value * normal
            d_normal = d_value * gain
            d_pre = scale * (
                d_normal
                - jnp.mean(d_normal, 0, keepdims=True)
                - normal * jnp.mean(d_normal * normal, 0, keepdims=True)
            )
            sums_s[0:C] += d_pre[:, :LANES] + d_pre[:, LANES:]
            sums_s[C : 2 * C] += d_gain[:, :LANES] + d_gain[:, LANES:]
            sums_s[2 * C : 3 * C] += d_value[:, :LANES] + d_value[:, LANES:]
            dwe_s[...] += nt(d_pre.astype(BF), window)
        return 0

    lax.fori_loop(0, own, gather, 0)
    packed_s[ROW_DEC:ROW_COND] = ddec_ref[...]
    packed_s[ROW_COND:ROW_ENC] = dcond_ref[...]
    packed_s[ROW_ENC:ROW_MASK] = nn_exact(dwe_s[...], encoder_ref[...])
    packed_s[ROW_MASK:ROW_VECTOR] = dmask_ref[...]
    ones = jnp.ones((8, LANES), F32)
    sums_s[3 * C : 7 * C] = lines_ref[...]
    sums_s[7 * C : 11 * C + 64] = head_ref[0:192]
    line = nn_exact(nt_exact(ones, sums_s[...]), place_ref[...])[0:1] + jnp.sum(dline_ref[...], 0, keepdims=True)
    packed_s[ROW_VECTOR : ROW_VECTOR + 8] = jnp.concatenate(
        [line[:, place * LANES : (place + 1) * LANES] for place in range(5)] + [jnp.zeros((3, LANES), F32)], axis=0
    )
    lost = jnp.sum(jnp.sum(head_ref[192:196], 0, keepdims=True), 1, keepdims=True)
    lane = lax.broadcasted_iota(jnp.int32, (1, LANES), 1)
    value = jnp.where(lane == 0, lost, scalar_ref[...])
    terms = []
    for _ in range(3):
        low = value.astype(BF).astype(F32)
        terms.append(low)
        value = value - low
    devices = block_ref.shape[0]
    large = ROW_DEC // devices
    small = SMALL // devices
    fill = jnp.zeros((PART - large - 2 * small - 3, LANES), F32)
    for device in range(devices):
        value = packed_s[ROW_DEC + device * small : ROW_DEC + (device + 1) * small]
        high = value.astype(BF).astype(F32)
        rows = [packed_s[device * large : (device + 1) * large], high, value - high] + terms + [fill]
        block_ref[device] = jnp.concatenate(rows, axis=0).astype(BF)


def total_kernel(got_ref, out_ref, scalar_ref):
    devices, rows, _ = got_ref.shape
    total = got_ref[0].astype(F32)
    for device in range(1, devices):
        total = total + got_ref[device].astype(F32)
    large = ROW_DEC // devices
    small = SMALL // devices
    end = large + 2 * small
    scalar_ref[...] = total[end : end + 1] + total[end + 1 : end + 2] + total[end + 2 : end + 3]
    value = total[large : large + small] + total[large + small : end]
    high = value.astype(BF).astype(F32)
    low = jnp.concatenate([total[:large], high, value - high, total[end:]], axis=0).astype(BF)
    for device in range(devices):
        out_ref[device] = low


def logit_map_kernel(hid_ref, sum_ref, out_ref, squares_ref, turned_s):
    logits = NK * KK
    eye = one_hot_eye(logits)
    groups, items, _ = sum_ref.shape
    for group in range(groups):
        turned_s[:, group * items : (group + 1) * items] = nt(eye, sum_ref[group]).astype(BF)
    squares = jnp.zeros((1, LANES), F32)
    stride = 2 * WB * C // LANES
    for row in range(2):
        for start in range(0, WB * C, 2 * LANES):
            hid = jnp.concatenate(
                [hid_ref[group, row, :, start : start + 2 * LANES] for group in range(groups)], axis=0
            )
            grad = nn(turned_s[...], hid)
            for one in range(2):
                part = grad[:, one * LANES : (one + 1) * LANES]
                squares = squares + jnp.sum(part * part, 0, keepdims=True)
                out_ref[pl.ds((start // LANES + one) * 2 + row, logits, stride=stride), :] = part
    squares_ref[...] = squares


def update(weight, grad, first, second, rate):
    first = BETA_ONE * first + (1.0 - BETA_ONE) * grad
    second = BETA_TWO * second + (1.0 - BETA_TWO) * grad * grad
    shown = second * (1.0 / (1.0 - BETA_TWO**STEP_NO))
    step = first * (1.0 / (1.0 - BETA_ONE**STEP_NO)) / (shown * lax.rsqrt(shown) + ADAM_EPS)
    return (weight - rate * (step + DECAY * weight), first, second)


def update_kernel(rates, got_ref, scalar_ref, dfc_ref, *refs):
    weights, firsts, seconds = refs[0:7], refs[7:14], refs[14:21]
    norm_ref = refs[21]
    news = refs[22:29], refs[29:36], refs[36:43]
    packed_s, fc_s, lstm_s, sems = refs[43:]
    devices = got_ref.shape[0]
    large = ROW_DEC // devices
    small = SMALL // devices
    for device in range(devices):
        rows = got_ref[device].astype(F32)
        packed_s[device * large : (device + 1) * large] = rows[:large]
        packed_s[ROW_DEC + device * small : ROW_DEC + (device + 1) * small] = (
            rows[large : large + small] + rows[large + small : large + 2 * small]
        )

    def add_rows(block, total):
        rows = packed_s[pl.ds(pl.multiple_of(block * 32, 32), 32)]
        return total + jnp.sum((rows * rows).reshape(4, 8, LANES), 0)

    squares = lax.fori_loop(0, ROWS // 32, add_rows, jnp.zeros((8, LANES), F32))
    terms = scalar_ref[...]
    squares = jnp.sum(jnp.sum(squares, 0, keepdims=True), 1, keepdims=True) + terms[:, 2:3]
    inv_count = 1.0 / terms[:, 1:2]
    norm = jnp.sqrt(squares) * inv_count
    factor = inv_count * (CLIP_NORM / jnp.maximum(norm, CLIP_NORM))
    norm_ref[...] = jnp.sum(norm)

    copies = []

    def in_blocks(index, grad_ref, scratch, chunks):
        rows = grad_ref.shape[0] if index == 2 else ROW_DEC
        chunk = rows // chunks
        wide = chunk // 2
        for at in range(chunks):

            def block(i, _):
                here = pl.ds(pl.multiple_of(at * chunk + i * wide, 8), wide)
                new = update(
                    weights[index][here], grad_ref[here] * factor, firsts[index][here], seconds[index][here],
                    rates[index],
                )
                for kind in range(3):
                    scratch[kind, here] = new[kind]
                return 0

            lax.fori_loop(0, chunk // wide, block, 0)
            for kind in range(3):
                here = pl.ds(at * chunk, chunk)
                copy = pltpu.make_async_copy(
                    scratch.at[kind, here], news[kind][index].at[here], sems.at[len(copies)]
                )
                copy.start()
                copies.append(copy)

    in_blocks(2, dfc_ref, fc_s, 5)
    in_blocks(1, packed_s, lstm_s, 2)

    def step(index, grad):
        new = update(weights[index][...], grad * factor, firsts[index][...], seconds[index][...], rates[index])
        for kind in range(3):
            news[kind][index][...] = new[kind]

    step(0, packed_s[ROW_ENC:ROW_MASK, : KK * 3])
    cond = jnp.concatenate([packed_s[ROW_COND : ROW_COND + 16], packed_s[ROW_COND + 16 : ROW_COND + 32]], axis=1)
    step(3, cond[:COND, : NK * KK])
    step(4, packed_s[ROW_DEC:ROW_COND])
    step(5, packed_s[ROW_MASK : ROW_MASK + NM, 0:C])
    line = jnp.concatenate([packed_s[ROW_VECTOR + place : ROW_VECTOR + place + 1] for place in range(5)], axis=1)
    step(6, line[:, : weights[6].shape[1]])
    for copy in copies:
        copy.wait()


SMEM_SPEC = pl.BlockSpec(memory_space=pltpu.SMEM)
VMEM_SPEC = pl.BlockSpec(memory_space=pltpu.VMEM)


def cost(micros):
    return pl.CostEstimate(flops=int(micros * 8e8), bytes_accessed=1024, transcendentals=0)


def call(kernel, micros, outs, scratch, half, *operands):
    return pl.pallas_call(
        kernel,
        cost_estimate=cost(micros),
        out_shape=[jax.ShapeDtypeStruct(shape, kind) for shape, kind in outs],
        in_specs=[SMEM_SPEC] + [VMEM_SPEC] * len(operands),
        out_specs=[VMEM_SPEC] * len(outs),
        scratch_shapes=[pltpu.VMEM(shape, kind) for shape, kind in scratch],
        compiler_params=pltpu.CompilerParams(vmem_limit_bytes=VMEM_BYTES),
    )(half, *operands)


def columns(values):
    return jnp.broadcast_to(values[:, None], (values.shape[0], LANES))


def exchange(block, axes):
    return lax.all_to_all(block, axes, 0, 0, tiled=True)


def to_all(block, axes):
    count = lax.axis_size(axes)
    return exchange(jnp.broadcast_to(block[None], (count,) + block.shape), axes)


def strip_order():
    sent = np.arange(WB * C)
    natural = sent % WB * C + sent // WB % 4 * 8 + sent // LANES
    order = np.zeros((WB * C, WB * C), np.float32)
    order[sent, natural] = 1.0
    return order


def whole_clips(
    frames, valid, flags, actions, states, latent,
    w_enc, w_lstm, w_fc, w_cond, w_deconv, w_mask, vector,
    m_enc, m_lstm, m_fc, m_cond, m_deconv, m_mask, m_vector,
    v_enc, v_lstm, v_fc, v_cond, v_deconv, v_mask, v_vector,
):
    clips, shots, _, strip_rows, width = frames.shape
    steps = shots - 1
    own = steps // HALVES
    count = lax.axis_size("row")
    place = lax.axis_index("row")
    clip = place // HALVES
    half = place % HALVES
    half_1 = half.reshape(1).astype(jnp.int32)
    b_enc, g_enc, s_enc, b_lstm, b_fc, b_dec, b_mask = split_vector(vector)
    places, encoder = window_places()
    flagged = jnp.pad(valid.astype(BF), ((0, 0), (1, 0), (0, 0), (0, 0)))
    pieces = jnp.concatenate([frames, flagged[:, :, None]], axis=2).reshape(clips, shots, 4, 2, 2, width)
    pieces = jnp.transpose(pieces, (0, 1, 4, 2, 3, 5)).reshape(clips, shots * 8, LANES)
    pieces = jnp.pad(pieces, ((0, 0), (0, 8), (0, 0)))
    raw = exchange(jnp.repeat(pieces, HALVES, axis=0), "row")

    wide_enc = jnp.einsum(
        "rk,ko->or", jnp.asarray(encoder, BF), w_enc.astype(BF), preferred_element_type=F32
    ).astype(BF)
    bias = columns(
        jnp.concatenate([vector[: 7 * C], b_dec, jnp.pad(b_mask, (0, 16 - NM), constant_values=-1e30)])
    )
    cells = (steps, TILES, C, LANES)
    x, enc, hid, act, cell, strips_out = call(
        forward_kernel,
        20,
        [
            ((shots, TILES, 16, LANES), BF), (cells, BF), (cells, BF), ((steps, TILES, 4 * C, LANES), F32),
            (cells, F32), ((count, own, 16, LANES), BF),
        ],
        [
            ((6, 48, LANES), BF), ((8, KS * C, LANES), BF), ((8, KS * C, LANES), BF), ((TILES, C, LANES), F32),
            ((KK * C, LANES), BF), ((4 * C, KK * C), BF), ((4 * C, KK * C), BF),
        ],
        half_1, raw, wide_enc, w_lstm, bias,
    )
    items = clips * steps
    order = jnp.asarray(strip_order(), BF)
    k_fc = w_fc.astype(BF)
    strip_hid = exchange(strips_out, "row").reshape(items, 2, WB * C)
    strip_hid = jnp.einsum("mjk,kl->jml", strip_hid, order, preferred_element_type=F32).astype(BF)
    parts = jnp.einsum("jmk,jnk->mn", strip_hid, k_fc, preferred_element_type=F32)
    strip_hid_all = to_all(strip_hid, "clip")
    summed = jnp.sum(exchange(parts.reshape(count, own, NK * KK), "row"), 0)
    presence = flags.astype(F32)
    conditions = jnp.concatenate(
        [
            actions * presence[..., :1],
            states * presence[..., 1:],
            jnp.broadcast_to(latent[:, None, :], (clips, steps, latent.shape[1])),
        ],
        -1,
    )
    cond = lax.dynamic_slice(conditions, (clip, half * own, 0), (1, own, COND))[0]
    logits = summed + (jnp.dot(cond, w_cond, precision=HIGH) + b_fc)
    logits = jnp.pad(
        logits.reshape(own, NK, KK), ((0, 0), (1, 5), (0, 32 - KK)), constant_values=-1e30
    )
    dec, d_logit, d_dec, d_mask, head_sums = call(
        head_kernel,
        30,
        [
            ((own, TILES, C, LANES), BF), ((own, 16, 32), F32), ((C, 4 * C), F32), ((16, LANES), F32),
            ((200, LANES), F32),
        ],
        [
            ((6, 48, LANES), F32), ((C, 4 * C), BF), ((4 * C, C), BF), ((64, 12 * C), BF),
            ((4 * C, 192), BF), ((4 * C + 64, LANES), F32), ((64, 4 * C), F32),
            ((4 * WIN, 32), BF), ((32, 4 * WIN), BF), ((4 * WIN, TILES * LANES), BF), ((own, 64, 4 * WIN), F32),
            ((own, 16, 32), F32),
        ],
        half_1, x, hid, logits, w_deconv, w_mask.T, bias,
        jnp.asarray(places, BF), jnp.asarray(places.transpose(0, 2, 1), BF),
    )
    d_logit = d_logit[:, 1 : NK + 1, :KK].reshape(own, NK * KK)
    every_sum = to_all(d_logit.astype(BF), ("clip", "row")).reshape(-1, items, NK * KK)
    d_sum = lax.dynamic_index_in_dim(every_sum, lax.axis_index("clip"), 0, False)
    back_fc = jnp.einsum("mn,jnk->mjk", d_sum, k_fc, preferred_element_type=F32).astype(BF)
    back_fc = lax.dot_general(
        back_fc.reshape(items * 2, WB * C), order, (((1,), (1,)), ((), ())), preferred_element_type=F32
    ).astype(BF)
    back_fc = exchange(back_fc.reshape(count, own, 16, LANES), "row")
    swap = [(index, index ^ 1) for index in range(count)]

    def in_order(block):
        other = lax.ppermute(block, "row", swap)
        return jnp.stack([jnp.where(half == 0, block, other), jnp.where(half == 0, other, block)])

    keep, d_enc, lines = call(
        backward_kernel,
        16,
        [((own, TILES, 4 * C, LANES), BF), ((own, TILES, C, LANES), F32), ((4 * C, LANES), F32)],
        [
            ((8, 4 * C, LANES), BF), ((TILES, C, LANES), F32), ((TILES, C, LANES), F32),
            ((KS * 2 * C, KS * 4 * C), BF),
        ],
        half_1, act, cell, in_order(dec), in_order(back_fc), w_lstm,
    )
    groups = lax.axis_size("clip")

    strip_hid_all, every_sum, _ = lax.optimization_barrier((strip_hid_all, every_sum, lines))
    d_fc, fc_squares = pl.pallas_call(
        logit_map_kernel,
        cost_estimate=cost(2),
        out_shape=[
            jax.ShapeDtypeStruct((w_fc.size // LANES, LANES), F32), jax.ShapeDtypeStruct((1, LANES), F32)
        ],
        in_specs=[VMEM_SPEC] * 2,
        out_specs=[VMEM_SPEC] * 2,
        scratch_shapes=[pltpu.VMEM((NK * KK, groups * items), BF)],
        compiler_params=pltpu.CompilerParams(vmem_limit_bytes=VMEM_BYTES),
    )(strip_hid_all, every_sum)
    fc_squares = jnp.sum(fc_squares) / groups

    d_cond = jnp.dot(cond.T, d_logit, precision=HIGH)
    d_cond = jnp.pad(d_cond, ((0, 16 - COND), (0, 2 * LANES - NK * KK)))
    d_cond = jnp.concatenate([d_cond[:, :LANES], d_cond[:, LANES:]], axis=0)
    d_line = jnp.pad(d_logit, ((0, 0), (7 * C, 5 * LANES - 7 * C - NK * KK)))
    scalars = jnp.stack([jnp.zeros_like(fc_squares), jnp.sum(valid.astype(F32)), fc_squares])
    scalars = jnp.pad(scalars, (0, LANES - 3)).reshape(1, LANES)
    both = ("clip", "row")
    devices = lax.axis_size(both)
    block = call(
        pack_kernel,
        12,
        [((devices, PART, LANES), BF)],
        [
            ((6, 48, LANES), BF), ((8, KS * 2 * C, LANES), BF), ((C, WIN), F32), ((11 * C + 64, LANES), F32),
            ((ROWS, LANES), F32),
        ],
        half_1, x, enc, hid, keep, d_enc, lines, head_sums, d_dec, d_mask, d_cond, d_line, scalars, wide_enc, bias,
        jnp.asarray(vector_places(), F32), jnp.asarray(np.pad(encoder, ((0, 0), (0, LANES - KK * 3))), F32),
    )[0]
    sums, scalars = pl.pallas_call(
        total_kernel,
        out_shape=[jax.ShapeDtypeStruct(block.shape, BF), jax.ShapeDtypeStruct((1, LANES), F32)],
        in_specs=[VMEM_SPEC],
        out_specs=[VMEM_SPEC, VMEM_SPEC],
        compiler_params=pltpu.CompilerParams(vmem_limit_bytes=VMEM_BYTES),
    )(exchange(block, both))
    sums = exchange(sums, both)
    rates = learning_rates(w_fc.shape[0] * count)

    def shown(group):
        enc, lstm, fc, cond, dec, mask, line = group
        fc = fc.reshape(2, NK * KK, WB * C // LANES, LANES)
        fc = jnp.transpose(fc, (1, 2, 0, 3)).reshape(-1, LANES)
        return [enc.T, lstm, fc, cond, dec, mask.T, line.reshape(1, -1)]

    def back(group):
        enc, lstm, fc, cond, dec, mask, line = group
        fc = fc.reshape(NK * KK, WB * C // LANES, 2, LANES)
        fc = jnp.transpose(fc, (2, 0, 1, 3)).reshape(w_fc.shape)
        return [enc.T, lstm, fc, cond, dec, mask.T, line.reshape(-1)]

    weights = shown([w_enc, w_lstm, w_fc, w_cond, w_deconv, w_mask, vector])
    firsts = shown([m_enc, m_lstm, m_fc, m_cond, m_deconv, m_mask, m_vector])
    seconds = shown([v_enc, v_lstm, v_fc, v_cond, v_deconv, v_mask, v_vector])
    shapes = [jax.ShapeDtypeStruct(value.shape, F32) for value in weights]
    any_spec = pl.BlockSpec(memory_space=pl.ANY)
    places_out = [VMEM_SPEC, any_spec, any_spec] + [VMEM_SPEC] * 4
    new = pl.pallas_call(
        functools.partial(update_kernel, rates),
        out_shape=[jax.ShapeDtypeStruct((), F32)] + shapes * 3,
        in_specs=[VMEM_SPEC] * 24,
        out_specs=[SMEM_SPEC] + places_out * 3,
        scratch_shapes=[
            pltpu.VMEM((ROWS, LANES), F32), pltpu.VMEM((3,) + shapes[2].shape, F32),
            pltpu.VMEM((3,) + shapes[1].shape, F32), pltpu.SemaphoreType.DMA((21,)),
        ],
        compiler_params=pltpu.CompilerParams(vmem_limit_bytes=VMEM_BYTES),
    )(sums, scalars, d_fc, *weights, *firsts, *seconds)
    outs = [scalars[0, 0], scalars[0, 1], new[0]]
    for kind in range(3):
        outs.extend(back(new[1 + 7 * kind : 8 + 7 * kind]))
    return tuple(outs)


def shards(frames, *rest):
    clips, _, _, strip_rows, width = frames.shape
    count = lax.axis_size("row")
    one_clip = strip_rows * count // 2 == TILES * BANDS and width // 2 == WB
    if one_clip and clips * HALVES == count:
        return whole_clips(frames, *rest)
    return strips(frames, *rest)


def solution(mesh):
    placed = (
        P("clip", None, None, "row", None),
        P("clip", None, "row", None),
        P("clip", None, None),
        P("clip", None, None),
        P("clip", None, None),
        P("clip", None),
        P(),
        P(),
        P("row", None, None),
        P(),
        P(),
        P(),
        P(),
        P(),
        P(),
        P("row", None, None),
        P(),
        P(),
        P(),
        P(),
        P(),
        P(),
        P("row", None, None),
        P(),
        P(),
        P(),
        P(),
    )
    return jax.shard_map(
        shards,
        mesh=mesh,
        in_specs=placed,
        out_specs=(
            P(),
            P(),
            P(),
            P(),
            P(),
            P("row", None, None),
            P(),
            P(),
            P(),
            P(),
            P(),
            P(),
            P("row", None, None),
            P(),
            P(),
            P(),
            P(),
            P(),
            P(),
            P("row", None, None),
            P(),
            P(),
            P(),
            P(),
        ),
        check_vma=False,
    )
```

```python
import functools

import jax
import jax.numpy as jnp
import numpy as np
from jax import lax
from jax.experimental import pallas as pl
from jax.experimental.pallas import tpu as pltpu
from jax.sharding import PartitionSpec as P

C = 32
KS = 5
NK = 10
STEP_NO = 10
KK = 25
NM = 11
COND = 15
WB = 32


NORM_EPS = 1e-05
CLIP_NORM = 0.001
BETA_ONE = 0.9
BETA_TWO = 0.999
ADAM_EPS = 1e-12
DECAY = 0.01
HIGH = lax.Precision.HIGHEST


def padded_2(cells, sides, width):
    for axis, dim in sides:
        count = lax.axis_size(axis)
        ends = count - 1
        head = lax.slice_in_dim(cells, 0, width, axis=dim)
        tail = lax.slice_in_dim(cells, cells.shape[dim] - width, cells.shape[dim], axis=dim)
        cells = jnp.concatenate(
            [
                lax.ppermute(tail, axis, [(i, (i + 1) % count) for i in range(ends)]),
                cells,
                lax.ppermute(head, axis, [((i + 1) % count, i) for i in range(ends)]),
            ],
            axis=dim,
        )
    return cells


def passed_along(block, axis, distance):
    devices = range(lax.axis_size(axis))
    route = [(i - distance, i) for i in devices if i - distance in devices]
    return lax.ppermute(block, axis, route)


def split_vector(vector):
    counts = [C, C, C, 4 * C, NK * KK, C, NM]
    pieces = []
    start = 0
    for count in counts:
        pieces.append(vector[start : start + count])
        start += count
    return pieces


def norm_act(pre, gain, shift):
    centered = pre - jnp.mean(pre, -1, keepdims=True)
    scale = lax.rsqrt(jnp.mean(centered * centered, -1, keepdims=True) + NORM_EPS)
    return jax.nn.silu(centered * scale * gain + shift)


def cell_step(gates, cell):
    gate_in, gate_keep, gate_out, gate_new = jnp.split(gates, 4, axis=-1)
    new_cell = jax.nn.sigmoid(gate_keep + 1.0) * cell + jax.nn.sigmoid(gate_in) * jnp.tanh(gate_new)
    return (jax.nn.sigmoid(gate_out) * jnp.tanh(new_cell), new_cell)


def upsample(values):
    clips, rows_in, cols_in, depth = values.shape
    grid = values.reshape(clips, rows_in, cols_in, 2, 2, depth // 4)
    return jnp.transpose(grid, (0, 1, 3, 2, 4, 5)).reshape(
        clips, 2 * rows_in, 2 * cols_in, depth // 4
    )


def predict(logits, upper, w_mask, b_mask, prev_pad):
    clips = logits.shape[0]
    kernels = jax.nn.softmax(logits.reshape(clips, NK, KK), axis=-1)
    activated = jax.nn.silu(upper)
    blend = jax.nn.softmax(
        jnp.einsum("byxc,cm->byxm", activated, w_mask, precision=HIGH) + b_mask, axis=-1
    )
    mixing = jnp.einsum("byxk,bko->byxo", blend[..., 1:], kernels, precision=HIGH)
    height = prev_pad.shape[1] - 4
    breadth = prev_pad.shape[2] - 4
    result = blend[..., :1] * prev_pad[:, 2 : 2 + height, 2 : 2 + breadth, :]
    for offset in range(KK):
        top = offset // KS
        left = offset % KS
        result = (
            result
            + mixing[..., offset : offset + 1]
            * prev_pad[:, top : top + height, left : left + breadth, :]
        )
    return result


def patches(padded, stride, out_rows, out_cols):
    pieces = []
    for offset in range(KK):
        top = offset // KS
        left = offset % KS
        pieces.append(
            padded[
                :,
                top : top + stride * (out_rows - 1) + 1 : stride,
                left : left + stride * (out_cols - 1) + 1 : stride,
                :,
            ]
        )
    return jnp.concatenate(pieces, -1)


def unpatch(grads, shape, stride):

    def extract(padded):
        return patches(padded, stride, grads.shape[1], grads.shape[2])

    _, pullback = jax.vjp(extract, jnp.zeros(shape, jnp.float32))
    return pullback(grads)[0]


def product(left, right, form):
    return jnp.einsum(form, left, right, preferred_element_type=jnp.float32)


def learning_rates(rows_total):
    return [
        0.5 * (KK * 3) ** (-0.5),
        0.5 * (KK * 2 * C) ** (-0.5),
        0.5 * (rows_total * WB * C // 16) ** (-0.5),
        0.5 * COND ** (-0.5),
        0.5 * C ** (-0.5),
        0.5 * (C // 4) ** (-0.5),
        0.1,
    ]


def adam(weight, grad, first, second, rate):
    first = BETA_ONE * first + (1.0 - BETA_ONE) * grad
    second = BETA_TWO * second + (1.0 - BETA_TWO) * grad * grad
    update = (
        first
        / (1.0 - BETA_ONE**STEP_NO)
        / (jnp.sqrt(second / (1.0 - BETA_TWO**STEP_NO)) + ADAM_EPS)
    )
    return (weight - rate * (update + DECAY * weight), first, second)


def strips(
    frames,
    valid,
    flags,
    actions,
    states,
    latent,
    w_enc,
    w_lstm,
    w_fc,
    w_cond,
    w_deconv,
    w_mask,
    vector,
    m_enc,
    m_lstm,
    m_fc,
    m_cond,
    m_deconv,
    m_mask,
    m_vector,
    v_enc,
    v_lstm,
    v_fc,
    v_cond,
    v_deconv,
    v_mask,
    v_vector,
):
    clips = frames.shape[0]
    out_rows = frames.shape[3] // 2
    out_cols = frames.shape[4] // 2
    b_enc, g_enc, s_enc, b_lstm, b_fc, b_dec, b_mask = split_vector(vector)
    k_enc = w_enc.astype(jnp.bfloat16)
    k_lstm = w_lstm.astype(jnp.bfloat16)
    k_fc = w_fc.astype(jnp.bfloat16)
    k_dec = w_deconv.astype(jnp.bfloat16)
    images = jnp.transpose(frames, (1, 0, 3, 4, 2))
    padded = padded_2(images, (("row", 2),), 2)
    padded = jnp.pad(padded, ((0, 0), (0, 0), (0, 0), (2, 2), (0, 0)))
    valid_steps = jnp.transpose(valid.astype(jnp.float32), (1, 0, 2, 3))
    presence = flags.astype(jnp.float32)
    conditions = jnp.concatenate(
        [
            actions * presence[..., :1],
            states * presence[..., 1:],
            jnp.broadcast_to(latent[:, None, :], (clips, actions.shape[1], latent.shape[1])),
        ],
        -1,
    )
    conditions = jnp.transpose(conditions, (1, 0, 2))
    valid_count = lax.psum(jnp.sum(valid_steps), ("clip", "row"))
    inv_count = 1.0 / valid_count

    def advance(carry, image_pad):
        hidden, cell = carry
        pre = product(patches(image_pad, 2, out_rows, out_cols), k_enc, "byxk,kc->byxc") + b_enc
        encoded = norm_act(pre, g_enc, s_enc).astype(jnp.bfloat16)
        joined = jnp.concatenate([encoded, hidden], -1)
        joined_pad = padded_2(joined, (("row", 1),), 2)
        joined_pad = jnp.pad(joined_pad, ((0, 0), (0, 0), (2, 2), (0, 0)))
        gates = (
            product(patches(joined_pad, 1, out_rows, out_cols), k_lstm, "byxk,kg->byxg") + b_lstm
        )
        new_hidden, new_cell = cell_step(gates, cell)
        hidden_low = new_hidden.astype(jnp.bfloat16)
        part = product(hidden_low.reshape(clips, out_rows, -1), k_fc, "bjk,jnk->bn")
        part = lax.psum(part, "row")
        upper = product(hidden_low, k_dec, "byxc,cd->byxd")
        return ((hidden_low, new_cell), (pre, joined_pad, gates, cell, hidden_low, part, upper))

    start = (
        jnp.zeros((clips, out_rows, out_cols, C), jnp.bfloat16),
        jnp.zeros((clips, out_rows, out_cols, C), jnp.float32),
    )
    _, saved = lax.scan(advance, start, padded[:-1])
    pre_all, joined_all, gates_all, cells_all, hidden_all, summed_all, uppers = saved
    targets = images[1:].astype(jnp.float32)

    def local_head(item):
        summed_t, upper_t, image_pad, target, mask, cond = item

        def error_of(summed_t, upper_t, w_cond, w_mask, b_fc, b_dec, b_mask):
            logits = summed_t + jnp.dot(cond, w_cond, precision=HIGH) + b_fc
            upper_full = upsample(upper_t) + b_dec
            result = predict(logits, upper_full, w_mask, b_mask, image_pad.astype(jnp.float32))
            return jnp.sum(mask * jnp.sum((result - target) ** 2, -1))

        error, pullback = jax.vjp(error_of, summed_t, upper_t, w_cond, w_mask, b_fc, b_dec, b_mask)
        return (error, pullback(inv_count))

    head_inputs = (summed_all, uppers, padded[:-1], targets, valid_steps, conditions)

    def retreat(carry, item):
        (
            back_hidden,
            back_cell,
            acc_enc,
            acc_lstm,
            acc_dec,
            acc_benc,
            acc_genc,
            acc_senc,
            acc_blstm,
        ) = carry
        saved_t, head_t = item
        pre, joined_pad, gates, cell_prev, hidden_low, image_pad = saved_t
        error, pulled_t = local_head(head_t)
        d_sum = lax.psum(pulled_t[0], "row")
        d_upper = pulled_t[1]
        extra = (error, pulled_t[2:])
        d_sum_low = d_sum.astype(jnp.bfloat16)
        d_upper_low = d_upper.astype(jnp.bfloat16)
        acc_dec = acc_dec + product(hidden_low, d_upper_low, "byxc,byxd->cd")
        back = back_hidden + product(d_upper_low, k_dec, "byxd,cd->byxc")
        back = back + product(d_sum_low, k_fc, "bn,jnk->bjk").reshape(back_hidden.shape)
        _, cell_pull = jax.vjp(cell_step, gates, cell_prev)
        d_gates, back_cell = cell_pull((back, back_cell))
        d_gates_low = d_gates.astype(jnp.bfloat16)
        acc_blstm = acc_blstm + jnp.sum(d_gates, (0, 1, 2))
        acc_lstm = acc_lstm + product(
            patches(joined_pad, 1, out_rows, out_cols), d_gates_low, "byxk,byxg->kg"
        )
        d_pad = unpatch(product(d_gates_low, k_lstm, "byxg,kg->byxk"), joined_pad.shape, 1)[
            :, :, 2:-2, :
        ]
        from_below = passed_along(d_pad[:, :2], "row", -1)
        from_above = passed_along(d_pad[:, -2:], "row", 1)
        d_joined = d_pad[:, 2:-2].at[:, -2:].add(from_below).at[:, :2].add(from_above)
        _, norm_pull = jax.vjp(norm_act, pre, g_enc, s_enc)
        d_pre, d_gain, d_shift = norm_pull(d_joined[..., :C])
        acc_benc = acc_benc + jnp.sum(d_pre, (0, 1, 2))
        acc_genc = acc_genc + d_gain
        acc_senc = acc_senc + d_shift
        acc_enc = acc_enc + product(
            patches(image_pad, 2, out_rows, out_cols), d_pre.astype(jnp.bfloat16), "byxk,byxc->kc"
        )
        new_carry = (
            d_joined[..., C:],
            back_cell,
            acc_enc,
            acc_lstm,
            acc_dec,
            acc_benc,
            acc_genc,
            acc_senc,
            acc_blstm,
        )
        return (new_carry, (d_sum_low, extra))

    zeros_state = jnp.zeros((clips, out_rows, out_cols, C), jnp.float32)
    zeros_small = jnp.zeros((C,), jnp.float32)
    init = (
        zeros_state,
        zeros_state,
        jnp.zeros(w_enc.shape, jnp.float32),
        jnp.zeros(w_lstm.shape, jnp.float32),
        jnp.zeros(w_deconv.shape, jnp.float32),
        zeros_small,
        zeros_small,
        zeros_small,
        jnp.zeros((4 * C,), jnp.float32),
    )
    final, (d_sums_low, extra) = lax.scan(
        retreat,
        init,
        ((pre_all, joined_all, gates_all, cells_all, hidden_all, padded[:-1]), head_inputs),
        reverse=True,
    )
    error_sum = jnp.sum(extra[0])
    head_sums = [jnp.sum(grad, 0) for grad in extra[1]]
    acc_enc, acc_lstm, acc_dec, acc_benc, acc_genc, acc_senc, acc_blstm = final[2:]
    flat_hidden = hidden_all.reshape(hidden_all.shape[0], clips, out_rows, -1)
    d_fc = lax.psum(
        product(flat_hidden, d_sums_low, "tbjk,tbn->jnk").astype(jnp.bfloat16), "clip"
    ).astype(jnp.float32)
    fc_squares = jnp.sum(d_fc * d_fc) / lax.axis_size("clip")
    d_vector = jnp.concatenate(
        [acc_benc, acc_genc, acc_senc, acc_blstm, head_sums[2], head_sums[3], head_sums[4]]
    )
    d_enc, d_lstm, d_cond, d_dec, d_mask, d_vector, loss_sum, squares = lax.psum(
        (acc_enc, acc_lstm, head_sums[0], acc_dec, head_sums[1], d_vector, error_sum, fc_squares),
        ("clip", "row"),
    )
    grads = (d_enc, d_lstm, d_fc, d_cond, d_dec, d_mask, d_vector)
    for index in (0, 1, 3, 4, 5, 6):
        squares = squares + jnp.sum(grads[index] * grads[index])
    grad_norm = jnp.sqrt(squares)
    factor = CLIP_NORM / jnp.maximum(grad_norm, CLIP_NORM)
    rates = learning_rates(w_fc.shape[0] * lax.axis_size("row"))
    weights = (w_enc, w_lstm, w_fc, w_cond, w_deconv, w_mask, vector)
    firsts = (m_enc, m_lstm, m_fc, m_cond, m_deconv, m_mask, m_vector)
    seconds = (v_enc, v_lstm, v_fc, v_cond, v_deconv, v_mask, v_vector)
    new = [
        adam(weights[index], grads[index] * factor, firsts[index], seconds[index], rates[index])
        for index in range(7)
    ]
    return (
        loss_sum,
        valid_count,
        grad_norm,
        new[0][0],
        new[1][0],
        new[2][0],
        new[3][0],
        new[4][0],
        new[5][0],
        new[6][0],
        new[0][1],
        new[1][1],
        new[2][1],
        new[3][1],
        new[4][1],
        new[5][1],
        new[6][1],
        new[0][2],
        new[1][2],
        new[2][2],
        new[3][2],
        new[4][2],
        new[5][2],
        new[6][2],
    )


LANES = 128
TILES = 4
BANDS = 4
HALVES = 2
FAR = 1
WIN = 9 * 16
BF = jnp.bfloat16
F32 = jnp.float32
VMEM_BYTES = 56 * 1024 * 1024


def window_places():
    places = np.zeros((4, WIN, 32), np.float32)
    encoder = np.zeros((WIN, KK * 3), np.float32)
    for sub in range(4):
        for tap in range(KK):
            off_y = tap // KS - 2 + sub // 2
            off_x = tap % KS - 2 + sub % 2
            block = (off_y // 2 + 1) * 3 + off_x // 2 + 1
            base = block * 16 + (off_x % 2) * 8 + (off_y % 2) * 4
            for channel in range(3):
                places[sub, base + channel, tap] = 1.0
                if sub == 0:
                    encoder[base + channel, tap * 3 + channel] = 1.0
    return places, encoder


def lane_places():
    lane = lax.broadcasted_iota(jnp.int32, (8, LANES), 1)
    return lane % WB, lane // WB


def moved(tile, lanes, d_col, d_band):
    if d_col == 0 and d_band == 0:
        return tile
    col, band = lanes
    rows = tile.shape[0]
    shift = (-(WB * d_band + d_col)) % LANES
    rolled = pltpu.roll(tile.reshape(rows // 8, 8, LANES), shift, 2)
    keep = None
    for place, delta, count in ((col, d_col, WB), (band, d_band, BANDS)):
        if delta > 0:
            inside = place < count - delta
        elif delta < 0:
            inside = place >= -delta
        else:
            continue
        keep = inside if keep is None else keep & inside
    return jnp.where(keep[None], rolled, 0.0).reshape(rows, LANES)


def spread(tiles, lanes, reach, target, width, start):
    rows = tiles[0].shape[0]
    for index in range(TILES + 2 * reach):
        tile = index - reach
        for shift in range(2 * reach + 1):
            place = shift * width + start
            target[index, place : place + rows, :] = moved(
                tiles[tile % TILES], lanes, shift - reach, tile // TILES
            ).astype(target.dtype)


def stacked(ref, tile, count):
    rows = count * ref.shape[1]
    return jnp.concatenate(
        [ref[tile : tile + count].reshape(rows, LANES), ref[tile + 1 : tile + 1 + count].reshape(rows, LANES)],
        axis=1,
    )


def nn(left, right):
    return lax.dot_general(left, right, (((1,), (0,)), ((), ())), preferred_element_type=F32)


def nt(left, right):
    return lax.dot_general(left, right, (((1,), (1,)), ((), ())), preferred_element_type=F32)


def nn_exact(left, right):
    return lax.dot_general(left, right, (((1,), (0,)), ((), ())), preferred_element_type=F32, precision=HIGH)


def nt_exact(left, right):
    return lax.dot_general(left, right, (((1,), (1,)), ((), ())), preferred_element_type=F32, precision=HIGH)


def logistic(v):
    return 0.5 * jnp.tanh(0.5 * v) + 0.5


def one_hot_eye(size):
    row = lax.broadcasted_iota(jnp.int32, (size, size), 0)
    return (row == lax.broadcasted_iota(jnp.int32, (size, size), 1)).astype(BF)


def split(value):
    high = value.astype(BF)
    return high, (value - high.astype(F32)).astype(BF)


def one_hot_mod(shape, period, axis):
    folded = lax.broadcasted_iota(jnp.int32, shape, axis) % period
    return (folded == lax.broadcasted_iota(jnp.int32, shape, 1 - axis)).astype(BF)


def unpack_images(raw_ref, x_ref):
    source = lax.broadcasted_iota(jnp.int32, (LANES, 4 * LANES), 0)
    goal = lax.broadcasted_iota(jnp.int32, (LANES, 4 * LANES), 1)
    same = (source // 64 == goal // 256) & (source % 2 == goal // LANES % 2) & (source // 2 % WB == goal % WB)
    picks = [(same & (goal // WB % BANDS == band)).astype(BF) for band in range(BANDS)]
    for pair in range(2):
        total = nn(raw_ref[pair], picks[0])
        for band in range(1, BANDS):
            total = total + nn(raw_ref[2 * band + pair], picks[band])
        for t in range(x_ref.shape[0]):
            rows = total[8 * t : 8 * t + 8]
            for low_row in range(2):
                start = 2 * LANES * low_row
                x_ref[t, 2 * pair + low_row] = jnp.concatenate(
                    [rows[:, start : start + LANES], rows[:, start + LANES : start + 2 * LANES]], axis=0
                ).astype(BF)


def image_tiles(x_ref, t):
    return [x_ref[t, tile].astype(F32) for tile in range(TILES)]


def block_swap(parts, band):
    swapped = []
    for out in range(BANDS):
        total = None
        for part in range(BANDS):
            shift = (WB * (part - out)) % LANES
            value = parts[part] if shift == 0 else pltpu.roll(parts[part], shift, 1)
            total = value if total is None else jnp.where(band == part, value, total)
        swapped.append(total)
    return swapped


def wide(tile):
    return jnp.concatenate([tile] * TILES, axis=1)


def folded(values):
    total = values[:, :LANES]
    for tile in range(1, values.shape[1] // LANES):
        total = total + values[:, tile * LANES : (tile + 1) * LANES]
    return total


def twice(tile):
    return jnp.concatenate([tile, tile], axis=1)


def forward_kernel(
    half_ref, raw_ref, we_ref, w_ref, bias_ref,
    x_ref, enc_ref, hid_ref, act_ref, cell_ref, strip_ref,
    win_s, enc_s, hid_s, state_s, rows_s, wx_s, wh_s, even_s, odd_s,
):
    steps = hid_ref.shape[0]
    lanes = lane_places()
    for kind, target in ((0, wx_s), (1, wh_s)):
        for tap in range(KK):
            start = tap * 2 * C + kind * C
            rows_s[tap * C : (tap + 1) * C, :] = w_ref[start : start + C, :].astype(BF)
        target[...] = nt(one_hot_eye(4 * C), rows_s[...]).astype(BF)
    unpack_images(raw_ref, x_ref)

    def encode(t, gates_s):
        spread(image_tiles(x_ref, t), lanes, 1, win_s, 16, 0)
        tiles = []
        for two in range(0, TILES, 2):
            pre = nn(we_ref[...], stacked(win_s, two, 3)) + twice(bias_ref[0:C])
            centered = pre - jnp.mean(pre, 0, keepdims=True)
            scale = lax.rsqrt(jnp.mean(centered * centered, 0, keepdims=True) + NORM_EPS)
            value = centered * scale * twice(bias_ref[C : 2 * C]) + twice(bias_ref[2 * C : 3 * C])
            value = (value * logistic(value)).astype(BF)
            for one in range(2):
                part = value[:, one * LANES : (one + 1) * LANES]
                enc_ref[t, two + one] = part
                tiles.append(part.astype(F32))
        spread(tiles, lanes, 2, enc_s, C, 0)
        for two in range(0, TILES, 2):
            gates = nn(wx_s[...], stacked(enc_s, two, KS)) + twice(bias_ref[3 * C : 7 * C])
            for one in range(2):
                gates_s[two + one] = gates[:, one * LANES : (one + 1) * LANES]

    hid_s[...] = jnp.zeros_like(hid_s)
    state_s[...] = jnp.zeros_like(state_s)

    def advance(t, gates_s, later_s):
        sums = [nn(wh_s[...], stacked(hid_s, two, KS)) for two in range(0, TILES, 2)]
        encode(t + 1, later_s)
        hidden = []
        for tile in range(TILES):
            start = tile % 2 * LANES
            gates = gates_s[tile] + sums[tile // 2][:, start : start + LANES]
            gate_in = logistic(gates[0:C])
            gate_keep = logistic(gates[C : 2 * C] + 1.0)
            gate_out = logistic(gates[2 * C : 3 * C])
            gate_new = jnp.tanh(gates[3 * C : 4 * C])
            cell = gate_keep * state_s[tile] + gate_in * gate_new
            act_ref[t, tile, 0:C] = gate_in
            act_ref[t, tile, C : 2 * C] = gate_keep
            act_ref[t, tile, 2 * C : 3 * C] = gate_out
            act_ref[t, tile, 3 * C : 4 * C] = gate_new
            state_s[tile] = cell
            cell_ref[t, tile] = cell
            low = (gate_out * jnp.tanh(cell)).astype(BF)
            hid_ref[t, tile] = low
            hidden.append(low.astype(F32))
        spread(hidden, lanes, 2, hid_s, C, 0)

    encode(0, even_s)

    def advance_two(pair, _):
        advance(2 * pair, even_s, odd_s)
        advance(2 * pair + 1, odd_s, even_s)
        return 0

    lax.fori_loop(0, steps // 2, advance_two, 0)
    own = steps // HALVES
    base = half_ref[0] * own

    def to_strips(i, _):
        for pair in range(2):
            rows = []
            for low_row in range(2):
                tile = hid_ref[base + i, 2 * pair + low_row].astype(F32)
                rows.append(block_swap([tile[8 * q : 8 * q + 8] for q in range(4)], lanes[1]))
            for band in range(BANDS):
                strip_ref[2 * band + pair, i] = jnp.concatenate(
                    [rows[0][band], rows[1][band]], axis=0
                ).astype(BF)
        return 0

    lax.fori_loop(0, own, to_strips, 0)


def head_kernel(
    half_ref, x_ref, hid_ref, logit_ref, w_ref, mask_ref, bias_ref, place_ref, placet_ref,
    back_ref, dlog_ref, dwd_ref, dwm_ref, sums_ref,
    even_s, odd_s, wd_ref, wdt_ref, wm_ref, wmt_ref, over_ref, wide_s, everywhere_s, turned_s, d_even_s, d_odd_s,
    d_spot_s, kernel_s,
):
    wd_ref[...] = w_ref[...].astype(BF)
    wdt_ref[...] = nt(one_hot_eye(4 * C), wd_ref[...]).astype(BF)
    row = lax.broadcasted_iota(jnp.int32, (4 * C, 64), 0)
    mine_t = row // C == lax.broadcasted_iota(jnp.int32, (4 * C, 64), 1) // 16
    row = lax.broadcasted_iota(jnp.int32, (64, 4 * C), 0)
    mine = row // 16 == lax.broadcasted_iota(jnp.int32, (64, 4 * C), 1) // C
    for kind, part in enumerate(split(mask_ref[...])):
        spread_mask = nt(one_hot_mod((4 * C, C), C, 0), part).astype(BF)
        wide_t = jnp.where(mine_t, nn(spread_mask, one_hot_mod((NM, 64), 16, 1)), 0.0).astype(BF)
        wide_m = jnp.where(mine, nt(one_hot_mod((64, NM), 16, 0), spread_mask), 0.0).astype(BF)
        wmt_ref[:, kind * 64 : kind * 64 + 64] = wide_t
        wm_ref[:, kind * 4 * C : (kind + 1) * 4 * C] = wide_m
        if kind == 0:
            wmt_ref[:, 128:192] = wide_t
            wm_ref[:, 8 * C : 12 * C] = wide_m
    for sub in range(4):
        over_ref[sub * C : (sub + 1) * C, :] = bias_ref[7 * C : 8 * C]
        over_ref[4 * C + sub * 16 : 4 * C + (sub + 1) * 16, :] = bias_ref[8 * C : 8 * C + 16]
    own = logit_ref.shape[0]
    base = half_ref[0] * own
    lanes = lane_places()
    dwd_ref[...] = jnp.zeros_like(dwd_ref)
    wide_s[...] = jnp.zeros_like(wide_s)
    sums_ref[...] = jnp.zeros_like(sums_ref)
    cells = TILES * LANES
    row8 = lax.broadcasted_iota(jnp.int32, (8, cells), 0)
    color = (row8 % 4) != 3
    row16 = lax.broadcasted_iota(jnp.int32, (16, 32), 0)
    lane16 = lax.broadcasted_iota(jnp.int32, (16, 32), 1)

    for sub in range(4):
        everywhere_s[sub * WIN : (sub + 1) * WIN] = place_ref[sub]
        turned_s[:, sub * WIN : (sub + 1) * WIN] = placet_ref[sub]
    row = lax.broadcasted_iota(jnp.int32, (4 * WIN, 64), 0) // WIN
    own_spots = row == lax.broadcasted_iota(jnp.int32, (4 * WIN, 64), 1) // 16
    row = lax.broadcasted_iota(jnp.int32, (64, 4 * WIN), 0) // 16
    own_turned = row == lax.broadcasted_iota(jnp.int32, (64, 4 * WIN), 1) // WIN

    def frame(i, win_s, d_mix_s):
        t = base + i
        spread(image_tiles(x_ref, t), lanes, 1, win_s, 16, 0)
        window = jnp.concatenate([win_s[tile : tile + 3].reshape(WIN, LANES) for tile in range(TILES)], axis=1)
        window = window.reshape(18, 8, cells)
        logits = logit_ref[i]
        powers = jnp.exp(logits - jnp.max(logits, -1, keepdims=True))
        kernels = powers / jnp.sum(powers, -1, keepdims=True)
        kernels = jnp.where(row16 == 0, (lane16 == KK // 2).astype(F32), jnp.where(row16 <= NK, kernels, 0.0))
        kernel_s[i] = kernels
        spots = []
        turned = []
        for part in split(kernels):
            part = jnp.concatenate([part, part, part, part], axis=0)
            spots.append(jnp.where(own_spots, nt(everywhere_s[...], part), 0.0).astype(BF))
            turned.append(jnp.where(own_turned, nn(part, turned_s[...]), 0.0).astype(BF))
        spots = jnp.concatenate([spots[0], spots[1], spots[0]], axis=1)
        turned = jnp.concatenate(turned, axis=0)
        hidden = jnp.concatenate([hid_ref[t, tile] for tile in range(TILES)], axis=1)
        upper = nn(wdt_ref[...], hidden) + wide(over_ref[0 : 4 * C])
        gate = logistic(upper)
        active, active_rest = split(upper * gate)
        scores = nn(wm_ref[...], jnp.concatenate([active, active, active_rest], axis=0)) + wide(over_ref[4 * C : 4 * C + 64])
        scores = scores.reshape(4, 16, cells)
        powers = jnp.exp(scores - jnp.max(scores, 1, keepdims=True))
        masks = powers / jnp.sum(powers, 1, keepdims=True)
        mask_low, mask_rest = split(masks.reshape(64, cells))
        mixing = nn(spots, jnp.concatenate([mask_low, mask_low, mask_rest], axis=0)).reshape(4, 18, 8, cells)
        after = jnp.concatenate([x_ref[t + 1, tile] for tile in range(TILES)], axis=1).astype(F32)
        lost = None
        for sub in range(4):
            both = jnp.sum(mixing[sub] * window, 0)
            result = both + pltpu.roll(both, 4, 0)
            goal = after[(sub % 2) * 8 : (sub % 2) * 8 + 8]
            goal = jnp.where((row8 < 4) == (sub // 2 == 0), goal, pltpu.roll(goal, 4, 0))
            diff = jnp.where(color, result - goal, 0.0)
            weighted = diff * goal[3:4]
            part = weighted * diff
            lost = part if lost is None else lost + part
            d_result = 2.0 * weighted
            d_mix_s[sub * WIN : (sub + 1) * WIN] = (window * d_result[None]).reshape(WIN, cells).astype(BF)
        sums_ref[192:200] += folded(lost)
        d_mask = nn(turned, d_mix_s[...])
        d_mask = (d_mask[:64] + d_mask[64:]).reshape(4, 16, cells)
        d_spot_s[i] = nt(mask_low, d_mix_s[...])
        inner = jnp.sum(masks * d_mask, 1, keepdims=True)
        d_score = (masks * (d_mask - inner)).reshape(64, cells)
        sums_ref[128:192] += folded(d_score)
        d_score_low, d_score_rest = split(d_score)
        d_active = nn(wmt_ref[...], jnp.concatenate([d_score_low, d_score_low, d_score_rest], axis=0))
        wide_s[...] += nt(d_score_low, active)
        d_upper = d_active * (gate * (1.0 + upper * (1.0 - gate)))
        sums_ref[0:128] += folded(d_upper)
        d_upper_low = d_upper.astype(BF)
        dwd_ref[...] += nt(hidden, d_upper_low)
        back = nn(wd_ref[...], d_upper_low).astype(BF)
        for tile in range(TILES):
            back_ref[i, tile] = back[:, tile * LANES : (tile + 1) * LANES]

    def two_frames(pair, _):
        frame(2 * pair, even_s, d_even_s)
        frame(2 * pair + 1, odd_s, d_odd_s)
        return 0

    lax.fori_loop(0, own // 2, two_frames, 0)
    d_kernels = None
    for sub in range(4):
        rows = jnp.concatenate([d_spot_s[i, sub * 16 : sub * 16 + 16] for i in range(own)], axis=0)
        place = lax.broadcasted_iota(jnp.int32, rows.shape, 1) // WIN
        part = nn_exact(jnp.where(place == sub, rows, 0.0), everywhere_s[...].astype(F32))
        d_kernels = part if d_kernels is None else d_kernels + part
    for i in range(own):
        kernels = kernel_s[i]
        d_one = d_kernels[16 * i : 16 * i + 16]
        inner = jnp.sum(d_one * kernels, -1, keepdims=True)
        dlog_ref[i] = kernels * (d_one - inner)
    row = lax.broadcasted_iota(jnp.int32, (64, 4 * C), 0)
    lane = lax.broadcasted_iota(jnp.int32, (64, 4 * C), 1)
    own_block = jnp.where(row // 16 == lane // C, wide_s[...], 0.0)
    fold = lax.broadcasted_iota(jnp.int32, (4 * C, LANES), 0) % C
    fold = (fold == lax.broadcasted_iota(jnp.int32, (4 * C, LANES), 1)).astype(F32)
    dwm_ref[...] = jnp.sum(nn_exact(own_block, fold).reshape(4, 16, LANES), 0)


def backward_kernel(
    half_ref, act_ref, cell_ref, dec_ref, other_dec_ref, fc_ref, other_fc_ref, w_ref,
    keep_ref, denc_ref, lines_ref,
    gate_s, back_s, state_s, wb_s, even_s, odd_s,
):
    for tap in range(KK):
        place = tap % KS * 2 * C
        turn = (KS - 1 - tap // KS) * 4 * C
        wb_s[place : place + 2 * C, turn : turn + 4 * C] = w_ref[tap * 2 * C : (tap + 1) * 2 * C, :].astype(BF)
    steps = act_ref.shape[0]
    own = steps // HALVES
    base = half_ref[0] * own
    lanes = lane_places()
    back_s[...] = jnp.zeros_like(back_s)
    state_s[...] = jnp.zeros_like(state_s)
    lines_ref[...] = jnp.zeros_like(lines_ref)

    def prepare(t, factor_s):
        half = t // own
        inside = t % own
        mine = half == half_ref[0]
        earlier = jnp.maximum(t - 1, 0)
        started = jnp.where(t > 0, 1.0, 0.0)
        for tile in range(TILES):
            pair = tile // 2
            low_row = tile % 2
            parts = [
                jnp.where(
                    mine, fc_ref[2 * band + pair, inside].astype(F32), other_fc_ref[2 * band + pair, inside].astype(F32)
                )[8 * low_row : 8 * low_row + 8]
                for band in range(BANDS)
            ]
            from_fc = jnp.concatenate(block_swap(parts, lanes[1]), axis=0)
            from_dec = jnp.where(
                mine, dec_ref[inside, tile].astype(F32), other_dec_ref[inside, tile].astype(F32)
            )
            gate_in = act_ref[t, tile, 0:C]
            gate_keep = act_ref[t, tile, C : 2 * C]
            gate_out = act_ref[t, tile, 2 * C : 3 * C]
            gate_new = act_ref[t, tile, 3 * C : 4 * C]
            bent = jnp.tanh(cell_ref[t, tile])
            factors = [
                from_fc + from_dec,
                gate_out * (1.0 - bent * bent),
                gate_keep,
                gate_new * gate_in * (1.0 - gate_in),
                (cell_ref[earlier, tile] * started) * gate_keep * (1.0 - gate_keep),
                bent * gate_out * (1.0 - gate_out),
                gate_in * (1.0 - gate_new * gate_new),
            ]
            for index, factor in enumerate(factors):
                factor_s[tile, index * C : (index + 1) * C] = factor

    def retreat(t, factor_s, next_s):
        half = t // own
        inside = t % own
        counted = jnp.where(half == half_ref[0], 1.0, 0.0)
        place = jnp.where(half == half_ref[0], inside, own)
        tiles = []
        for tile in range(TILES):
            back = back_s[tile] + factor_s[tile, 0:C]
            d_cell = state_s[tile] + back * factor_s[tile, C : 2 * C]
            state_s[tile] = d_cell * factor_s[tile, 2 * C : 3 * C]
            d_gates = jnp.concatenate(
                [
                    d_cell * factor_s[tile, 3 * C : 4 * C],
                    d_cell * factor_s[tile, 4 * C : 5 * C],
                    back * factor_s[tile, 5 * C : 6 * C],
                    d_cell * factor_s[tile, 6 * C : 7 * C],
                ],
                axis=0,
            )
            lines_ref[...] += d_gates * counted
            low = d_gates.astype(BF)
            keep_ref[place, tile] = low
            tiles.append(low.astype(F32))
        for index in range(TILES + 4):
            tile = index - 2
            gate_s[index] = moved(tiles[tile % TILES], lanes, 0, tile // TILES).astype(BF)
        prepare(jnp.maximum(t - 1, 0), next_s)
        for two in range(0, TILES, 2):
            sums = nn(wb_s[...], stacked(gate_s, two, KS))
            for one in range(2):
                part = sums[:, one * LANES : (one + 1) * LANES]
                total = None
                for shift in range(KS):
                    value = moved(part[shift * 2 * C : (shift + 1) * 2 * C], lanes, 2 - shift, 0)
                    total = value if total is None else total + value
                denc_ref[place, two + one] = total[:C]
                back_s[two + one] = total[C:]

    prepare(steps - 1, even_s)

    def retreat_two(pair, _):
        retreat(steps - 1 - 2 * pair, even_s, odd_s)
        retreat(steps - 2 - 2 * pair, odd_s, even_s)
        return 0

    lax.fori_loop(0, steps // 2, retreat_two, 0)


ROW_DEC = KK * 2 * C
ROW_COND = ROW_DEC + C
ROW_ENC = ROW_COND + 32
ROW_MASK = ROW_ENC + C
ROW_VECTOR = ROW_MASK + 16
ROWS = ROW_VECTOR + 16
PART = 64
SMALL = ROWS - ROW_DEC


def vector_places():
    place = np.zeros((7 * C + 4 * C + 64, 5 * LANES), np.float32)
    for line in range(7 * C):
        place[line, line] = 1.0
    for line in range(4 * C):
        place[7 * C + line, 7 * C + NK * KK + line % C] = 1.0
    for line in range(64):
        if line % 16 < NM:
            place[11 * C + line, 8 * C + NK * KK + line % 16] = 1.0
    return place


def pack_kernel(
    half_ref, x_ref, enc_ref, hid_ref, keep_ref, denc_ref, lines_ref, head_ref, ddec_ref, dmask_ref, dcond_ref,
    dline_ref, count_ref, squares_ref, we_ref, bias_ref, place_ref, encoder_ref,
    block_ref,
    win_s, join_s, dwe_s, sums_s, packed_s,
):
    own = keep_ref.shape[0] - 1
    base = half_ref[0] * own
    lanes = lane_places()
    dwe_s[...] = jnp.zeros_like(dwe_s)
    sums_s[...] = jnp.zeros_like(sums_s)
    packed_s[...] = jnp.zeros_like(packed_s)

    def gather(i, _):
        t = base + i
        earlier = jnp.maximum(t - 1, 0)
        started = jnp.where(t > 0, 1.0, 0.0)
        spread([enc_ref[t, tile].astype(F32) for tile in range(TILES)], lanes, 2, join_s, 2 * C, 0)
        spread(
            [hid_ref[earlier, tile].astype(F32) * started for tile in range(TILES)], lanes, 2, join_s, 2 * C, C
        )
        d_gates = jnp.concatenate([keep_ref[i, tile] for tile in range(TILES)], axis=1)
        joined = jnp.concatenate([stacked(join_s, 0, KS), stacked(join_s, 2, KS)], axis=1)
        packed_s[0:ROW_DEC] += nt(joined, d_gates)
        spread(image_tiles(x_ref, t), lanes, 1, win_s, 16, 0)
        for two in range(0, TILES, 2):
            window = stacked(win_s, two, 3)
            pre = nn(we_ref[...], window) + twice(bias_ref[0:C])
            centered = pre - jnp.mean(pre, 0, keepdims=True)
            scale = lax.rsqrt(jnp.mean(centered * centered, 0, keepdims=True) + NORM_EPS)
            normal = centered * scale
            gain = twice(bias_ref[C : 2 * C])
            value = normal * gain + twice(bias_ref[2 * C : 3 * C])
            gate = logistic(value)
            d_out = jnp.concatenate([denc_ref[i, two], denc_ref[i, two + 1]], axis=1)
            d_value = d_out * (gate * (1.0 + value * (1.0 - gate)))
            d_gain = d_value * normal
            d_normal = d_value * gain
            d_pre = scale * (
                d_normal
                - jnp.mean(d_normal, 0, keepdims=True)
                - normal * jnp.mean(d_normal * normal, 0, keepdims=True)
            )
            sums_s[0:C] += d_pre[:, :LANES] + d_pre[:, LANES:]
            sums_s[C : 2 * C] += d_gain[:, :LANES] + d_gain[:, LANES:]
            sums_s[2 * C : 3 * C] += d_value[:, :LANES] + d_value[:, LANES:]
            dwe_s[...] += nt(d_pre.astype(BF), window)
        return 0

    lax.fori_loop(0, own, gather, 0)
    packed_s[ROW_DEC:ROW_COND] = ddec_ref[...]
    packed_s[ROW_COND:ROW_ENC] = dcond_ref[...]
    packed_s[ROW_ENC:ROW_MASK] = nn_exact(dwe_s[...], encoder_ref[...])
    packed_s[ROW_MASK:ROW_VECTOR] = dmask_ref[...]
    ones = jnp.ones((8, LANES), F32)
    sums_s[3 * C : 7 * C] = lines_ref[...]
    sums_s[7 * C : 11 * C + 64] = head_ref[0:192]
    line = nn_exact(nt_exact(ones, sums_s[...]), place_ref[...])[0:1] + jnp.sum(dline_ref[...], 0, keepdims=True)
    packed_s[ROW_VECTOR : ROW_VECTOR + 8] = jnp.concatenate(
        [line[:, place * LANES : (place + 1) * LANES] for place in range(5)] + [jnp.zeros((3, LANES), F32)], axis=0
    )
    lost = jnp.sum(jnp.sum(head_ref[192:196], 0, keepdims=True), 1, keepdims=True)
    lane = lax.broadcasted_iota(jnp.int32, (1, LANES), 1)
    value = jnp.where(lane == 0, lost, jnp.where(lane == 1, count_ref[...], jnp.where(lane == 2, squares_ref[...], 0.0)))
    terms = []
    for _ in range(3):
        low = value.astype(BF).astype(F32)
        terms.append(low)
        value = value - low
    devices = block_ref.shape[0]
    large = ROW_DEC // devices
    small = SMALL // devices
    fill = jnp.zeros((PART - large - 2 * small - 3, LANES), F32)
    for device in range(devices):
        value = packed_s[ROW_DEC + device * small : ROW_DEC + (device + 1) * small]
        high = value.astype(BF).astype(F32)
        rows = [packed_s[device * large : (device + 1) * large], high, value - high] + terms + [fill]
        block_ref[device] = jnp.concatenate(rows, axis=0).astype(BF)


def total_kernel(got_ref, out_ref, scalar_ref):
    devices, rows, _ = got_ref.shape
    total = got_ref[0].astype(F32)
    for device in range(1, devices):
        total = total + got_ref[device].astype(F32)
    large = ROW_DEC // devices
    small = SMALL // devices
    end = large + 2 * small
    scalar_ref[...] = total[end : end + 1] + total[end + 1 : end + 2] + total[end + 2 : end + 3]
    value = total[large : large + small] + total[large + small : end]
    high = value.astype(BF).astype(F32)
    low = jnp.concatenate([total[:large], high, value - high, total[end:]], axis=0).astype(BF)
    for device in range(devices):
        out_ref[device] = low


def logit_map_kernel(hid_ref, sum_ref, out_ref, squares_ref, turned_s):
    logits = NK * KK
    eye = one_hot_eye(logits)
    groups, items, _ = sum_ref.shape
    for group in range(groups):
        turned_s[:, group * items : (group + 1) * items] = nt(eye, sum_ref[group]).astype(BF)
    squares = jnp.zeros((1, LANES), F32)
    stride = 2 * WB * C // LANES
    for row in range(2):
        for start in range(0, WB * C, 2 * LANES):
            hid = jnp.concatenate(
                [hid_ref[group, row, :, start : start + 2 * LANES] for group in range(groups)], axis=0
            )
            grad = nn(turned_s[...], hid)
            for one in range(2):
                part = grad[:, one * LANES : (one + 1) * LANES]
                squares = squares + jnp.sum(part * part, 0, keepdims=True)
                out_ref[pl.ds((start // LANES + one) * 2 + row, logits, stride=stride), :] = part
    squares_ref[...] = jnp.broadcast_to(jnp.sum(squares, 1, keepdims=True) * (1.0 / groups), (1, LANES))


def update(weight, grad, factor, first, second, rate):
    first = BETA_ONE * first + (factor * (1.0 - BETA_ONE)) * grad
    second = BETA_TWO * second + (factor * factor * (1.0 - BETA_TWO)) * (grad * grad)
    root = (second * lax.rsqrt(second)) * (1.0 - BETA_TWO**STEP_NO) ** -0.5 + ADAM_EPS
    turned = pl.reciprocal(root, approx=True)
    turned = turned * (2.0 - root * turned)
    step = first * turned * (rate / (1.0 - BETA_ONE**STEP_NO))
    return (weight * (1.0 - rate * DECAY) - step, first, second)


def update_kernel(rates, got_ref, scalar_ref, dfc_ref, *refs):
    weights, firsts, seconds = refs[0:7], refs[7:14], refs[14:21]
    norm_ref = refs[21]
    news = refs[22:29], refs[29:36], refs[36:43]
    packed_s, fc_s, lstm_s, sems = refs[43:]
    devices = got_ref.shape[0]
    large = ROW_DEC // devices
    small = SMALL // devices
    for device in range(devices):
        rows = got_ref[device].astype(F32)
        packed_s[device * large : (device + 1) * large] = rows[:large]
        packed_s[ROW_DEC + device * small : ROW_DEC + (device + 1) * small] = (
            rows[large : large + small] + rows[large + small : large + 2 * small]
        )

    def add_rows(block, total):
        rows = packed_s[pl.ds(pl.multiple_of(block * 32, 32), 32)]
        return total + jnp.sum((rows * rows).reshape(4, 8, LANES), 0)

    squares = lax.fori_loop(0, ROWS // 32, add_rows, jnp.zeros((8, LANES), F32))
    terms = scalar_ref[...]
    squares = jnp.sum(jnp.sum(squares, 0, keepdims=True), 1, keepdims=True) + terms[:, 2:3]
    inv_count = 1.0 / terms[:, 1:2]
    norm = jnp.sqrt(squares) * inv_count
    factor = inv_count * (CLIP_NORM / jnp.maximum(norm, CLIP_NORM))
    norm_ref[...] = jnp.sum(norm)

    copies = []

    def in_blocks(index, grad_ref, scratch, chunks):
        rows = grad_ref.shape[0] if index == 2 else ROW_DEC
        chunk = rows // chunks
        wide = chunk // 2
        for at in range(chunks):

            def block(i, _):
                here = pl.ds(pl.multiple_of(at * chunk + i * wide, 8), wide)
                new = update(
                    weights[index][here], grad_ref[here], factor, firsts[index][here], seconds[index][here],
                    rates[index],
                )
                for kind in range(3):
                    scratch[kind, here] = new[kind]
                return 0

            lax.fori_loop(0, chunk // wide, block, 0)
            for kind in range(3):
                here = pl.ds(at * chunk, chunk)
                copy = pltpu.make_async_copy(
                    scratch.at[kind, here], news[kind][index].at[here], sems.at[len(copies)]
                )
                copy.start()
                copies.append(copy)

    in_blocks(2, dfc_ref, fc_s, 5)
    in_blocks(1, packed_s, lstm_s, 2)

    def step(index, grad):
        new = update(weights[index][...], grad, factor, firsts[index][...], seconds[index][...], rates[index])
        for kind in range(3):
            news[kind][index][...] = new[kind]

    step(0, packed_s[ROW_ENC:ROW_MASK, : KK * 3])
    cond = jnp.concatenate([packed_s[ROW_COND : ROW_COND + 16], packed_s[ROW_COND + 16 : ROW_COND + 32]], axis=1)
    step(3, cond[:COND, : NK * KK])
    step(4, packed_s[ROW_DEC:ROW_COND])
    step(5, packed_s[ROW_MASK : ROW_MASK + NM, 0:C])
    line = jnp.concatenate([packed_s[ROW_VECTOR + place : ROW_VECTOR + place + 1] for place in range(5)], axis=1)
    width = weights[6].shape[0]
    new = update(
        weights[6][...].reshape(1, width), line[:, :width], factor, firsts[6][...].reshape(1, width),
        seconds[6][...].reshape(1, width), rates[6],
    )
    for kind in range(3):
        news[kind][6][...] = new[kind].reshape(width)
    for copy in copies:
        copy.wait()


SMEM_SPEC = pl.BlockSpec(memory_space=pltpu.SMEM)
VMEM_SPEC = pl.BlockSpec(memory_space=pltpu.VMEM)


def cost(micros):
    return pl.CostEstimate(flops=int(micros * 8e8), bytes_accessed=1024, transcendentals=0)


def call(kernel, micros, outs, scratch, half, *operands):
    return pl.pallas_call(
        kernel,
        cost_estimate=cost(micros),
        out_shape=[jax.ShapeDtypeStruct(shape, kind) for shape, kind in outs],
        in_specs=[SMEM_SPEC] + [VMEM_SPEC] * len(operands),
        out_specs=[VMEM_SPEC] * len(outs),
        scratch_shapes=[pltpu.VMEM(shape, kind) for shape, kind in scratch],
        compiler_params=pltpu.CompilerParams(vmem_limit_bytes=VMEM_BYTES),
    )(half, *operands)


def columns(values):
    return jnp.broadcast_to(values[:, None], (values.shape[0], LANES))


def exchange(block, axes):
    return lax.all_to_all(block, axes, 0, 0, tiled=True)


def to_all(block, axes):
    count = lax.axis_size(axes)
    return exchange(jnp.broadcast_to(block[None], (count,) + block.shape), axes)


def strip_order():
    sent = np.arange(WB * C)
    natural = sent % WB * C + sent // WB % 4 * 8 + sent // LANES
    order = np.zeros((WB * C, WB * C), np.float32)
    order[sent, natural] = 1.0
    return order


def whole_clips(
    frames, valid, flags, actions, states, latent,
    w_enc, w_lstm, w_fc, w_cond, w_deconv, w_mask, vector,
    m_enc, m_lstm, m_fc, m_cond, m_deconv, m_mask, m_vector,
    v_enc, v_lstm, v_fc, v_cond, v_deconv, v_mask, v_vector,
):
    clips, shots, _, strip_rows, width = frames.shape
    steps = shots - 1
    own = steps // HALVES
    count = lax.axis_size("row")
    place = lax.axis_index("row")
    clip = place // HALVES
    half = place % HALVES
    half_1 = half.reshape(1).astype(jnp.int32)
    b_enc, g_enc, s_enc, b_lstm, b_fc, b_dec, b_mask = split_vector(vector)
    places, encoder = window_places()
    flagged = jnp.pad(valid.astype(BF), ((0, 0), (1, 0), (0, 0), (0, 0)))
    pieces = jnp.concatenate([frames, flagged[:, :, None]], axis=2).reshape(clips, shots, 4, 2, 2, width)
    pieces = jnp.transpose(pieces, (0, 1, 4, 2, 3, 5)).reshape(clips, shots * 8, LANES)
    pieces = jnp.pad(pieces, ((0, 0), (0, 8), (0, 0)))
    raw = exchange(jnp.repeat(pieces, HALVES, axis=0), "row")

    wide_enc = jnp.einsum(
        "rk,ko->or", jnp.asarray(encoder, BF), w_enc.astype(BF), preferred_element_type=F32
    ).astype(BF)
    bias = columns(
        jnp.concatenate([vector[: 7 * C], b_dec, jnp.pad(b_mask, (0, 16 - NM), constant_values=-1e30)])
    )
    cells = (steps, TILES, C, LANES)
    x, enc, hid, act, cell, strips_out = call(
        forward_kernel,
        20,
        [
            ((shots, TILES, 16, LANES), BF), ((shots,) + cells[1:], BF), (cells, BF),
            ((steps, TILES, 4 * C, LANES), F32),
            (cells, F32), ((count, own, 16, LANES), BF),
        ],
        [
            ((6, 48, LANES), BF), ((8, KS * C, LANES), BF), ((8, KS * C, LANES), BF), ((TILES, C, LANES), F32),
            ((KK * C, LANES), BF), ((4 * C, KK * C), BF), ((4 * C, KK * C), BF),
            ((TILES, 4 * C, LANES), F32), ((TILES, 4 * C, LANES), F32),
        ],
        half_1, raw, wide_enc, w_lstm, bias,
    )
    items = clips * steps
    order = jnp.asarray(strip_order(), BF)
    k_fc = jnp.einsum("jnl,kl->jnk", w_fc.astype(BF), order, preferred_element_type=F32).astype(BF)
    strip_hid = exchange(strips_out, "row").reshape(items, 2, WB * C)
    parts = jnp.einsum("mjk,jnk->mn", strip_hid, k_fc, preferred_element_type=F32)
    strip_hid = jnp.einsum("mjk,kl->jml", strip_hid, order, preferred_element_type=F32).astype(BF)
    strip_hid_all = to_all(strip_hid, "clip")
    summed = jnp.sum(exchange(parts.reshape(count, own, NK * KK), "row"), 0)
    presence = flags.astype(F32)
    conditions = jnp.concatenate(
        [
            actions * presence[..., :1],
            states * presence[..., 1:],
            jnp.broadcast_to(latent[:, None, :], (clips, steps, latent.shape[1])),
        ],
        -1,
    )
    cond = lax.dynamic_slice(conditions, (clip, half * own, 0), (1, own, COND))[0]
    logits = summed + (jnp.dot(cond, w_cond, precision=HIGH) + b_fc)
    logits = jnp.pad(
        logits.reshape(own, NK, KK), ((0, 0), (1, 5), (0, 32 - KK)), constant_values=-1e30
    )
    dec, d_logit, d_dec, d_mask, head_sums = call(
        head_kernel,
        30,
        [
            ((own, TILES, C, LANES), BF), ((own, 16, 32), F32), ((C, 4 * C), F32), ((16, LANES), F32),
            ((200, LANES), F32),
        ],
        [
            ((6, 48, LANES), F32), ((6, 48, LANES), F32), ((C, 4 * C), BF), ((4 * C, C), BF), ((64, 12 * C), BF),
            ((4 * C, 192), BF), ((4 * C + 64, LANES), F32), ((64, 4 * C), F32),
            ((4 * WIN, 32), BF), ((32, 4 * WIN), BF), ((4 * WIN, TILES * LANES), BF),
            ((4 * WIN, TILES * LANES), BF), ((own, 64, 4 * WIN), F32),
            ((own, 16, 32), F32),
        ],
        half_1, x, hid, logits, w_deconv, w_mask.T, bias,
        jnp.asarray(places, BF), jnp.asarray(places.transpose(0, 2, 1), BF),
    )
    d_logit = d_logit[:, 1 : NK + 1, :KK].reshape(own, NK * KK)
    every_sum = to_all(d_logit.astype(BF), ("clip", "row")).reshape(-1, items, NK * KK)
    d_sum = lax.dynamic_index_in_dim(every_sum, lax.axis_index("clip"), 0, False)
    back_fc = jnp.einsum("mn,jnk->mjk", d_sum, k_fc, preferred_element_type=F32).astype(BF)
    back_fc = exchange(back_fc.reshape(count, own, 16, LANES), "row")
    swap = [(index, index ^ 1) for index in range(count)]

    keep, d_enc, lines = call(
        backward_kernel,
        0.1,
        [((own + 1, TILES, 4 * C, LANES), BF), ((own + 1, TILES, C, LANES), F32), ((4 * C, LANES), F32)],
        [
            ((8, 4 * C, LANES), BF), ((TILES, C, LANES), F32), ((TILES, C, LANES), F32),
            ((KS * 2 * C, KS * 4 * C), BF), ((TILES, 7 * C, LANES), F32), ((TILES, 7 * C, LANES), F32),
        ],
        half_1, act, cell, dec, lax.ppermute(dec, "row", swap), back_fc, lax.ppermute(back_fc, "row", swap), w_lstm,
    )
    groups = lax.axis_size("clip")

    strip_hid_all, every_sum, _ = lax.optimization_barrier((strip_hid_all, every_sum, lines))
    d_fc, fc_squares = pl.pallas_call(
        logit_map_kernel,
        cost_estimate=cost(2),
        out_shape=[
            jax.ShapeDtypeStruct((w_fc.size // LANES, LANES), F32), jax.ShapeDtypeStruct((1, LANES), F32)
        ],
        in_specs=[VMEM_SPEC] * 2,
        out_specs=[VMEM_SPEC] * 2,
        scratch_shapes=[pltpu.VMEM((NK * KK, groups * items), BF)],
        compiler_params=pltpu.CompilerParams(vmem_limit_bytes=VMEM_BYTES),
    )(strip_hid_all, every_sum)
    d_cond = jnp.dot(cond.T, d_logit, precision=HIGH)
    d_cond = jnp.pad(d_cond, ((0, 16 - COND), (0, 2 * LANES - NK * KK)))
    d_cond = jnp.concatenate([d_cond[:, :LANES], d_cond[:, LANES:]], axis=0)
    d_line = jnp.pad(d_logit, ((0, 0), (7 * C, 5 * LANES - 7 * C - NK * KK)))
    counted = jnp.broadcast_to(jnp.sum(valid.astype(F32)), (1, LANES))
    both = ("clip", "row")
    devices = lax.axis_size(both)
    block = call(
        pack_kernel,
        12,
        [((devices, PART, LANES), BF)],
        [
            ((6, 48, LANES), BF), ((8, KS * 2 * C, LANES), BF), ((C, WIN), F32), ((11 * C + 64, LANES), F32),
            ((ROWS, LANES), F32),
        ],
        half_1, x, enc, hid, keep, d_enc, lines, head_sums, d_dec, d_mask, d_cond, d_line, counted, fc_squares, wide_enc, bias,
        jnp.asarray(vector_places(), F32), jnp.asarray(np.pad(encoder, ((0, 0), (0, LANES - KK * 3))), F32),
    )[0]
    sums, scalars = pl.pallas_call(
        total_kernel,
        out_shape=[jax.ShapeDtypeStruct(block.shape, BF), jax.ShapeDtypeStruct((1, LANES), F32)],
        in_specs=[VMEM_SPEC],
        out_specs=[VMEM_SPEC, VMEM_SPEC],
        compiler_params=pltpu.CompilerParams(vmem_limit_bytes=VMEM_BYTES),
    )(exchange(block, both))
    sums = exchange(sums, both)
    rates = learning_rates(w_fc.shape[0] * count)

    def shown(group):
        enc, lstm, fc, cond, dec, mask, line = group
        fc = fc.reshape(2, NK * KK, WB * C // LANES, LANES)
        fc = jnp.transpose(fc, (1, 2, 0, 3)).reshape(-1, LANES)
        return [enc.T, lstm, fc, cond, dec, mask.T, line]

    def back(group):
        enc, lstm, fc, cond, dec, mask, line = group
        fc = fc.reshape(NK * KK, WB * C // LANES, 2, LANES)
        fc = jnp.transpose(fc, (2, 0, 1, 3)).reshape(w_fc.shape)
        return [enc.T, lstm, fc, cond, dec, mask.T, line]

    weights = shown([w_enc, w_lstm, w_fc, w_cond, w_deconv, w_mask, vector])
    firsts = shown([m_enc, m_lstm, m_fc, m_cond, m_deconv, m_mask, m_vector])
    seconds = shown([v_enc, v_lstm, v_fc, v_cond, v_deconv, v_mask, v_vector])
    shapes = [jax.ShapeDtypeStruct(value.shape, F32) for value in weights]
    any_spec = pl.BlockSpec(memory_space=pl.ANY)
    places_out = [VMEM_SPEC, any_spec, any_spec] + [VMEM_SPEC] * 4
    new = pl.pallas_call(
        functools.partial(update_kernel, rates),
        out_shape=[jax.ShapeDtypeStruct((), F32)] + shapes * 3,
        in_specs=[VMEM_SPEC] * 24,
        out_specs=[SMEM_SPEC] + places_out * 3,
        scratch_shapes=[
            pltpu.VMEM((ROWS, LANES), F32), pltpu.VMEM((3,) + shapes[2].shape, F32),
            pltpu.VMEM((3,) + shapes[1].shape, F32), pltpu.SemaphoreType.DMA((21,)),
        ],
        compiler_params=pltpu.CompilerParams(vmem_limit_bytes=VMEM_BYTES),
    )(sums, scalars, d_fc, *weights, *firsts, *seconds)
    outs = [scalars[0, 0], scalars[0, 1], new[0]]
    for kind in range(3):
        outs.extend(back(new[1 + 7 * kind : 8 + 7 * kind]))
    return tuple(outs)


def shards(frames, *rest):
    clips, _, _, strip_rows, width = frames.shape
    count = lax.axis_size("row")
    one_clip = strip_rows * count // 2 == TILES * BANDS and width // 2 == WB
    if one_clip and clips * HALVES == count:
        return whole_clips(frames, *rest)
    return strips(frames, *rest)


def solution(mesh):
    placed = (
        P("clip", None, None, "row", None),
        P("clip", None, "row", None),
        P("clip", None, None),
        P("clip", None, None),
        P("clip", None, None),
        P("clip", None),
        P(),
        P(),
        P("row", None, None),
        P(),
        P(),
        P(),
        P(),
        P(),
        P(),
        P("row", None, None),
        P(),
        P(),
        P(),
        P(),
        P(),
        P(),
        P("row", None, None),
        P(),
        P(),
        P(),
        P(),
    )
    return jax.shard_map(
        shards,
        mesh=mesh,
        in_specs=placed,
        out_specs=(
            P(),
            P(),
            P(),
            P(),
            P(),
            P("row", None, None),
            P(),
            P(),
            P(),
            P(),
            P(),
            P(),
            P("row", None, None),
            P(),
            P(),
            P(),
            P(),
            P(),
            P(),
            P("row", None, None),
            P(),
            P(),
            P(),
            P(),
        ),
        check_vma=False,
    )
```

```python
import functools

import jax
import jax.numpy as jnp
import numpy as np
from jax import lax
from jax.experimental import pallas as pl
from jax.experimental.pallas import tpu as pltpu
from jax.sharding import PartitionSpec as P

C = 32
KS = 5
NK = 10
STEP_NO = 10
KK = 25
NM = 11
COND = 15
WB = 32


NORM_EPS = 1e-05
CLIP_NORM = 0.001
BETA_ONE = 0.9
BETA_TWO = 0.999
ADAM_EPS = 1e-12
DECAY = 0.01
HIGH = lax.Precision.HIGHEST


def padded_2(cells, sides, width):
    for axis, dim in sides:
        count = lax.axis_size(axis)
        ends = count - 1
        head = lax.slice_in_dim(cells, 0, width, axis=dim)
        tail = lax.slice_in_dim(cells, cells.shape[dim] - width, cells.shape[dim], axis=dim)
        cells = jnp.concatenate(
            [
                lax.ppermute(tail, axis, [(i, (i + 1) % count) for i in range(ends)]),
                cells,
                lax.ppermute(head, axis, [((i + 1) % count, i) for i in range(ends)]),
            ],
            axis=dim,
        )
    return cells


def passed_along(block, axis, distance):
    devices = range(lax.axis_size(axis))
    route = [(i - distance, i) for i in devices if i - distance in devices]
    return lax.ppermute(block, axis, route)


def split_vector(vector):
    counts = [C, C, C, 4 * C, NK * KK, C, NM]
    pieces = []
    start = 0
    for count in counts:
        pieces.append(vector[start : start + count])
        start += count
    return pieces


def norm_act(pre, gain, shift):
    centered = pre - jnp.mean(pre, -1, keepdims=True)
    scale = lax.rsqrt(jnp.mean(centered * centered, -1, keepdims=True) + NORM_EPS)
    return jax.nn.silu(centered * scale * gain + shift)


def cell_step(gates, cell):
    gate_in, gate_keep, gate_out, gate_new = jnp.split(gates, 4, axis=-1)
    new_cell = jax.nn.sigmoid(gate_keep + 1.0) * cell + jax.nn.sigmoid(gate_in) * jnp.tanh(gate_new)
    return (jax.nn.sigmoid(gate_out) * jnp.tanh(new_cell), new_cell)


def upsample(values):
    clips, rows_in, cols_in, depth = values.shape
    grid = values.reshape(clips, rows_in, cols_in, 2, 2, depth // 4)
    return jnp.transpose(grid, (0, 1, 3, 2, 4, 5)).reshape(
        clips, 2 * rows_in, 2 * cols_in, depth // 4
    )


def predict(logits, upper, w_mask, b_mask, prev_pad):
    clips = logits.shape[0]
    kernels = jax.nn.softmax(logits.reshape(clips, NK, KK), axis=-1)
    activated = jax.nn.silu(upper)
    blend = jax.nn.softmax(
        jnp.einsum("byxc,cm->byxm", activated, w_mask, precision=HIGH) + b_mask, axis=-1
    )
    mixing = jnp.einsum("byxk,bko->byxo", blend[..., 1:], kernels, precision=HIGH)
    height = prev_pad.shape[1] - 4
    breadth = prev_pad.shape[2] - 4
    result = blend[..., :1] * prev_pad[:, 2 : 2 + height, 2 : 2 + breadth, :]
    for offset in range(KK):
        top = offset // KS
        left = offset % KS
        result = (
            result
            + mixing[..., offset : offset + 1]
            * prev_pad[:, top : top + height, left : left + breadth, :]
        )
    return result


def patches(padded, stride, out_rows, out_cols):
    pieces = []
    for offset in range(KK):
        top = offset // KS
        left = offset % KS
        pieces.append(
            padded[
                :,
                top : top + stride * (out_rows - 1) + 1 : stride,
                left : left + stride * (out_cols - 1) + 1 : stride,
                :,
            ]
        )
    return jnp.concatenate(pieces, -1)


def unpatch(grads, shape, stride):

    def extract(padded):
        return patches(padded, stride, grads.shape[1], grads.shape[2])

    _, pullback = jax.vjp(extract, jnp.zeros(shape, jnp.float32))
    return pullback(grads)[0]


def product(left, right, form):
    return jnp.einsum(form, left, right, preferred_element_type=jnp.float32)


def learning_rates(rows_total):
    return [
        0.5 * (KK * 3) ** (-0.5),
        0.5 * (KK * 2 * C) ** (-0.5),
        0.5 * (rows_total * WB * C // 16) ** (-0.5),
        0.5 * COND ** (-0.5),
        0.5 * C ** (-0.5),
        0.5 * (C // 4) ** (-0.5),
        0.1,
    ]


def adam(weight, grad, first, second, rate):
    first = BETA_ONE * first + (1.0 - BETA_ONE) * grad
    second = BETA_TWO * second + (1.0 - BETA_TWO) * grad * grad
    update = (
        first
        / (1.0 - BETA_ONE**STEP_NO)
        / (jnp.sqrt(second / (1.0 - BETA_TWO**STEP_NO)) + ADAM_EPS)
    )
    return (weight - rate * (update + DECAY * weight), first, second)


def strips(
    frames,
    valid,
    flags,
    actions,
    states,
    latent,
    w_enc,
    w_lstm,
    w_fc,
    w_cond,
    w_deconv,
    w_mask,
    vector,
    m_enc,
    m_lstm,
    m_fc,
    m_cond,
    m_deconv,
    m_mask,
    m_vector,
    v_enc,
    v_lstm,
    v_fc,
    v_cond,
    v_deconv,
    v_mask,
    v_vector,
):
    clips = frames.shape[0]
    out_rows = frames.shape[3] // 2
    out_cols = frames.shape[4] // 2
    b_enc, g_enc, s_enc, b_lstm, b_fc, b_dec, b_mask = split_vector(vector)
    k_enc = w_enc.astype(jnp.bfloat16)
    k_lstm = w_lstm.astype(jnp.bfloat16)
    k_fc = w_fc.astype(jnp.bfloat16)
    k_dec = w_deconv.astype(jnp.bfloat16)
    images = jnp.transpose(frames, (1, 0, 3, 4, 2))
    padded = padded_2(images, (("row", 2),), 2)
    padded = jnp.pad(padded, ((0, 0), (0, 0), (0, 0), (2, 2), (0, 0)))
    valid_steps = jnp.transpose(valid.astype(jnp.float32), (1, 0, 2, 3))
    presence = flags.astype(jnp.float32)
    conditions = jnp.concatenate(
        [
            actions * presence[..., :1],
            states * presence[..., 1:],
            jnp.broadcast_to(latent[:, None, :], (clips, actions.shape[1], latent.shape[1])),
        ],
        -1,
    )
    conditions = jnp.transpose(conditions, (1, 0, 2))
    valid_count = lax.psum(jnp.sum(valid_steps), ("clip", "row"))
    inv_count = 1.0 / valid_count

    def advance(carry, image_pad):
        hidden, cell = carry
        pre = product(patches(image_pad, 2, out_rows, out_cols), k_enc, "byxk,kc->byxc") + b_enc
        encoded = norm_act(pre, g_enc, s_enc).astype(jnp.bfloat16)
        joined = jnp.concatenate([encoded, hidden], -1)
        joined_pad = padded_2(joined, (("row", 1),), 2)
        joined_pad = jnp.pad(joined_pad, ((0, 0), (0, 0), (2, 2), (0, 0)))
        gates = (
            product(patches(joined_pad, 1, out_rows, out_cols), k_lstm, "byxk,kg->byxg") + b_lstm
        )
        new_hidden, new_cell = cell_step(gates, cell)
        hidden_low = new_hidden.astype(jnp.bfloat16)
        part = product(hidden_low.reshape(clips, out_rows, -1), k_fc, "bjk,jnk->bn")
        part = lax.psum(part, "row")
        upper = product(hidden_low, k_dec, "byxc,cd->byxd")
        return ((hidden_low, new_cell), (pre, joined_pad, gates, cell, hidden_low, part, upper))

    start = (
        jnp.zeros((clips, out_rows, out_cols, C), jnp.bfloat16),
        jnp.zeros((clips, out_rows, out_cols, C), jnp.float32),
    )
    _, saved = lax.scan(advance, start, padded[:-1])
    pre_all, joined_all, gates_all, cells_all, hidden_all, summed_all, uppers = saved
    targets = images[1:].astype(jnp.float32)

    def local_head(item):
        summed_t, upper_t, image_pad, target, mask, cond = item

        def error_of(summed_t, upper_t, w_cond, w_mask, b_fc, b_dec, b_mask):
            logits = summed_t + jnp.dot(cond, w_cond, precision=HIGH) + b_fc
            upper_full = upsample(upper_t) + b_dec
            result = predict(logits, upper_full, w_mask, b_mask, image_pad.astype(jnp.float32))
            return jnp.sum(mask * jnp.sum((result - target) ** 2, -1))

        error, pullback = jax.vjp(error_of, summed_t, upper_t, w_cond, w_mask, b_fc, b_dec, b_mask)
        return (error, pullback(inv_count))

    head_inputs = (summed_all, uppers, padded[:-1], targets, valid_steps, conditions)

    def retreat(carry, item):
        (
            back_hidden,
            back_cell,
            acc_enc,
            acc_lstm,
            acc_dec,
            acc_benc,
            acc_genc,
            acc_senc,
            acc_blstm,
        ) = carry
        saved_t, head_t = item
        pre, joined_pad, gates, cell_prev, hidden_low, image_pad = saved_t
        error, pulled_t = local_head(head_t)
        d_sum = lax.psum(pulled_t[0], "row")
        d_upper = pulled_t[1]
        extra = (error, pulled_t[2:])
        d_sum_low = d_sum.astype(jnp.bfloat16)
        d_upper_low = d_upper.astype(jnp.bfloat16)
        acc_dec = acc_dec + product(hidden_low, d_upper_low, "byxc,byxd->cd")
        back = back_hidden + product(d_upper_low, k_dec, "byxd,cd->byxc")
        back = back + product(d_sum_low, k_fc, "bn,jnk->bjk").reshape(back_hidden.shape)
        _, cell_pull = jax.vjp(cell_step, gates, cell_prev)
        d_gates, back_cell = cell_pull((back, back_cell))
        d_gates_low = d_gates.astype(jnp.bfloat16)
        acc_blstm = acc_blstm + jnp.sum(d_gates, (0, 1, 2))
        acc_lstm = acc_lstm + product(
            patches(joined_pad, 1, out_rows, out_cols), d_gates_low, "byxk,byxg->kg"
        )
        d_pad = unpatch(product(d_gates_low, k_lstm, "byxg,kg->byxk"), joined_pad.shape, 1)[
            :, :, 2:-2, :
        ]
        from_below = passed_along(d_pad[:, :2], "row", -1)
        from_above = passed_along(d_pad[:, -2:], "row", 1)
        d_joined = d_pad[:, 2:-2].at[:, -2:].add(from_below).at[:, :2].add(from_above)
        _, norm_pull = jax.vjp(norm_act, pre, g_enc, s_enc)
        d_pre, d_gain, d_shift = norm_pull(d_joined[..., :C])
        acc_benc = acc_benc + jnp.sum(d_pre, (0, 1, 2))
        acc_genc = acc_genc + d_gain
        acc_senc = acc_senc + d_shift
        acc_enc = acc_enc + product(
            patches(image_pad, 2, out_rows, out_cols), d_pre.astype(jnp.bfloat16), "byxk,byxc->kc"
        )
        new_carry = (
            d_joined[..., C:],
            back_cell,
            acc_enc,
            acc_lstm,
            acc_dec,
            acc_benc,
            acc_genc,
            acc_senc,
            acc_blstm,
        )
        return (new_carry, (d_sum_low, extra))

    zeros_state = jnp.zeros((clips, out_rows, out_cols, C), jnp.float32)
    zeros_small = jnp.zeros((C,), jnp.float32)
    init = (
        zeros_state,
        zeros_state,
        jnp.zeros(w_enc.shape, jnp.float32),
        jnp.zeros(w_lstm.shape, jnp.float32),
        jnp.zeros(w_deconv.shape, jnp.float32),
        zeros_small,
        zeros_small,
        zeros_small,
        jnp.zeros((4 * C,), jnp.float32),
    )
    final, (d_sums_low, extra) = lax.scan(
        retreat,
        init,
        ((pre_all, joined_all, gates_all, cells_all, hidden_all, padded[:-1]), head_inputs),
        reverse=True,
    )
    error_sum = jnp.sum(extra[0])
    head_sums = [jnp.sum(grad, 0) for grad in extra[1]]
    acc_enc, acc_lstm, acc_dec, acc_benc, acc_genc, acc_senc, acc_blstm = final[2:]
    flat_hidden = hidden_all.reshape(hidden_all.shape[0], clips, out_rows, -1)
    d_fc = lax.psum(
        product(flat_hidden, d_sums_low, "tbjk,tbn->jnk").astype(jnp.bfloat16), "clip"
    ).astype(jnp.float32)
    fc_squares = jnp.sum(d_fc * d_fc) / lax.axis_size("clip")
    d_vector = jnp.concatenate(
        [acc_benc, acc_genc, acc_senc, acc_blstm, head_sums[2], head_sums[3], head_sums[4]]
    )
    d_enc, d_lstm, d_cond, d_dec, d_mask, d_vector, loss_sum, squares = lax.psum(
        (acc_enc, acc_lstm, head_sums[0], acc_dec, head_sums[1], d_vector, error_sum, fc_squares),
        ("clip", "row"),
    )
    grads = (d_enc, d_lstm, d_fc, d_cond, d_dec, d_mask, d_vector)
    for index in (0, 1, 3, 4, 5, 6):
        squares = squares + jnp.sum(grads[index] * grads[index])
    grad_norm = jnp.sqrt(squares)
    factor = CLIP_NORM / jnp.maximum(grad_norm, CLIP_NORM)
    rates = learning_rates(w_fc.shape[0] * lax.axis_size("row"))
    weights = (w_enc, w_lstm, w_fc, w_cond, w_deconv, w_mask, vector)
    firsts = (m_enc, m_lstm, m_fc, m_cond, m_deconv, m_mask, m_vector)
    seconds = (v_enc, v_lstm, v_fc, v_cond, v_deconv, v_mask, v_vector)
    new = [
        adam(weights[index], grads[index] * factor, firsts[index], seconds[index], rates[index])
        for index in range(7)
    ]
    return (
        loss_sum,
        valid_count,
        grad_norm,
        new[0][0],
        new[1][0],
        new[2][0],
        new[3][0],
        new[4][0],
        new[5][0],
        new[6][0],
        new[0][1],
        new[1][1],
        new[2][1],
        new[3][1],
        new[4][1],
        new[5][1],
        new[6][1],
        new[0][2],
        new[1][2],
        new[2][2],
        new[3][2],
        new[4][2],
        new[5][2],
        new[6][2],
    )


LANES = 128
TILES = 4
BANDS = 4
HALVES = 2
FAR = 1
WIN = 9 * 16
BF = jnp.bfloat16
F32 = jnp.float32
VMEM_BYTES = 56 * 1024 * 1024


def window_places():
    places = np.zeros((4, WIN, 32), np.float32)
    encoder = np.zeros((WIN, KK * 3), np.float32)
    for sub in range(4):
        for tap in range(KK):
            off_y = tap // KS - 2 + sub // 2
            off_x = tap % KS - 2 + sub % 2
            block = (off_y // 2 + 1) * 3 + off_x // 2 + 1
            base = block * 16 + (off_x % 2) * 8 + (off_y % 2) * 4
            for channel in range(3):
                places[sub, base + channel, tap] = 1.0
                if sub == 0:
                    encoder[base + channel, tap * 3 + channel] = 1.0
    return places, encoder


def lane_places():
    lane = lax.broadcasted_iota(jnp.int32, (8, LANES), 1)
    return lane % WB, lane // WB


def moved(tile, lanes, d_col, d_band):
    if d_col == 0 and d_band == 0:
        return tile
    col, band = lanes
    rows = tile.shape[0]
    shift = (-(WB * d_band + d_col)) % LANES
    rolled = pltpu.roll(tile.reshape(rows // 8, 8, LANES), shift, 2)
    keep = None
    for place, delta, count in ((col, d_col, WB), (band, d_band, BANDS)):
        if delta > 0:
            inside = place < count - delta
        elif delta < 0:
            inside = place >= -delta
        else:
            continue
        keep = inside if keep is None else keep & inside
    return jnp.where(keep[None], rolled, 0.0).reshape(rows, LANES)


def spread(tiles, lanes, reach, target, width, start):
    rows = tiles[0].shape[0]
    for index in range(TILES + 2 * reach):
        tile = index - reach
        for shift in range(2 * reach + 1):
            place = shift * width + start
            target[index, place : place + rows, :] = moved(
                tiles[tile % TILES], lanes, shift - reach, tile // TILES
            ).astype(target.dtype)


def stacked(ref, tile, count):
    rows = count * ref.shape[1]
    return jnp.concatenate(
        [ref[tile : tile + count].reshape(rows, LANES), ref[tile + 1 : tile + 1 + count].reshape(rows, LANES)],
        axis=1,
    )


def nn(left, right):
    return lax.dot_general(left, right, (((1,), (0,)), ((), ())), preferred_element_type=F32)


def nt(left, right):
    return lax.dot_general(left, right, (((1,), (1,)), ((), ())), preferred_element_type=F32)


def nn_exact(left, right):
    return lax.dot_general(left, right, (((1,), (0,)), ((), ())), preferred_element_type=F32, precision=HIGH)


def nt_exact(left, right):
    return lax.dot_general(left, right, (((1,), (1,)), ((), ())), preferred_element_type=F32, precision=HIGH)


def logistic(v):
    return 0.5 * jnp.tanh(0.5 * v) + 0.5


def one_hot_eye(size):
    row = lax.broadcasted_iota(jnp.int32, (size, size), 0)
    return (row == lax.broadcasted_iota(jnp.int32, (size, size), 1)).astype(BF)


def split(value):
    high = value.astype(BF)
    return high, (value - high.astype(F32)).astype(BF)


def one_hot_mod(shape, period, axis):
    folded = lax.broadcasted_iota(jnp.int32, shape, axis) % period
    return (folded == lax.broadcasted_iota(jnp.int32, shape, 1 - axis)).astype(BF)


def unpack_images(raw_ref, x_ref):
    source = lax.broadcasted_iota(jnp.int32, (LANES, 4 * LANES), 0)
    goal = lax.broadcasted_iota(jnp.int32, (LANES, 4 * LANES), 1)
    same = (source // 64 == goal // 256) & (source % 2 == goal // LANES % 2) & (source // 2 % WB == goal % WB)
    picks = [(same & (goal // WB % BANDS == band)).astype(BF) for band in range(BANDS)]
    for pair in range(2):
        total = nn(raw_ref[pair], picks[0])
        for band in range(1, BANDS):
            total = total + nn(raw_ref[2 * band + pair], picks[band])
        for t in range(x_ref.shape[0]):
            rows = total[8 * t : 8 * t + 8]
            for low_row in range(2):
                start = 2 * LANES * low_row
                x_ref[t, 2 * pair + low_row] = jnp.concatenate(
                    [rows[:, start : start + LANES], rows[:, start + LANES : start + 2 * LANES]], axis=0
                ).astype(BF)


def image_tiles(x_ref, t):
    return [x_ref[t, tile].astype(F32) for tile in range(TILES)]


def block_swap(parts, band):
    swapped = []
    for out in range(BANDS):
        total = None
        for part in range(BANDS):
            shift = (WB * (part - out)) % LANES
            value = parts[part] if shift == 0 else pltpu.roll(parts[part], shift, 1)
            total = value if total is None else jnp.where(band == part, value, total)
        swapped.append(total)
    return swapped


def wide(tile):
    return jnp.concatenate([tile] * TILES, axis=1)


def folded(values):
    total = values[:, :LANES]
    for tile in range(1, values.shape[1] // LANES):
        total = total + values[:, tile * LANES : (tile + 1) * LANES]
    return total


def twice(tile):
    return jnp.concatenate([tile, tile], axis=1)


def forward_kernel(
    half_ref, raw_ref, we_ref, w_ref, bias_ref,
    x_ref, enc_ref, hid_ref, far_act_ref, far_cell_ref, strip_ref,
    win_s, enc_s, hid_s, state_s, rows_s, wx_s, wh_s, even_s, odd_s, act_ref, cell_ref, sems,
):
    steps = hid_ref.shape[0]
    lanes = lane_places()
    for kind, target in ((0, wx_s), (1, wh_s)):
        for tap in range(KK):
            start = tap * 2 * C + kind * C
            rows_s[tap * C : (tap + 1) * C, :] = w_ref[start : start + C, :].astype(BF)
        target[...] = nt(one_hot_eye(4 * C), rows_s[...]).astype(BF)
    unpack_images(raw_ref, x_ref)

    def encode(t, gates_s):
        spread(image_tiles(x_ref, t), lanes, 1, win_s, 16, 0)
        tiles = []
        for two in range(0, TILES, 2):
            pre = nn(we_ref[...], stacked(win_s, two, 3)) + twice(bias_ref[0:C])
            centered = pre - jnp.mean(pre, 0, keepdims=True)
            scale = lax.rsqrt(jnp.mean(centered * centered, 0, keepdims=True) + NORM_EPS)
            value = centered * scale * twice(bias_ref[C : 2 * C]) + twice(bias_ref[2 * C : 3 * C])
            value = (value * logistic(value)).astype(BF)
            for one in range(2):
                part = value[:, one * LANES : (one + 1) * LANES]
                enc_ref[t, two + one] = part
                tiles.append(part.astype(F32))
        spread(tiles, lanes, 2, enc_s, C, 0)
        for two in range(0, TILES, 2):
            gates = nn(wx_s[...], stacked(enc_s, two, KS)) + twice(bias_ref[3 * C : 7 * C])
            for one in range(2):
                gates_s[two + one] = gates[:, one * LANES : (one + 1) * LANES]

    hid_s[...] = jnp.zeros_like(hid_s)
    state_s[...] = jnp.zeros_like(state_s)

    def advance(t, gates_s, later_s):
        sums = [nn(wh_s[...], stacked(hid_s, two, KS)) for two in range(0, TILES, 2)]
        encode(t + 1, later_s)
        hidden = []
        for tile in range(TILES):
            start = tile % 2 * LANES
            gates = gates_s[tile] + sums[tile // 2][:, start : start + LANES]
            gate_in = logistic(gates[0:C])
            gate_keep = logistic(gates[C : 2 * C] + 1.0)
            gate_out = logistic(gates[2 * C : 3 * C])
            gate_new = jnp.tanh(gates[3 * C : 4 * C])
            cell = gate_keep * state_s[tile] + gate_in * gate_new
            act_ref[t, tile, 0:C] = gate_in
            act_ref[t, tile, C : 2 * C] = gate_keep
            act_ref[t, tile, 2 * C : 3 * C] = gate_out
            act_ref[t, tile, 3 * C : 4 * C] = gate_new
            state_s[tile] = cell
            cell_ref[t, tile] = cell
            low = (gate_out * jnp.tanh(cell)).astype(BF)
            hid_ref[t, tile] = low
            hidden.append(low.astype(F32))
        spread(hidden, lanes, 2, hid_s, C, 0)

    def out_copies(t):
        return [
            pltpu.make_async_copy(act_ref.at[t], far_act_ref.at[t], sems.at[0, t]),
            pltpu.make_async_copy(cell_ref.at[t], far_cell_ref.at[t], sems.at[1, t]),
        ]

    encode(0, even_s)

    def advance_two(pair, _):
        for one, slots in enumerate(((even_s, odd_s), (odd_s, even_s))):
            advance(2 * pair + one, *slots)
        for one in range(2):
            for copy in out_copies(2 * pair + one):
                copy.start()
        return 0

    lax.fori_loop(0, steps // 2, advance_two, 0)
    own = steps // HALVES
    base = half_ref[0] * own

    def to_strips(i, _):
        for pair in range(2):
            rows = []
            for low_row in range(2):
                tile = hid_ref[base + i, 2 * pair + low_row].astype(F32)
                rows.append(block_swap([tile[8 * q : 8 * q + 8] for q in range(4)], lanes[1]))
            for band in range(BANDS):
                strip_ref[2 * band + pair, i] = jnp.concatenate(
                    [rows[0][band], rows[1][band]], axis=0
                ).astype(BF)
        return 0

    lax.fori_loop(0, own, to_strips, 0)
    for t in range(steps):
        for copy in out_copies(t):
            copy.wait()


def head_kernel(
    half_ref, x_ref, hid_ref, logit_ref, w_ref, mask_ref, bias_ref, place_ref, placet_ref,
    back_ref, dlog_ref, dwd_ref, dwm_ref, sums_ref,
    even_s, odd_s, wd_ref, wdt_ref, wm_ref, wmt_ref, over_ref, wide_s, everywhere_s, turned_s, d_even_s, d_odd_s,
    d_spot_s, kernel_s, d_logit_s,
):
    wd_ref[...] = w_ref[...].astype(BF)
    wdt_ref[...] = nt(one_hot_eye(4 * C), wd_ref[...]).astype(BF)
    row = lax.broadcasted_iota(jnp.int32, (4 * C, 64), 0)
    mine_t = row // C == lax.broadcasted_iota(jnp.int32, (4 * C, 64), 1) // 16
    row = lax.broadcasted_iota(jnp.int32, (64, 4 * C), 0)
    mine = row // 16 == lax.broadcasted_iota(jnp.int32, (64, 4 * C), 1) // C
    for kind, part in enumerate(split(mask_ref[...])):
        spread_mask = nt(one_hot_mod((4 * C, C), C, 0), part).astype(BF)
        wide_t = jnp.where(mine_t, nn(spread_mask, one_hot_mod((NM, 64), 16, 1)), 0.0).astype(BF)
        wide_m = jnp.where(mine, nt(one_hot_mod((64, NM), 16, 0), spread_mask), 0.0).astype(BF)
        wmt_ref[:, kind * 64 : kind * 64 + 64] = wide_t
        wm_ref[:, kind * 4 * C : (kind + 1) * 4 * C] = wide_m
        if kind == 0:
            wmt_ref[:, 128:192] = wide_t
            wm_ref[:, 8 * C : 12 * C] = wide_m
    for sub in range(4):
        over_ref[sub * C : (sub + 1) * C, :] = bias_ref[7 * C : 8 * C]
        over_ref[4 * C + sub * 16 : 4 * C + (sub + 1) * 16, :] = bias_ref[8 * C : 8 * C + 16]
    own = logit_ref.shape[0]
    base = half_ref[0] * own
    lanes = lane_places()
    dwd_ref[...] = jnp.zeros_like(dwd_ref)
    wide_s[...] = jnp.zeros_like(wide_s)
    sums_ref[...] = jnp.zeros_like(sums_ref)
    cells = TILES * LANES
    row8 = lax.broadcasted_iota(jnp.int32, (8, cells), 0)
    color = (row8 % 4) != 3
    row16 = lax.broadcasted_iota(jnp.int32, (16, 32), 0)
    lane16 = lax.broadcasted_iota(jnp.int32, (16, 32), 1)

    for sub in range(4):
        everywhere_s[sub * WIN : (sub + 1) * WIN] = place_ref[sub]
        turned_s[:, sub * WIN : (sub + 1) * WIN] = placet_ref[sub]
    row = lax.broadcasted_iota(jnp.int32, (4 * WIN, 64), 0) // WIN
    own_spots = row == lax.broadcasted_iota(jnp.int32, (4 * WIN, 64), 1) // 16
    row = lax.broadcasted_iota(jnp.int32, (64, 4 * WIN), 0) // 16
    own_turned = row == lax.broadcasted_iota(jnp.int32, (64, 4 * WIN), 1) // WIN

    def frame(i, win_s, d_mix_s):
        t = base + i
        spread(image_tiles(x_ref, t), lanes, 1, win_s, 16, 0)
        window = jnp.concatenate([win_s[tile : tile + 3].reshape(WIN, LANES) for tile in range(TILES)], axis=1)
        window = window.reshape(18, 8, cells)
        logits = logit_ref[i]
        powers = jnp.exp(logits - jnp.max(logits, -1, keepdims=True))
        kernels = powers / jnp.sum(powers, -1, keepdims=True)
        kernels = jnp.where(row16 == 0, (lane16 == KK // 2).astype(F32), jnp.where(row16 <= NK, kernels, 0.0))
        kernel_s[i] = kernels
        spots = []
        turned = []
        for part in split(kernels):
            part = jnp.concatenate([part, part, part, part], axis=0)
            spots.append(jnp.where(own_spots, nt(everywhere_s[...], part), 0.0).astype(BF))
            turned.append(jnp.where(own_turned, nn(part, turned_s[...]), 0.0).astype(BF))
        spots = jnp.concatenate([spots[0], spots[1], spots[0]], axis=1)
        turned = jnp.concatenate(turned, axis=0)
        hidden = jnp.concatenate([hid_ref[t, tile] for tile in range(TILES)], axis=1)
        upper = nn(wdt_ref[...], hidden) + wide(over_ref[0 : 4 * C])
        gate = logistic(upper)
        active, active_rest = split(upper * gate)
        scores = nn(wm_ref[...], jnp.concatenate([active, active, active_rest], axis=0)) + wide(over_ref[4 * C : 4 * C + 64])
        scores = scores.reshape(4, 16, cells)
        powers = jnp.exp(scores - jnp.max(scores, 1, keepdims=True))
        masks = powers / jnp.sum(powers, 1, keepdims=True)
        mask_low, mask_rest = split(masks.reshape(64, cells))
        mixing = nn(spots, jnp.concatenate([mask_low, mask_low, mask_rest], axis=0)).reshape(4, 18, 8, cells)
        after = jnp.concatenate([x_ref[t + 1, tile] for tile in range(TILES)], axis=1).astype(F32)
        lost = None
        for sub in range(4):
            both = jnp.sum(mixing[sub] * window, 0)
            result = both + pltpu.roll(both, 4, 0)
            goal = after[(sub % 2) * 8 : (sub % 2) * 8 + 8]
            goal = jnp.where((row8 < 4) == (sub // 2 == 0), goal, pltpu.roll(goal, 4, 0))
            diff = jnp.where(color, result - goal, 0.0)
            weighted = diff * goal[3:4]
            part = jnp.where(row8 == 3, goal[3:4], weighted * diff)
            lost = part if lost is None else lost + part
            d_result = 2.0 * weighted
            d_mix_s[sub * WIN : (sub + 1) * WIN] = (window * d_result[None]).reshape(WIN, cells).astype(BF)
        sums_ref[192:200] += folded(lost)
        d_mask = nn(turned, d_mix_s[...])
        d_mask = (d_mask[:64] + d_mask[64:]).reshape(4, 16, cells)
        d_spot_s[i] = nt(mask_low, d_mix_s[...])
        inner = jnp.sum(masks * d_mask, 1, keepdims=True)
        d_score = (masks * (d_mask - inner)).reshape(64, cells)
        sums_ref[128:192] += folded(d_score)
        d_score_low, d_score_rest = split(d_score)
        d_active = nn(wmt_ref[...], jnp.concatenate([d_score_low, d_score_low, d_score_rest], axis=0))
        wide_s[...] += nt(d_score_low, active)
        d_upper = d_active * (gate * (1.0 + upper * (1.0 - gate)))
        sums_ref[0:128] += folded(d_upper)
        d_upper_low = d_upper.astype(BF)
        dwd_ref[...] += nt(hidden, d_upper_low)
        back = nn(wd_ref[...], d_upper_low).astype(BF)
        for tile in range(TILES):
            back_ref[i, tile] = back[:, tile * LANES : (tile + 1) * LANES]

    def two_frames(pair, _):
        frame(2 * pair, even_s, d_even_s)
        frame(2 * pair + 1, odd_s, d_odd_s)
        return 0

    lax.fori_loop(0, own // 2, two_frames, 0)
    d_kernels = None
    for sub in range(4):
        rows = jnp.concatenate([d_spot_s[i, sub * 16 : sub * 16 + 16] for i in range(own)], axis=0)
        place = lax.broadcasted_iota(jnp.int32, rows.shape, 1) // WIN
        part = nn_exact(jnp.where(place == sub, rows, 0.0), everywhere_s[...].astype(F32))
        d_kernels = part if d_kernels is None else d_kernels + part
    for i in range(own):
        kernels = kernel_s[i]
        d_one = d_kernels[16 * i : 16 * i + 16]
        inner = jnp.sum(d_one * kernels, -1, keepdims=True)
        d_logit_s[16 * i : 16 * i + 16] = kernels * (d_one - inner)
    total = jnp.zeros(dlog_ref.shape, F32)
    tap = lax.broadcasted_iota(jnp.int32, (32, 2 * LANES), 0)
    lane = lax.broadcasted_iota(jnp.int32, (32, 2 * LANES), 1)
    for kernel in range(NK):
        place = ((tap < KK) & (lane == kernel * KK + tap)).astype(F32)
        total = total + nn_exact(d_logit_s[pl.ds(kernel + 1, own, stride=16), :], place)
    dlog_ref[...] = total
    row = lax.broadcasted_iota(jnp.int32, (64, 4 * C), 0)
    lane = lax.broadcasted_iota(jnp.int32, (64, 4 * C), 1)
    own_block = jnp.where(row // 16 == lane // C, wide_s[...], 0.0)
    fold = lax.broadcasted_iota(jnp.int32, (4 * C, LANES), 0) % C
    fold = (fold == lax.broadcasted_iota(jnp.int32, (4 * C, LANES), 1)).astype(F32)
    dwm_ref[...] = jnp.sum(nn_exact(own_block, fold).reshape(4, 16, LANES), 0)


def backward_kernel(
    half_ref, far_act_ref, far_cell_ref, dec_ref, other_dec_ref, fc_ref, other_fc_ref, w_ref,
    keep_ref, denc_ref, lines_ref,
    gate_s, back_s, state_s, wb_s, even_s, odd_s, act_ref, cell_ref, sems,
):
    steps = far_act_ref.shape[0]

    def act_copy(t):
        return pltpu.make_async_copy(far_act_ref.at[t], act_ref.at[t], sems.at[0, t])

    def cell_copy(t):
        return pltpu.make_async_copy(far_cell_ref.at[t], cell_ref.at[t], sems.at[1, t])

    for t in reversed(range(steps)):
        act_copy(t).start()
        cell_copy(t).start()
    for tap in range(KK):
        place = tap % KS * 2 * C
        turn = (KS - 1 - tap // KS) * 4 * C
        wb_s[place : place + 2 * C, turn : turn + 4 * C] = w_ref[tap * 2 * C : (tap + 1) * 2 * C, :].astype(BF)
    own = steps // HALVES
    lanes = lane_places()
    back_s[...] = jnp.zeros_like(back_s)
    state_s[...] = jnp.zeros_like(state_s)
    lines_ref[...] = jnp.zeros_like(lines_ref)

    def prepare(t, factor_s):
        half = t // own
        inside = t % own
        mine = half == half_ref[0]
        earlier = jnp.maximum(t - 1, 0)
        started = jnp.where(t > 0, 1.0, 0.0)
        for tile in range(TILES):
            pair = tile // 2
            low_row = tile % 2
            parts = [
                jnp.where(
                    mine, fc_ref[2 * band + pair, inside].astype(F32), other_fc_ref[2 * band + pair, inside].astype(F32)
                )[8 * low_row : 8 * low_row + 8]
                for band in range(BANDS)
            ]
            from_fc = jnp.concatenate(block_swap(parts, lanes[1]), axis=0)
            from_dec = jnp.where(
                mine, dec_ref[inside, tile].astype(F32), other_dec_ref[inside, tile].astype(F32)
            )
            gate_in = act_ref[t, tile, 0:C]
            gate_keep = act_ref[t, tile, C : 2 * C]
            gate_out = act_ref[t, tile, 2 * C : 3 * C]
            gate_new = act_ref[t, tile, 3 * C : 4 * C]
            bent = jnp.tanh(cell_ref[t, tile])
            factors = [
                from_fc + from_dec,
                gate_out * (1.0 - bent * bent),
                gate_keep,
                gate_new * gate_in * (1.0 - gate_in),
                (cell_ref[earlier, tile] * started) * gate_keep * (1.0 - gate_keep),
                bent * gate_out * (1.0 - gate_out),
                gate_in * (1.0 - gate_new * gate_new),
            ]
            for index, factor in enumerate(factors):
                factor_s[tile, index * C : (index + 1) * C] = factor

    def retreat(t, factor_s, next_s):
        half = t // own
        inside = t % own
        counted = jnp.where(half == half_ref[0], 1.0, 0.0)
        place = jnp.where(half == half_ref[0], inside, own)
        tiles = []
        for tile in range(TILES):
            back = back_s[tile] + factor_s[tile, 0:C]
            d_cell = state_s[tile] + back * factor_s[tile, C : 2 * C]
            state_s[tile] = d_cell * factor_s[tile, 2 * C : 3 * C]
            d_gates = jnp.concatenate(
                [
                    d_cell * factor_s[tile, 3 * C : 4 * C],
                    d_cell * factor_s[tile, 4 * C : 5 * C],
                    back * factor_s[tile, 5 * C : 6 * C],
                    d_cell * factor_s[tile, 6 * C : 7 * C],
                ],
                axis=0,
            )
            lines_ref[...] += d_gates * counted
            low = d_gates.astype(BF)
            keep_ref[place, tile] = low
            tiles.append(low.astype(F32))
        for index in range(TILES + 4):
            tile = index - 2
            gate_s[index] = moved(tiles[tile % TILES], lanes, 0, tile // TILES).astype(BF)
        prepare(jnp.maximum(t - 1, 0), next_s)
        for two in range(0, TILES, 2):
            sums = nn(wb_s[...], stacked(gate_s, two, KS))
            for one in range(2):
                part = sums[:, one * LANES : (one + 1) * LANES]
                total = None
                for shift in range(KS):
                    value = moved(part[shift * 2 * C : (shift + 1) * 2 * C], lanes, 2 - shift, 0)
                    total = value if total is None else total + value
                denc_ref[place, two + one] = total[:C]
                back_s[two + one] = total[C:]

    cell_copy(steps - 1).wait()
    act_copy(steps - 1).wait()
    cell_copy(steps - 2).wait()
    prepare(steps - 1, even_s)

    def retreat_two(pair, _):
        t = steps - 1 - 2 * pair
        act_copy(t - 1).wait()

        @pl.when(pair < steps // 2 - 1)
        def _():
            act_copy(t - 2).wait()
            cell_copy(t - 2).wait()
            cell_copy(t - 3).wait()

        retreat(t, even_s, odd_s)
        retreat(t - 1, odd_s, even_s)
        return 0

    lax.fori_loop(0, steps // 2, retreat_two, 0)


ROW_DEC = KK * 2 * C
ROW_COND = ROW_DEC + C
ROW_ENC = ROW_COND + 32
ROW_MASK = ROW_ENC + C
ROW_VECTOR = ROW_MASK + 16
ROWS = ROW_VECTOR + 16
PART = 64
SMALL = ROWS - ROW_DEC


def vector_places():
    place = np.zeros((7 * C + 4 * C + 64, 5 * LANES), np.float32)
    for line in range(7 * C):
        place[line, line] = 1.0
    for line in range(4 * C):
        place[7 * C + line, 7 * C + NK * KK + line % C] = 1.0
    for line in range(64):
        if line % 16 < NM:
            place[11 * C + line, 8 * C + NK * KK + line % 16] = 1.0
    return place


def logit_map_gradient(hid_ref, sum_ref, out_ref, turned_s):
    logits = NK * KK
    groups, items, width = sum_ref.shape
    eye = one_hot_eye(width)
    for group in range(groups):
        turned_s[:, group * items : (group + 1) * items] = nt(eye, sum_ref[group]).astype(BF)
    squares = jnp.zeros((1, LANES), F32)
    stride = 2 * WB * C // LANES
    for row in range(2):
        for start in range(0, WB * C, 2 * LANES):
            hid = jnp.concatenate(
                [hid_ref[group, row, :, start : start + 2 * LANES] for group in range(groups)], axis=0
            )
            grad = nn(turned_s[...], hid)[:logits]
            for one in range(2):
                part = grad[:, one * LANES : (one + 1) * LANES]
                squares = squares + jnp.sum(part * part, 0, keepdims=True)
                out_ref[pl.ds((start // LANES + one) * 2 + row, logits, stride=stride), :] = part
    return jnp.sum(squares, 1, keepdims=True) * (1.0 / groups)


def pack_kernel(
    half_ref, x_ref, enc_ref, hid_ref, keep_ref, denc_ref, lines_ref, head_ref, ddec_ref, dmask_ref, dcond_ref,
    dline_ref, far_hid_ref, sum_ref, we_ref, bias_ref, place_ref, encoder_ref,
    block_ref, far_dfc_ref,
    win_s, join_s, dwe_s, sums_s, packed_s, every_s, dfc_s, turned_s, sems,
):
    every_copy = pltpu.make_async_copy(far_hid_ref, every_s, sems.at[0])
    every_copy.start()
    own = keep_ref.shape[0] - 1
    base = half_ref[0] * own
    lanes = lane_places()
    dwe_s[...] = jnp.zeros_like(dwe_s)
    sums_s[...] = jnp.zeros_like(sums_s)
    packed_s[...] = jnp.zeros_like(packed_s)

    def gather(i, _):
        t = base + i
        earlier = jnp.maximum(t - 1, 0)
        started = jnp.where(t > 0, 1.0, 0.0)
        spread([enc_ref[t, tile].astype(F32) for tile in range(TILES)], lanes, 2, join_s, 2 * C, 0)
        spread(
            [hid_ref[earlier, tile].astype(F32) * started for tile in range(TILES)], lanes, 2, join_s, 2 * C, C
        )
        d_gates = jnp.concatenate([keep_ref[i, tile] for tile in range(TILES)], axis=1)
        joined = jnp.concatenate([stacked(join_s, 0, KS), stacked(join_s, 2, KS)], axis=1)
        packed_s[0:ROW_DEC] += nt(joined, d_gates)
        spread(image_tiles(x_ref, t), lanes, 1, win_s, 16, 0)
        for two in range(0, TILES, 2):
            window = stacked(win_s, two, 3)
            pre = nn(we_ref[...], window) + twice(bias_ref[0:C])
            centered = pre - jnp.mean(pre, 0, keepdims=True)
            scale = lax.rsqrt(jnp.mean(centered * centered, 0, keepdims=True) + NORM_EPS)
            normal = centered * scale
            gain = twice(bias_ref[C : 2 * C])
            value = normal * gain + twice(bias_ref[2 * C : 3 * C])
            gate = logistic(value)
            d_out = jnp.concatenate([denc_ref[i, two], denc_ref[i, two + 1]], axis=1)
            d_value = d_out * (gate * (1.0 + value * (1.0 - gate)))
            d_gain = d_value * normal
            d_normal = d_value * gain
            d_pre = scale * (
                d_normal
                - jnp.mean(d_normal, 0, keepdims=True)
                - normal * jnp.mean(d_normal * normal, 0, keepdims=True)
            )
            sums_s[0:C] += d_pre[:, :LANES] + d_pre[:, LANES:]
            sums_s[C : 2 * C] += d_gain[:, :LANES] + d_gain[:, LANES:]
            sums_s[2 * C : 3 * C] += d_value[:, :LANES] + d_value[:, LANES:]
            dwe_s[...] += nt(d_pre.astype(BF), window)
        return 0

    lax.fori_loop(0, own, gather, 0)
    every_copy.wait()
    squares = logit_map_gradient(every_s, sum_ref, dfc_s, turned_s)
    dfc_copy = pltpu.make_async_copy(dfc_s, far_dfc_ref, sems.at[1])
    dfc_copy.start()
    packed_s[ROW_DEC:ROW_COND] = ddec_ref[...]
    packed_s[ROW_COND:ROW_ENC] = dcond_ref[...]
    packed_s[ROW_ENC:ROW_MASK] = nn_exact(dwe_s[...], encoder_ref[...])
    packed_s[ROW_MASK:ROW_VECTOR] = dmask_ref[...]
    ones = jnp.ones((8, LANES), F32)
    sums_s[3 * C : 7 * C] = lines_ref[...]
    sums_s[7 * C : 11 * C + 64] = head_ref[0:192]
    line = nn_exact(nt_exact(ones, sums_s[...]), place_ref[...].astype(F32))[0:1] + jnp.sum(dline_ref[...], 0, keepdims=True)
    packed_s[ROW_VECTOR : ROW_VECTOR + 8] = jnp.concatenate(
        [line[:, place * LANES : (place + 1) * LANES] for place in range(5)] + [jnp.zeros((3, LANES), F32)], axis=0
    )
    lost = jnp.sum(jnp.sum(head_ref[192:195], 0, keepdims=True), 1, keepdims=True)
    counted = jnp.sum(head_ref[195:196], 1, keepdims=True)
    lane = lax.broadcasted_iota(jnp.int32, (1, LANES), 1)
    value = jnp.where(lane == 0, lost, jnp.where(lane == 1, counted, jnp.where(lane == 2, squares, 0.0)))
    terms = []
    for _ in range(3):
        low = value.astype(BF).astype(F32)
        terms.append(low)
        value = value - low
    devices = block_ref.shape[0]
    large = ROW_DEC // devices
    small = SMALL // devices
    fill = jnp.zeros((PART - large - 2 * small - 3, LANES), F32)
    for device in range(devices):
        value = packed_s[ROW_DEC + device * small : ROW_DEC + (device + 1) * small]
        high = value.astype(BF).astype(F32)
        rows = [packed_s[device * large : (device + 1) * large], high, value - high] + terms + [fill]
        block_ref[device] = jnp.concatenate(rows, axis=0).astype(BF)
    dfc_copy.wait()


def total_kernel(got_ref, out_ref, scalar_ref):
    devices, rows, _ = got_ref.shape
    total = got_ref[0].astype(F32)
    for device in range(1, devices):
        total = total + got_ref[device].astype(F32)
    large = ROW_DEC // devices
    small = SMALL // devices
    end = large + 2 * small
    scalar_ref[...] = total[end : end + 1] + total[end + 1 : end + 2] + total[end + 2 : end + 3]
    value = total[large : large + small] + total[large + small : end]
    high = value.astype(BF).astype(F32)
    low = jnp.concatenate([total[:large], high, value - high, total[end:]], axis=0).astype(BF)
    for device in range(devices):
        out_ref[device] = low


def update(weight, grad, factor, first, second, rate):
    first = BETA_ONE * first + (factor * (1.0 - BETA_ONE)) * grad
    second = BETA_TWO * second + (factor * factor * (1.0 - BETA_TWO)) * (grad * grad)
    root = (second * lax.rsqrt(second)) * (1.0 - BETA_TWO**STEP_NO) ** -0.5 + ADAM_EPS
    turned = pl.reciprocal(root, approx=True)
    turned = turned * (2.0 - root * turned)
    step = first * turned * (rate / (1.0 - BETA_ONE**STEP_NO))
    return (weight * (1.0 - rate * DECAY) - step, first, second)


def update_kernel(rates, got_ref, scalar_ref, dfc_ref, *refs):
    weights, firsts, seconds = refs[0:7], refs[7:14], refs[14:21]
    norm_ref = refs[21]
    news = refs[22:29], refs[29:36], refs[36:43]
    packed_s, fc_s, lstm_s, sems, fc_in_s, lstm_in_s, in_sems = refs[43:]
    ins = []
    plan = ((2, fc_in_s, 5), (1, lstm_in_s, 2))
    for index, scratch, chunks in plan:
        sources = [weights[index], firsts[index], seconds[index]] + ([dfc_ref] if index == 2 else [])
        chunk = sources[0].shape[0] // chunks
        for at in range(chunks):
            for kind, source in enumerate(sources):
                here = pl.ds(at * chunk, chunk)
                copy = pltpu.make_async_copy(source.at[here], scratch.at[kind, here], in_sems.at[len(ins)])
                copy.start()
                ins.append(copy)
    devices = got_ref.shape[0]
    large = ROW_DEC // devices
    small = SMALL // devices
    for device in range(devices):
        rows = got_ref[device].astype(F32)
        packed_s[device * large : (device + 1) * large] = rows[:large]
        packed_s[ROW_DEC + device * small : ROW_DEC + (device + 1) * small] = (
            rows[large : large + small] + rows[large + small : large + 2 * small]
        )

    def add_rows(block, total):
        rows = packed_s[pl.ds(pl.multiple_of(block * 32, 32), 32)]
        return total + jnp.sum((rows * rows).reshape(4, 8, LANES), 0)

    squares = lax.fori_loop(0, ROWS // 32, add_rows, jnp.zeros((8, LANES), F32))
    terms = scalar_ref[...]
    squares = jnp.sum(jnp.sum(squares, 0, keepdims=True), 1, keepdims=True) + terms[:, 2:3]
    inv_count = 1.0 / terms[:, 1:2]
    norm = jnp.sqrt(squares) * inv_count
    factor = inv_count * (CLIP_NORM / jnp.maximum(norm, CLIP_NORM))
    norm_ref[...] = jnp.sum(norm)

    copies = []
    for (index, scratch, chunks), outs in zip(plan, (fc_s, lstm_s)):
        rows = scratch.shape[1]
        chunk = rows // chunks
        wide = chunk // 2
        for at in range(chunks):
            for _ in range(scratch.shape[0]):
                ins.pop(0).wait()

            def block(i, _):
                here = pl.ds(pl.multiple_of(at * chunk + i * wide, 8), wide)
                grad = scratch[3, here] if index == 2 else packed_s[here]
                new = update(scratch[0, here], grad, factor, scratch[1, here], scratch[2, here], rates[index])
                for kind in range(3):
                    outs[kind, here] = new[kind]
                return 0

            lax.fori_loop(0, 2, block, 0)
            for kind in range(3):
                here = pl.ds(at * chunk, chunk)
                copy = pltpu.make_async_copy(outs.at[kind, here], news[kind][index].at[here], sems.at[len(copies)])
                copy.start()
                copies.append(copy)

    def step(index, grad):
        new = update(weights[index][...], grad, factor, firsts[index][...], seconds[index][...], rates[index])
        for kind in range(3):
            news[kind][index][...] = new[kind]

    step(0, packed_s[ROW_ENC:ROW_MASK, : KK * 3])
    cond = jnp.concatenate([packed_s[ROW_COND : ROW_COND + 16], packed_s[ROW_COND + 16 : ROW_COND + 32]], axis=1)
    step(3, cond[:COND, : NK * KK])
    step(4, packed_s[ROW_DEC:ROW_COND])
    step(5, packed_s[ROW_MASK : ROW_MASK + NM, 0:C])
    line = jnp.concatenate([packed_s[ROW_VECTOR + place : ROW_VECTOR + place + 1] for place in range(5)], axis=1)
    width = weights[6].shape[0]
    new = update(
        weights[6][...].reshape(1, width), line[:, :width], factor, firsts[6][...].reshape(1, width),
        seconds[6][...].reshape(1, width), rates[6],
    )
    for kind in range(3):
        news[kind][6][...] = new[kind].reshape(width)
    for copy in copies:
        copy.wait()


SMEM_SPEC = pl.BlockSpec(memory_space=pltpu.SMEM)
VMEM_SPEC = pl.BlockSpec(memory_space=pltpu.VMEM)


def cost(micros):
    return pl.CostEstimate(flops=int(micros * 8e8), bytes_accessed=1024, transcendentals=0)


ANY_SPEC = pl.BlockSpec(memory_space=pl.ANY)


def call(kernel, micros, outs, scratch, half, *operands, far_in=(), far_out=()):
    def specs(count, far):
        return [ANY_SPEC if index in far else VMEM_SPEC for index in range(count)]

    return pl.pallas_call(
        kernel,
        cost_estimate=cost(micros),
        out_shape=[jax.ShapeDtypeStruct(shape, kind) for shape, kind in outs],
        in_specs=[SMEM_SPEC] + specs(len(operands), far_in),
        out_specs=specs(len(outs), far_out),
        scratch_shapes=[
            pltpu.SemaphoreType.DMA(kind) if shape is None else pltpu.VMEM(shape, kind) for shape, kind in scratch
        ],
        compiler_params=pltpu.CompilerParams(vmem_limit_bytes=VMEM_BYTES),
    )(half, *operands)


def columns(values):
    return jnp.broadcast_to(values[:, None], (values.shape[0], LANES))


def exchange(block, axes):
    return lax.all_to_all(block, axes, 0, 0, tiled=True)


def to_all(block, axes):
    count = lax.axis_size(axes)
    return exchange(jnp.broadcast_to(block[None], (count,) + block.shape), axes)


def strip_order():
    sent = np.arange(WB * C)
    natural = sent % WB * C + sent // WB % 4 * 8 + sent // LANES
    order = np.zeros((WB * C, WB * C), np.float32)
    order[sent, natural] = 1.0
    return order


def whole_clips(
    frames, valid, flags, actions, states, latent,
    w_enc, w_lstm, w_fc, w_cond, w_deconv, w_mask, vector,
    m_enc, m_lstm, m_fc, m_cond, m_deconv, m_mask, m_vector,
    v_enc, v_lstm, v_fc, v_cond, v_deconv, v_mask, v_vector,
):
    clips, shots, _, strip_rows, width = frames.shape
    steps = shots - 1
    own = steps // HALVES
    count = lax.axis_size("row")
    place = lax.axis_index("row")
    clip = place // HALVES
    half = place % HALVES
    half_1 = half.reshape(1).astype(jnp.int32)
    b_enc, g_enc, s_enc, b_lstm, b_fc, b_dec, b_mask = split_vector(vector)
    places, encoder = window_places()
    flagged = jnp.pad(valid.astype(BF), ((0, 0), (1, 0), (0, 0), (0, 0)))
    pieces = jnp.concatenate([frames, flagged[:, :, None]], axis=2).reshape(clips, shots, 4, 2, 2, width)
    pieces = jnp.transpose(pieces, (0, 1, 4, 2, 3, 5)).reshape(clips, shots * 8, LANES)
    pieces = jnp.pad(pieces, ((0, 0), (0, 8), (0, 0)))
    raw = exchange(jnp.repeat(pieces, HALVES, axis=0), "row")

    wide_enc = jnp.einsum(
        "rk,ko->or", jnp.asarray(encoder, BF), w_enc.astype(BF), preferred_element_type=F32
    ).astype(BF)
    bias = columns(
        jnp.concatenate([vector[: 7 * C], b_dec, jnp.pad(b_mask, (0, 16 - NM), constant_values=-1e30)])
    )
    cells = (steps, TILES, C, LANES)
    x, enc, hid, act, cell, strips_out = call(
        forward_kernel,
        20,
        [
            ((shots, TILES, 16, LANES), BF), ((shots,) + cells[1:], BF), (cells, BF),
            ((steps, TILES, 4 * C, LANES), F32),
            (cells, F32), ((count, own, 16, LANES), BF),
        ],
        [
            ((6, 48, LANES), BF), ((8, KS * C, LANES), BF), ((8, KS * C, LANES), BF), ((TILES, C, LANES), F32),
            ((KK * C, LANES), BF), ((4 * C, KK * C), BF), ((4 * C, KK * C), BF),
            ((TILES, 4 * C, LANES), F32), ((TILES, 4 * C, LANES), F32),
            ((steps, TILES, 4 * C, LANES), F32), (cells, F32), (None, (2, steps)),
        ],
        half_1, raw, wide_enc, w_lstm, bias, far_out=(3, 4),
    )
    items = clips * steps
    order = jnp.asarray(strip_order(), BF)
    k_fc = jnp.pad(w_fc.astype(BF), ((0, 0), (0, 2 * LANES - NK * KK), (0, 0)))
    k_fc = jnp.einsum("jnl,kl->jnk", k_fc, order, preferred_element_type=F32).astype(BF)
    strip_hid = exchange(strips_out, "row").reshape(items, 2, WB * C)
    parts = jnp.einsum("mjk,jnk->mn", strip_hid, k_fc, preferred_element_type=F32)
    strip_hid = jnp.einsum("mjk,kl->jml", strip_hid, order, preferred_element_type=F32).astype(BF)
    strip_hid_all = to_all(strip_hid, "clip")
    summed = jnp.sum(exchange(parts.reshape(count, own, 2 * LANES), "row"), 0)[:, : NK * KK]
    presence = flags.astype(F32)
    conditions = jnp.concatenate(
        [
            actions * presence[..., :1],
            states * presence[..., 1:],
            jnp.broadcast_to(latent[:, None, :], (clips, steps, latent.shape[1])),
        ],
        -1,
    )
    cond = lax.dynamic_slice(conditions, (clip, half * own, 0), (1, own, COND))[0]
    logits = summed + (jnp.dot(cond, w_cond, precision=HIGH) + b_fc)
    logits = jnp.pad(
        logits.reshape(own, NK, KK), ((0, 0), (1, 5), (0, 32 - KK)), constant_values=-1e30
    )
    dec, d_logit, d_dec, d_mask, head_sums = call(
        head_kernel,
        30,
        [
            ((own, TILES, C, LANES), BF), ((own, 2 * LANES), F32), ((C, 4 * C), F32), ((16, LANES), F32),
            ((200, LANES), F32),
        ],
        [
            ((6, 48, LANES), F32), ((6, 48, LANES), F32), ((C, 4 * C), BF), ((4 * C, C), BF), ((64, 12 * C), BF),
            ((4 * C, 192), BF), ((4 * C + 64, LANES), F32), ((64, 4 * C), F32),
            ((4 * WIN, 32), BF), ((32, 4 * WIN), BF), ((4 * WIN, TILES * LANES), BF),
            ((4 * WIN, TILES * LANES), BF), ((own, 64, 4 * WIN), F32),
            ((own, 16, 32), F32), ((own * 16, 32), F32),
        ],
        half_1, x, hid, logits, w_deconv, w_mask.T, bias,
        jnp.asarray(places, BF), jnp.asarray(places.transpose(0, 2, 1), BF),
    )
    d_logit, strip_hid_all = lax.optimization_barrier((d_logit, strip_hid_all))
    every_sum = to_all(d_logit.astype(BF), ("clip", "row")).reshape(-1, items, 2 * LANES)
    d_sum = lax.dynamic_index_in_dim(every_sum, lax.axis_index("clip"), 0, False)
    back_fc = jnp.einsum("mn,jnk->mjk", d_sum, k_fc, preferred_element_type=F32).astype(BF)
    back_fc = exchange(back_fc.reshape(count, own, 16, LANES), "row")
    swap = [(index, index ^ 1) for index in range(count)]

    keep, d_enc, lines = call(
        backward_kernel,
        0.1,
        [((own + 1, TILES, 4 * C, LANES), BF), ((own + 1, TILES, C, LANES), F32), ((4 * C, LANES), F32)],
        [
            ((8, 4 * C, LANES), BF), ((TILES, C, LANES), F32), ((TILES, C, LANES), F32),
            ((KS * 2 * C, KS * 4 * C), BF), ((TILES, 7 * C, LANES), F32), ((TILES, 7 * C, LANES), F32),
            ((steps, TILES, 4 * C, LANES), F32), (cells, F32), (None, (2, steps)),
        ],
        half_1, act, cell, dec, lax.ppermute(dec, "row", swap), back_fc, lax.ppermute(back_fc, "row", swap), w_lstm,
        far_in=(0, 1),
    )
    d_cond = jnp.dot(cond.T, d_logit, precision=HIGH)
    d_cond = jnp.pad(d_cond, ((0, 16 - COND), (0, 0)))
    d_cond = jnp.concatenate([d_cond[:, :LANES], d_cond[:, LANES:]], axis=0)
    d_line = jnp.pad(d_logit[:, : NK * KK], ((0, 0), (7 * C, 5 * LANES - 7 * C - NK * KK)))
    both = ("clip", "row")
    devices = lax.axis_size(both)
    block, d_fc = call(
        pack_kernel,
        12,
        [((devices, PART, LANES), BF), ((w_fc.size // LANES, LANES), F32)],
        [
            ((6, 48, LANES), BF), ((8, KS * 2 * C, LANES), BF), ((C, WIN), F32), ((11 * C + 64, LANES), F32),
            ((ROWS, LANES), F32), (strip_hid_all.shape, BF), ((w_fc.size // LANES, LANES), F32),
            ((2 * LANES, strip_hid_all.shape[0] * items), BF), (None, (2,)),
        ],
        half_1, x, enc, hid, keep, d_enc, lines, head_sums, d_dec, d_mask, d_cond, d_line, strip_hid_all, every_sum,
        wide_enc, bias,
        jnp.asarray(vector_places(), BF), jnp.asarray(np.pad(encoder, ((0, 0), (0, LANES - KK * 3))), F32),
        far_in=(11,), far_out=(1,),
    )
    sums, scalars = pl.pallas_call(
        total_kernel,
        out_shape=[jax.ShapeDtypeStruct(block.shape, BF), jax.ShapeDtypeStruct((1, LANES), F32)],
        in_specs=[VMEM_SPEC],
        out_specs=[VMEM_SPEC, VMEM_SPEC],
        compiler_params=pltpu.CompilerParams(vmem_limit_bytes=VMEM_BYTES),
    )(exchange(block, both))
    sums = exchange(sums, both)
    rates = learning_rates(w_fc.shape[0] * count)

    def shown(group):
        enc, lstm, fc, cond, dec, mask, line = group
        fc = fc.reshape(2, NK * KK, WB * C // LANES, LANES)
        fc = jnp.transpose(fc, (1, 2, 0, 3)).reshape(-1, LANES)
        return [enc.T, lstm, fc, cond, dec, mask.T, line]

    def back(group):
        enc, lstm, fc, cond, dec, mask, line = group
        fc = fc.reshape(NK * KK, WB * C // LANES, 2, LANES)
        fc = jnp.transpose(fc, (2, 0, 1, 3)).reshape(w_fc.shape)
        return [enc.T, lstm, fc, cond, dec, mask.T, line]

    weights = shown([w_enc, w_lstm, w_fc, w_cond, w_deconv, w_mask, vector])
    firsts = shown([m_enc, m_lstm, m_fc, m_cond, m_deconv, m_mask, m_vector])
    seconds = shown([v_enc, v_lstm, v_fc, v_cond, v_deconv, v_mask, v_vector])
    shapes = [jax.ShapeDtypeStruct(value.shape, F32) for value in weights]
    places_out = [VMEM_SPEC, ANY_SPEC, ANY_SPEC] + [VMEM_SPEC] * 4
    new = pl.pallas_call(
        functools.partial(update_kernel, rates),
        out_shape=[jax.ShapeDtypeStruct((), F32)] + shapes * 3,
        in_specs=[VMEM_SPEC, VMEM_SPEC, ANY_SPEC] + places_out * 3,
        out_specs=[SMEM_SPEC] + places_out * 3,
        scratch_shapes=[
            pltpu.VMEM((ROWS, LANES), F32), pltpu.VMEM((3,) + shapes[2].shape, F32),
            pltpu.VMEM((3,) + shapes[1].shape, F32), pltpu.SemaphoreType.DMA((21,)),
            pltpu.VMEM((4,) + shapes[2].shape, F32), pltpu.VMEM((3,) + shapes[1].shape, F32),
            pltpu.SemaphoreType.DMA((26,)),
        ],
        compiler_params=pltpu.CompilerParams(vmem_limit_bytes=VMEM_BYTES),
    )(sums, scalars, d_fc, *weights, *firsts, *seconds)
    outs = [scalars[0, 0], scalars[0, 1], new[0]]
    for kind in range(3):
        outs.extend(back(new[1 + 7 * kind : 8 + 7 * kind]))
    return tuple(outs)


def shards(frames, *rest):
    clips, _, _, strip_rows, width = frames.shape
    count = lax.axis_size("row")
    one_clip = strip_rows * count // 2 == TILES * BANDS and width // 2 == WB
    if one_clip and clips * HALVES == count:
        return whole_clips(frames, *rest)
    return strips(frames, *rest)


def solution(mesh):
    placed = (
        P("clip", None, None, "row", None),
        P("clip", None, "row", None),
        P("clip", None, None),
        P("clip", None, None),
        P("clip", None, None),
        P("clip", None),
        P(),
        P(),
        P("row", None, None),
        P(),
        P(),
        P(),
        P(),
        P(),
        P(),
        P("row", None, None),
        P(),
        P(),
        P(),
        P(),
        P(),
        P(),
        P("row", None, None),
        P(),
        P(),
        P(),
        P(),
    )
    return jax.shard_map(
        shards,
        mesh=mesh,
        in_specs=placed,
        out_specs=(
            P(),
            P(),
            P(),
            P(),
            P(),
            P("row", None, None),
            P(),
            P(),
            P(),
            P(),
            P(),
            P(),
            P("row", None, None),
            P(),
            P(),
            P(),
            P(),
            P(),
            P(),
            P("row", None, None),
            P(),
            P(),
            P(),
            P(),
        ),
        check_vma=False,
    )
```

```python
import functools

import jax
import jax.numpy as jnp
import numpy as np
from jax import lax
from jax.experimental import pallas as pl
from jax.experimental.pallas import tpu as pltpu
from jax.sharding import PartitionSpec as P

C = 32
KS = 5
NK = 10
STEP_NO = 10
KK = 25
NM = 11
COND = 15
WB = 32


NORM_EPS = 1e-05
CLIP_NORM = 0.001
BETA_ONE = 0.9
BETA_TWO = 0.999
ADAM_EPS = 1e-12
DECAY = 0.01
HIGH = lax.Precision.HIGHEST


def padded_2(cells, sides, width):
    for axis, dim in sides:
        count = lax.axis_size(axis)
        ends = count - 1
        head = lax.slice_in_dim(cells, 0, width, axis=dim)
        tail = lax.slice_in_dim(cells, cells.shape[dim] - width, cells.shape[dim], axis=dim)
        cells = jnp.concatenate(
            [
                lax.ppermute(tail, axis, [(i, (i + 1) % count) for i in range(ends)]),
                cells,
                lax.ppermute(head, axis, [((i + 1) % count, i) for i in range(ends)]),
            ],
            axis=dim,
        )
    return cells


def passed_along(block, axis, distance):
    devices = range(lax.axis_size(axis))
    route = [(i - distance, i) for i in devices if i - distance in devices]
    return lax.ppermute(block, axis, route)


def split_vector(vector):
    counts = [C, C, C, 4 * C, NK * KK, C, NM]
    pieces = []
    start = 0
    for count in counts:
        pieces.append(vector[start : start + count])
        start += count
    return pieces


def norm_act(pre, gain, shift):
    centered = pre - jnp.mean(pre, -1, keepdims=True)
    scale = lax.rsqrt(jnp.mean(centered * centered, -1, keepdims=True) + NORM_EPS)
    return jax.nn.silu(centered * scale * gain + shift)


def cell_step(gates, cell):
    gate_in, gate_keep, gate_out, gate_new = jnp.split(gates, 4, axis=-1)
    new_cell = jax.nn.sigmoid(gate_keep + 1.0) * cell + jax.nn.sigmoid(gate_in) * jnp.tanh(gate_new)
    return (jax.nn.sigmoid(gate_out) * jnp.tanh(new_cell), new_cell)


def upsample(values):
    clips, rows_in, cols_in, depth = values.shape
    grid = values.reshape(clips, rows_in, cols_in, 2, 2, depth // 4)
    return jnp.transpose(grid, (0, 1, 3, 2, 4, 5)).reshape(
        clips, 2 * rows_in, 2 * cols_in, depth // 4
    )


def predict(logits, upper, w_mask, b_mask, prev_pad):
    clips = logits.shape[0]
    kernels = jax.nn.softmax(logits.reshape(clips, NK, KK), axis=-1)
    activated = jax.nn.silu(upper)
    blend = jax.nn.softmax(
        jnp.einsum("byxc,cm->byxm", activated, w_mask, precision=HIGH) + b_mask, axis=-1
    )
    mixing = jnp.einsum("byxk,bko->byxo", blend[..., 1:], kernels, precision=HIGH)
    height = prev_pad.shape[1] - 4
    breadth = prev_pad.shape[2] - 4
    result = blend[..., :1] * prev_pad[:, 2 : 2 + height, 2 : 2 + breadth, :]
    for offset in range(KK):
        top = offset // KS
        left = offset % KS
        result = (
            result
            + mixing[..., offset : offset + 1]
            * prev_pad[:, top : top + height, left : left + breadth, :]
        )
    return result


def patches(padded, stride, out_rows, out_cols):
    pieces = []
    for offset in range(KK):
        top = offset // KS
        left = offset % KS
        pieces.append(
            padded[
                :,
                top : top + stride * (out_rows - 1) + 1 : stride,
                left : left + stride * (out_cols - 1) + 1 : stride,
                :,
            ]
        )
    return jnp.concatenate(pieces, -1)


def unpatch(grads, shape, stride):

    def extract(padded):
        return patches(padded, stride, grads.shape[1], grads.shape[2])

    _, pullback = jax.vjp(extract, jnp.zeros(shape, jnp.float32))
    return pullback(grads)[0]


def product(left, right, form):
    return jnp.einsum(form, left, right, preferred_element_type=jnp.float32)


def learning_rates(rows_total):
    return [
        0.5 * (KK * 3) ** (-0.5),
        0.5 * (KK * 2 * C) ** (-0.5),
        0.5 * (rows_total * WB * C // 16) ** (-0.5),
        0.5 * COND ** (-0.5),
        0.5 * C ** (-0.5),
        0.5 * (C // 4) ** (-0.5),
        0.1,
    ]


def adam(weight, grad, first, second, rate):
    first = BETA_ONE * first + (1.0 - BETA_ONE) * grad
    second = BETA_TWO * second + (1.0 - BETA_TWO) * grad * grad
    update = (
        first
        / (1.0 - BETA_ONE**STEP_NO)
        / (jnp.sqrt(second / (1.0 - BETA_TWO**STEP_NO)) + ADAM_EPS)
    )
    return (weight - rate * (update + DECAY * weight), first, second)


def strips(
    frames,
    valid,
    flags,
    actions,
    states,
    latent,
    w_enc,
    w_lstm,
    w_fc,
    w_cond,
    w_deconv,
    w_mask,
    vector,
    m_enc,
    m_lstm,
    m_fc,
    m_cond,
    m_deconv,
    m_mask,
    m_vector,
    v_enc,
    v_lstm,
    v_fc,
    v_cond,
    v_deconv,
    v_mask,
    v_vector,
):
    clips = frames.shape[0]
    out_rows = frames.shape[3] // 2
    out_cols = frames.shape[4] // 2
    b_enc, g_enc, s_enc, b_lstm, b_fc, b_dec, b_mask = split_vector(vector)
    k_enc = w_enc.astype(jnp.bfloat16)
    k_lstm = w_lstm.astype(jnp.bfloat16)
    k_fc = w_fc.astype(jnp.bfloat16)
    k_dec = w_deconv.astype(jnp.bfloat16)
    images = jnp.transpose(frames, (1, 0, 3, 4, 2))
    padded = padded_2(images, (("row", 2),), 2)
    padded = jnp.pad(padded, ((0, 0), (0, 0), (0, 0), (2, 2), (0, 0)))
    valid_steps = jnp.transpose(valid.astype(jnp.float32), (1, 0, 2, 3))
    presence = flags.astype(jnp.float32)
    conditions = jnp.concatenate(
        [
            actions * presence[..., :1],
            states * presence[..., 1:],
            jnp.broadcast_to(latent[:, None, :], (clips, actions.shape[1], latent.shape[1])),
        ],
        -1,
    )
    conditions = jnp.transpose(conditions, (1, 0, 2))
    valid_count = lax.psum(jnp.sum(valid_steps), ("clip", "row"))
    inv_count = 1.0 / valid_count

    def advance(carry, image_pad):
        hidden, cell = carry
        pre = product(patches(image_pad, 2, out_rows, out_cols), k_enc, "byxk,kc->byxc") + b_enc
        encoded = norm_act(pre, g_enc, s_enc).astype(jnp.bfloat16)
        joined = jnp.concatenate([encoded, hidden], -1)
        joined_pad = padded_2(joined, (("row", 1),), 2)
        joined_pad = jnp.pad(joined_pad, ((0, 0), (0, 0), (2, 2), (0, 0)))
        gates = (
            product(patches(joined_pad, 1, out_rows, out_cols), k_lstm, "byxk,kg->byxg") + b_lstm
        )
        new_hidden, new_cell = cell_step(gates, cell)
        hidden_low = new_hidden.astype(jnp.bfloat16)
        part = product(hidden_low.reshape(clips, out_rows, -1), k_fc, "bjk,jnk->bn")
        part = lax.psum(part, "row")
        upper = product(hidden_low, k_dec, "byxc,cd->byxd")
        return ((hidden_low, new_cell), (pre, joined_pad, gates, cell, hidden_low, part, upper))

    start = (
        jnp.zeros((clips, out_rows, out_cols, C), jnp.bfloat16),
        jnp.zeros((clips, out_rows, out_cols, C), jnp.float32),
    )
    _, saved = lax.scan(advance, start, padded[:-1])
    pre_all, joined_all, gates_all, cells_all, hidden_all, summed_all, uppers = saved
    targets = images[1:].astype(jnp.float32)

    def local_head(item):
        summed_t, upper_t, image_pad, target, mask, cond = item

        def error_of(summed_t, upper_t, w_cond, w_mask, b_fc, b_dec, b_mask):
            logits = summed_t + jnp.dot(cond, w_cond, precision=HIGH) + b_fc
            upper_full = upsample(upper_t) + b_dec
            result = predict(logits, upper_full, w_mask, b_mask, image_pad.astype(jnp.float32))
            return jnp.sum(mask * jnp.sum((result - target) ** 2, -1))

        error, pullback = jax.vjp(error_of, summed_t, upper_t, w_cond, w_mask, b_fc, b_dec, b_mask)
        return (error, pullback(inv_count))

    head_inputs = (summed_all, uppers, padded[:-1], targets, valid_steps, conditions)

    def retreat(carry, item):
        (
            back_hidden,
            back_cell,
            acc_enc,
            acc_lstm,
            acc_dec,
            acc_benc,
            acc_genc,
            acc_senc,
            acc_blstm,
        ) = carry
        saved_t, head_t = item
        pre, joined_pad, gates, cell_prev, hidden_low, image_pad = saved_t
        error, pulled_t = local_head(head_t)
        d_sum = lax.psum(pulled_t[0], "row")
        d_upper = pulled_t[1]
        extra = (error, pulled_t[2:])
        d_sum_low = d_sum.astype(jnp.bfloat16)
        d_upper_low = d_upper.astype(jnp.bfloat16)
        acc_dec = acc_dec + product(hidden_low, d_upper_low, "byxc,byxd->cd")
        back = back_hidden + product(d_upper_low, k_dec, "byxd,cd->byxc")
        back = back + product(d_sum_low, k_fc, "bn,jnk->bjk").reshape(back_hidden.shape)
        _, cell_pull = jax.vjp(cell_step, gates, cell_prev)
        d_gates, back_cell = cell_pull((back, back_cell))
        d_gates_low = d_gates.astype(jnp.bfloat16)
        acc_blstm = acc_blstm + jnp.sum(d_gates, (0, 1, 2))
        acc_lstm = acc_lstm + product(
            patches(joined_pad, 1, out_rows, out_cols), d_gates_low, "byxk,byxg->kg"
        )
        d_pad = unpatch(product(d_gates_low, k_lstm, "byxg,kg->byxk"), joined_pad.shape, 1)[
            :, :, 2:-2, :
        ]
        from_below = passed_along(d_pad[:, :2], "row", -1)
        from_above = passed_along(d_pad[:, -2:], "row", 1)
        d_joined = d_pad[:, 2:-2].at[:, -2:].add(from_below).at[:, :2].add(from_above)
        _, norm_pull = jax.vjp(norm_act, pre, g_enc, s_enc)
        d_pre, d_gain, d_shift = norm_pull(d_joined[..., :C])
        acc_benc = acc_benc + jnp.sum(d_pre, (0, 1, 2))
        acc_genc = acc_genc + d_gain
        acc_senc = acc_senc + d_shift
        acc_enc = acc_enc + product(
            patches(image_pad, 2, out_rows, out_cols), d_pre.astype(jnp.bfloat16), "byxk,byxc->kc"
        )
        new_carry = (
            d_joined[..., C:],
            back_cell,
            acc_enc,
            acc_lstm,
            acc_dec,
            acc_benc,
            acc_genc,
            acc_senc,
            acc_blstm,
        )
        return (new_carry, (d_sum_low, extra))

    zeros_state = jnp.zeros((clips, out_rows, out_cols, C), jnp.float32)
    zeros_small = jnp.zeros((C,), jnp.float32)
    init = (
        zeros_state,
        zeros_state,
        jnp.zeros(w_enc.shape, jnp.float32),
        jnp.zeros(w_lstm.shape, jnp.float32),
        jnp.zeros(w_deconv.shape, jnp.float32),
        zeros_small,
        zeros_small,
        zeros_small,
        jnp.zeros((4 * C,), jnp.float32),
    )
    final, (d_sums_low, extra) = lax.scan(
        retreat,
        init,
        ((pre_all, joined_all, gates_all, cells_all, hidden_all, padded[:-1]), head_inputs),
        reverse=True,
    )
    error_sum = jnp.sum(extra[0])
    head_sums = [jnp.sum(grad, 0) for grad in extra[1]]
    acc_enc, acc_lstm, acc_dec, acc_benc, acc_genc, acc_senc, acc_blstm = final[2:]
    flat_hidden = hidden_all.reshape(hidden_all.shape[0], clips, out_rows, -1)
    d_fc = lax.psum(
        product(flat_hidden, d_sums_low, "tbjk,tbn->jnk").astype(jnp.bfloat16), "clip"
    ).astype(jnp.float32)
    fc_squares = jnp.sum(d_fc * d_fc) / lax.axis_size("clip")
    d_vector = jnp.concatenate(
        [acc_benc, acc_genc, acc_senc, acc_blstm, head_sums[2], head_sums[3], head_sums[4]]
    )
    d_enc, d_lstm, d_cond, d_dec, d_mask, d_vector, loss_sum, squares = lax.psum(
        (acc_enc, acc_lstm, head_sums[0], acc_dec, head_sums[1], d_vector, error_sum, fc_squares),
        ("clip", "row"),
    )
    grads = (d_enc, d_lstm, d_fc, d_cond, d_dec, d_mask, d_vector)
    for index in (0, 1, 3, 4, 5, 6):
        squares = squares + jnp.sum(grads[index] * grads[index])
    grad_norm = jnp.sqrt(squares)
    factor = CLIP_NORM / jnp.maximum(grad_norm, CLIP_NORM)
    rates = learning_rates(w_fc.shape[0] * lax.axis_size("row"))
    weights = (w_enc, w_lstm, w_fc, w_cond, w_deconv, w_mask, vector)
    firsts = (m_enc, m_lstm, m_fc, m_cond, m_deconv, m_mask, m_vector)
    seconds = (v_enc, v_lstm, v_fc, v_cond, v_deconv, v_mask, v_vector)
    new = [
        adam(weights[index], grads[index] * factor, firsts[index], seconds[index], rates[index])
        for index in range(7)
    ]
    return (
        loss_sum,
        valid_count,
        grad_norm,
        new[0][0],
        new[1][0],
        new[2][0],
        new[3][0],
        new[4][0],
        new[5][0],
        new[6][0],
        new[0][1],
        new[1][1],
        new[2][1],
        new[3][1],
        new[4][1],
        new[5][1],
        new[6][1],
        new[0][2],
        new[1][2],
        new[2][2],
        new[3][2],
        new[4][2],
        new[5][2],
        new[6][2],
    )


LANES = 128
TILES = 4
BANDS = 4
HALVES = 2
FAR = 1
WIN = 9 * 16
BF = jnp.bfloat16
F32 = jnp.float32
VMEM_BYTES = 56 * 1024 * 1024


def window_places():
    places = np.zeros((4, WIN, 32), np.float32)
    encoder = np.zeros((WIN, KK * 3), np.float32)
    for sub in range(4):
        for tap in range(KK):
            off_y = tap // KS - 2 + sub // 2
            off_x = tap % KS - 2 + sub % 2
            block = (off_y // 2 + 1) * 3 + off_x // 2 + 1
            base = block * 16 + (off_x % 2) * 8 + (off_y % 2) * 4
            for channel in range(3):
                places[sub, base + channel, tap] = 1.0
                if sub == 0:
                    encoder[base + channel, tap * 3 + channel] = 1.0
    return places, encoder


def lane_places():
    lane = lax.broadcasted_iota(jnp.int32, (8, LANES), 1)
    return lane % WB, lane // WB


def moved(tile, lanes, d_col, d_band):
    if d_col == 0 and d_band == 0:
        return tile
    col, band = lanes
    rows = tile.shape[0]
    shift = (-(WB * d_band + d_col)) % LANES
    rolled = pltpu.roll(tile.reshape(rows // 8, 8, LANES), shift, 2)
    keep = None
    for place, delta, count in ((col, d_col, WB), (band, d_band, BANDS)):
        if delta > 0:
            inside = place < count - delta
        elif delta < 0:
            inside = place >= -delta
        else:
            continue
        keep = inside if keep is None else keep & inside
    return jnp.where(keep[None], rolled, 0.0).reshape(rows, LANES)


def spread(tiles, lanes, reach, target, width, start):
    rows = tiles[0].shape[0]
    for index in range(TILES + 2 * reach):
        tile = index - reach
        for shift in range(2 * reach + 1):
            place = shift * width + start
            target[index, place : place + rows, :] = moved(
                tiles[tile % TILES], lanes, shift - reach, tile // TILES
            ).astype(target.dtype)


def stacked(ref, tile, count):
    rows = count * ref.shape[1]
    return jnp.concatenate(
        [ref[tile : tile + count].reshape(rows, LANES), ref[tile + 1 : tile + 1 + count].reshape(rows, LANES)],
        axis=1,
    )


def nn(left, right):
    return lax.dot_general(left, right, (((1,), (0,)), ((), ())), preferred_element_type=F32)


def nt(left, right):
    return lax.dot_general(left, right, (((1,), (1,)), ((), ())), preferred_element_type=F32)


def nn_exact(left, right):
    return lax.dot_general(left, right, (((1,), (0,)), ((), ())), preferred_element_type=F32, precision=HIGH)


def nt_exact(left, right):
    return lax.dot_general(left, right, (((1,), (1,)), ((), ())), preferred_element_type=F32, precision=HIGH)


def logistic(v):
    return 0.5 * jnp.tanh(0.5 * v) + 0.5


def one_hot_eye(size):
    row = lax.broadcasted_iota(jnp.int32, (size, size), 0)
    return (row == lax.broadcasted_iota(jnp.int32, (size, size), 1)).astype(BF)


def split(value):
    high = value.astype(BF)
    return high, (value - high.astype(F32)).astype(BF)


def one_hot_mod(shape, period, axis):
    folded = lax.broadcasted_iota(jnp.int32, shape, axis) % period
    return (folded == lax.broadcasted_iota(jnp.int32, shape, 1 - axis)).astype(BF)


def unpack_images(raw_ref, x_ref):
    source = lax.broadcasted_iota(jnp.int32, (LANES, 4 * LANES), 0)
    goal = lax.broadcasted_iota(jnp.int32, (LANES, 4 * LANES), 1)
    same = (source // 64 == goal // 256) & (source % 2 == goal // LANES % 2) & (source // 2 % WB == goal % WB)
    picks = [(same & (goal // WB % BANDS == band)).astype(BF) for band in range(BANDS)]
    for pair in range(2):
        total = nn(raw_ref[pair], picks[0])
        for band in range(1, BANDS):
            total = total + nn(raw_ref[2 * band + pair], picks[band])
        for t in range(x_ref.shape[0]):
            rows = total[8 * t : 8 * t + 8]
            for low_row in range(2):
                start = 2 * LANES * low_row
                x_ref[t, 2 * pair + low_row] = jnp.concatenate(
                    [rows[:, start : start + LANES], rows[:, start + LANES : start + 2 * LANES]], axis=0
                ).astype(BF)


def image_tiles(x_ref, t):
    return [x_ref[t, tile].astype(F32) for tile in range(TILES)]


def block_swap(parts, band):
    swapped = []
    for out in range(BANDS):
        total = None
        for part in range(BANDS):
            shift = (WB * (part - out)) % LANES
            value = parts[part] if shift == 0 else pltpu.roll(parts[part], shift, 1)
            total = value if total is None else jnp.where(band == part, value, total)
        swapped.append(total)
    return swapped


def wide(tile):
    return jnp.concatenate([tile] * TILES, axis=1)


def folded(values):
    total = values[:, :LANES]
    for tile in range(1, values.shape[1] // LANES):
        total = total + values[:, tile * LANES : (tile + 1) * LANES]
    return total


def twice(tile):
    return jnp.concatenate([tile, tile], axis=1)


def forward_kernel(
    half_ref, raw_ref, we_ref, w_ref, bias_ref,
    x_ref, enc_ref, hid_ref, far_act_ref, far_cell_ref, strip_ref,
    win_s, enc_s, hid_s, state_s, rows_s, wx_s, wh_s, even_s, odd_s, act_ref, cell_ref, sems,
):
    steps = hid_ref.shape[0]
    lanes = lane_places()
    for kind, target in ((0, wx_s), (1, wh_s)):
        for tap in range(KK):
            start = tap * 2 * C + kind * C
            rows_s[tap * C : (tap + 1) * C, :] = w_ref[start : start + C, :].astype(BF)
        target[...] = nt(one_hot_eye(4 * C), rows_s[...]).astype(BF)
    unpack_images(raw_ref, x_ref)

    def encode(t, gates_s):
        spread(image_tiles(x_ref, t), lanes, 1, win_s, 16, 0)
        tiles = []
        for two in range(0, TILES, 2):
            pre = nn(we_ref[...], stacked(win_s, two, 3)) + twice(bias_ref[0:C])
            centered = pre - jnp.mean(pre, 0, keepdims=True)
            scale = lax.rsqrt(jnp.mean(centered * centered, 0, keepdims=True) + NORM_EPS)
            value = centered * scale * twice(bias_ref[C : 2 * C]) + twice(bias_ref[2 * C : 3 * C])
            value = (value * logistic(value)).astype(BF)
            for one in range(2):
                part = value[:, one * LANES : (one + 1) * LANES]
                enc_ref[t, two + one] = part
                tiles.append(part.astype(F32))
        spread(tiles, lanes, 2, enc_s, C, 0)
        for two in range(0, TILES, 2):
            gates = nn(wx_s[...], stacked(enc_s, two, KS)) + twice(bias_ref[3 * C : 7 * C])
            for one in range(2):
                gates_s[two + one] = gates[:, one * LANES : (one + 1) * LANES]

    hid_s[...] = jnp.zeros_like(hid_s)
    state_s[...] = jnp.zeros_like(state_s)

    def advance(t, gates_s, later_s):
        sums = [nn(wh_s[...], stacked(hid_s, two, KS)) for two in range(0, TILES, 2)]
        encode(t + 1, later_s)
        hidden = []
        for tile in range(TILES):
            start = tile % 2 * LANES
            gates = gates_s[tile] + sums[tile // 2][:, start : start + LANES]
            gate_in = logistic(gates[0:C])
            gate_keep = logistic(gates[C : 2 * C] + 1.0)
            gate_out = logistic(gates[2 * C : 3 * C])
            gate_new = jnp.tanh(gates[3 * C : 4 * C])
            cell = gate_keep * state_s[tile] + gate_in * gate_new
            act_ref[t, tile, 0:C] = gate_in
            act_ref[t, tile, C : 2 * C] = gate_keep
            act_ref[t, tile, 2 * C : 3 * C] = gate_out
            act_ref[t, tile, 3 * C : 4 * C] = gate_new
            state_s[tile] = cell
            cell_ref[t, tile] = cell
            low = (gate_out * jnp.tanh(cell)).astype(BF)
            hid_ref[t, tile] = low
            hidden.append(low.astype(F32))
        spread(hidden, lanes, 2, hid_s, C, 0)

    def out_copies(t):
        return [
            pltpu.make_async_copy(act_ref.at[t], far_act_ref.at[t], sems.at[0, t]),
            pltpu.make_async_copy(cell_ref.at[t], far_cell_ref.at[t], sems.at[1, t]),
        ]

    encode(0, even_s)

    def advance_two(pair, _):
        for one, slots in enumerate(((even_s, odd_s), (odd_s, even_s))):
            advance(2 * pair + one, *slots)
        for one in range(2):
            for copy in out_copies(2 * pair + one):
                copy.start()
        return 0

    lax.fori_loop(0, steps // 2, advance_two, 0)
    own = steps // HALVES
    base = half_ref[0] * own

    def to_strips(i, _):
        for pair in range(2):
            rows = []
            for low_row in range(2):
                tile = hid_ref[base + i, 2 * pair + low_row].astype(F32)
                rows.append(block_swap([tile[8 * q : 8 * q + 8] for q in range(4)], lanes[1]))
            for band in range(BANDS):
                strip_ref[2 * band + pair, i] = jnp.concatenate(
                    [rows[0][band], rows[1][band]], axis=0
                ).astype(BF)
        return 0

    lax.fori_loop(0, own, to_strips, 0)
    for t in range(steps):
        for copy in out_copies(t):
            copy.wait()


def head_kernel(
    half_ref, x_ref, hid_ref, logit_ref, w_ref, mask_ref, bias_ref, place_ref, placet_ref, cond_ref,
    back_ref, dlog_ref, dwd_ref, dwm_ref, sums_ref, copies_ref, dcond_ref,
    even_s, odd_s, wd_ref, wdt_ref, wm_ref, wmt_ref, over_ref, wide_s, everywhere_s, turned_s, d_even_s, d_odd_s,
    d_spot_s, kernel_s, d_logit_s,
):
    wd_ref[...] = w_ref[...].astype(BF)
    wdt_ref[...] = nt(one_hot_eye(4 * C), wd_ref[...]).astype(BF)
    row = lax.broadcasted_iota(jnp.int32, (4 * C, 64), 0)
    mine_t = row // C == lax.broadcasted_iota(jnp.int32, (4 * C, 64), 1) // 16
    row = lax.broadcasted_iota(jnp.int32, (64, 4 * C), 0)
    mine = row // 16 == lax.broadcasted_iota(jnp.int32, (64, 4 * C), 1) // C
    for kind, part in enumerate(split(mask_ref[...])):
        spread_mask = nt(one_hot_mod((4 * C, C), C, 0), part).astype(BF)
        wide_t = jnp.where(mine_t, nn(spread_mask, one_hot_mod((NM, 64), 16, 1)), 0.0).astype(BF)
        wide_m = jnp.where(mine, nt(one_hot_mod((64, NM), 16, 0), spread_mask), 0.0).astype(BF)
        wmt_ref[:, kind * 64 : kind * 64 + 64] = wide_t
        wm_ref[:, kind * 4 * C : (kind + 1) * 4 * C] = wide_m
        if kind == 0:
            wmt_ref[:, 128:192] = wide_t
            wm_ref[:, 8 * C : 12 * C] = wide_m
    for sub in range(4):
        over_ref[sub * C : (sub + 1) * C, :] = bias_ref[7 * C : 8 * C]
        over_ref[4 * C + sub * 16 : 4 * C + (sub + 1) * 16, :] = bias_ref[8 * C : 8 * C + 16]
    own = logit_ref.shape[0]
    base = half_ref[0] * own
    lanes = lane_places()
    dwd_ref[...] = jnp.zeros_like(dwd_ref)
    wide_s[...] = jnp.zeros_like(wide_s)
    sums_ref[...] = jnp.zeros_like(sums_ref)
    cells = TILES * LANES
    row8 = lax.broadcasted_iota(jnp.int32, (8, cells), 0)
    color = (row8 % 4) != 3
    row16 = lax.broadcasted_iota(jnp.int32, (16, 32), 0)
    lane16 = lax.broadcasted_iota(jnp.int32, (16, 32), 1)

    for sub in range(4):
        everywhere_s[sub * WIN : (sub + 1) * WIN] = place_ref[sub]
        turned_s[:, sub * WIN : (sub + 1) * WIN] = placet_ref[sub]
    row = lax.broadcasted_iota(jnp.int32, (4 * WIN, 64), 0) // WIN
    own_spots = row == lax.broadcasted_iota(jnp.int32, (4 * WIN, 64), 1) // 16
    row = lax.broadcasted_iota(jnp.int32, (64, 4 * WIN), 0) // 16
    own_turned = row == lax.broadcasted_iota(jnp.int32, (64, 4 * WIN), 1) // WIN

    def frame(i, win_s, d_mix_s):
        t = base + i
        spread(image_tiles(x_ref, t), lanes, 1, win_s, 16, 0)
        window = jnp.concatenate([win_s[tile : tile + 3].reshape(WIN, LANES) for tile in range(TILES)], axis=1)
        window = window.reshape(18, 8, cells)
        logits = logit_ref[i]
        powers = jnp.exp(logits - jnp.max(logits, -1, keepdims=True))
        kernels = powers / jnp.sum(powers, -1, keepdims=True)
        kernels = jnp.where(row16 == 0, (lane16 == KK // 2).astype(F32), jnp.where(row16 <= NK, kernels, 0.0))
        kernel_s[i] = kernels
        spots = []
        turned = []
        for part in split(kernels):
            part = jnp.concatenate([part, part, part, part], axis=0)
            spots.append(jnp.where(own_spots, nt(everywhere_s[...], part), 0.0).astype(BF))
            turned.append(jnp.where(own_turned, nn(part, turned_s[...]), 0.0).astype(BF))
        spots = jnp.concatenate([spots[0], spots[1], spots[0]], axis=1)
        turned = jnp.concatenate(turned, axis=0)
        hidden = jnp.concatenate([hid_ref[t, tile] for tile in range(TILES)], axis=1)
        upper = nn(wdt_ref[...], hidden) + wide(over_ref[0 : 4 * C])
        gate = logistic(upper)
        active, active_rest = split(upper * gate)
        scores = nn(wm_ref[...], jnp.concatenate([active, active, active_rest], axis=0)) + wide(over_ref[4 * C : 4 * C + 64])
        scores = scores.reshape(4, 16, cells)
        powers = jnp.exp(scores - jnp.max(scores, 1, keepdims=True))
        masks = powers / jnp.sum(powers, 1, keepdims=True)
        mask_low, mask_rest = split(masks.reshape(64, cells))
        mixing = nn(spots, jnp.concatenate([mask_low, mask_low, mask_rest], axis=0)).reshape(4, 18, 8, cells)
        after = jnp.concatenate([x_ref[t + 1, tile] for tile in range(TILES)], axis=1).astype(F32)
        lost = None
        for sub in range(4):
            both = jnp.sum(mixing[sub] * window, 0)
            result = both + pltpu.roll(both, 4, 0)
            goal = after[(sub % 2) * 8 : (sub % 2) * 8 + 8]
            goal = jnp.where((row8 < 4) == (sub // 2 == 0), goal, pltpu.roll(goal, 4, 0))
            diff = jnp.where(color, result - goal, 0.0)
            weighted = diff * goal[3:4]
            part = jnp.where(row8 == 3, goal[3:4], weighted * diff)
            lost = part if lost is None else lost + part
            d_result = 2.0 * weighted
            d_mix_s[sub * WIN : (sub + 1) * WIN] = (window * d_result[None]).reshape(WIN, cells).astype(BF)
        sums_ref[192:200] += folded(lost)
        d_mask = nn(turned, d_mix_s[...])
        d_mask = (d_mask[:64] + d_mask[64:]).reshape(4, 16, cells)
        d_spot_s[i] = nt(mask_low, d_mix_s[...])
        inner = jnp.sum(masks * d_mask, 1, keepdims=True)
        d_score = (masks * (d_mask - inner)).reshape(64, cells)
        sums_ref[128:192] += folded(d_score)
        d_score_low, d_score_rest = split(d_score)
        d_active = nn(wmt_ref[...], jnp.concatenate([d_score_low, d_score_low, d_score_rest], axis=0))
        wide_s[...] += nt(d_score_low, active)
        d_upper = d_active * (gate * (1.0 + upper * (1.0 - gate)))
        sums_ref[0:128] += folded(d_upper)
        d_upper_low = d_upper.astype(BF)
        dwd_ref[...] += nt(hidden, d_upper_low)
        back = nn(wd_ref[...], d_upper_low).astype(BF)
        for tile in range(TILES):
            back_ref[i, tile] = back[:, tile * LANES : (tile + 1) * LANES]

    def two_frames(pair, _):
        frame(2 * pair, even_s, d_even_s)
        frame(2 * pair + 1, odd_s, d_odd_s)
        return 0

    lax.fori_loop(0, own // 2, two_frames, 0)
    d_kernels = None
    for sub in range(4):
        rows = jnp.concatenate([d_spot_s[i, sub * 16 : sub * 16 + 16] for i in range(own)], axis=0)
        place = lax.broadcasted_iota(jnp.int32, rows.shape, 1) // WIN
        part = nn_exact(jnp.where(place == sub, rows, 0.0), everywhere_s[...].astype(F32))
        d_kernels = part if d_kernels is None else d_kernels + part
    for i in range(own):
        kernels = kernel_s[i]
        d_one = d_kernels[16 * i : 16 * i + 16]
        inner = jnp.sum(d_one * kernels, -1, keepdims=True)
        d_logit_s[16 * i : 16 * i + 16] = kernels * (d_one - inner)
    total = jnp.zeros(dlog_ref.shape, F32)
    tap = lax.broadcasted_iota(jnp.int32, (32, 2 * LANES), 0)
    lane = lax.broadcasted_iota(jnp.int32, (32, 2 * LANES), 1)
    for kernel in range(NK):
        place = ((tap < KK) & (lane == kernel * KK + tap)).astype(F32)
        total = total + nn_exact(d_logit_s[pl.ds(kernel + 1, own, stride=16), :], place)
    dlog_ref[...] = total
    low = total.astype(BF)
    for device in range(copies_ref.shape[0]):
        copies_ref[device] = low
    d_cond = nn_exact(cond_ref[...], total)
    dcond_ref[0:16] = d_cond[:, :LANES]
    dcond_ref[16:32] = d_cond[:, LANES:]
    row = lax.broadcasted_iota(jnp.int32, (64, 4 * C), 0)
    lane = lax.broadcasted_iota(jnp.int32, (64, 4 * C), 1)
    own_block = jnp.where(row // 16 == lane // C, wide_s[...], 0.0)
    fold = lax.broadcasted_iota(jnp.int32, (4 * C, LANES), 0) % C
    fold = (fold == lax.broadcasted_iota(jnp.int32, (4 * C, LANES), 1)).astype(F32)
    dwm_ref[...] = jnp.sum(nn_exact(own_block, fold).reshape(4, 16, LANES), 0)


def backward_kernel(
    half_ref, far_act_ref, far_cell_ref, dec_ref, other_dec_ref, fc_ref, other_fc_ref, w_ref,
    keep_ref, denc_ref, lines_ref,
    gate_s, back_s, state_s, wb_s, even_s, odd_s, act_ref, cell_ref, sems,
):
    steps = far_act_ref.shape[0]

    def act_copy(t):
        return pltpu.make_async_copy(far_act_ref.at[t], act_ref.at[t], sems.at[0, t])

    def cell_copy(t):
        return pltpu.make_async_copy(far_cell_ref.at[t], cell_ref.at[t], sems.at[1, t])

    for t in reversed(range(steps)):
        act_copy(t).start()
        cell_copy(t).start()
    for tap in range(KK):
        place = tap % KS * 2 * C
        turn = (KS - 1 - tap // KS) * 4 * C
        wb_s[place : place + 2 * C, turn : turn + 4 * C] = w_ref[tap * 2 * C : (tap + 1) * 2 * C, :].astype(BF)
    own = steps // HALVES
    lanes = lane_places()
    back_s[...] = jnp.zeros_like(back_s)
    state_s[...] = jnp.zeros_like(state_s)
    lines_ref[...] = jnp.zeros_like(lines_ref)

    def prepare(t, factor_s):
        half = t // own
        inside = t % own
        mine = half == half_ref[0]
        earlier = jnp.maximum(t - 1, 0)
        started = jnp.where(t > 0, 1.0, 0.0)
        for tile in range(TILES):
            pair = tile // 2
            low_row = tile % 2
            parts = [
                jnp.where(
                    mine, fc_ref[2 * band + pair, inside].astype(F32), other_fc_ref[2 * band + pair, inside].astype(F32)
                )[8 * low_row : 8 * low_row + 8]
                for band in range(BANDS)
            ]
            from_fc = jnp.concatenate(block_swap(parts, lanes[1]), axis=0)
            from_dec = jnp.where(
                mine, dec_ref[inside, tile].astype(F32), other_dec_ref[inside, tile].astype(F32)
            )
            gate_in = act_ref[t, tile, 0:C]
            gate_keep = act_ref[t, tile, C : 2 * C]
            gate_out = act_ref[t, tile, 2 * C : 3 * C]
            gate_new = act_ref[t, tile, 3 * C : 4 * C]
            bent = jnp.tanh(cell_ref[t, tile])
            factors = [
                from_fc + from_dec,
                gate_out * (1.0 - bent * bent),
                gate_keep,
                gate_new * gate_in * (1.0 - gate_in),
                (cell_ref[earlier, tile] * started) * gate_keep * (1.0 - gate_keep),
                bent * gate_out * (1.0 - gate_out),
                gate_in * (1.0 - gate_new * gate_new),
            ]
            for index, factor in enumerate(factors):
                factor_s[tile, index * C : (index + 1) * C] = factor

    def retreat(t, factor_s, next_s):
        half = t // own
        inside = t % own
        counted = jnp.where(half == half_ref[0], 1.0, 0.0)
        place = jnp.where(half == half_ref[0], inside, own)
        tiles = []
        for tile in range(TILES):
            back = back_s[tile] + factor_s[tile, 0:C]
            d_cell = state_s[tile] + back * factor_s[tile, C : 2 * C]
            state_s[tile] = d_cell * factor_s[tile, 2 * C : 3 * C]
            d_gates = jnp.concatenate(
                [
                    d_cell * factor_s[tile, 3 * C : 4 * C],
                    d_cell * factor_s[tile, 4 * C : 5 * C],
                    back * factor_s[tile, 5 * C : 6 * C],
                    d_cell * factor_s[tile, 6 * C : 7 * C],
                ],
                axis=0,
            )
            lines_ref[...] += d_gates * counted
            low = d_gates.astype(BF)
            keep_ref[place, tile] = low
            tiles.append(low.astype(F32))
        for index in range(TILES + 4):
            tile = index - 2
            gate_s[index] = moved(tiles[tile % TILES], lanes, 0, tile // TILES).astype(BF)
        prepare(jnp.maximum(t - 1, 0), next_s)
        for two in range(0, TILES, 2):
            sums = nn(wb_s[...], stacked(gate_s, two, KS))
            for one in range(2):
                part = sums[:, one * LANES : (one + 1) * LANES]
                total = None
                for shift in range(KS):
                    value = moved(part[shift * 2 * C : (shift + 1) * 2 * C], lanes, 2 - shift, 0)
                    total = value if total is None else total + value
                denc_ref[place, two + one] = total[:C]
                back_s[two + one] = total[C:]

    cell_copy(steps - 1).wait()
    act_copy(steps - 1).wait()
    cell_copy(steps - 2).wait()
    prepare(steps - 1, even_s)

    def retreat_two(pair, _):
        t = steps - 1 - 2 * pair
        act_copy(t - 1).wait()

        @pl.when(pair < steps // 2 - 1)
        def _():
            act_copy(t - 2).wait()
            cell_copy(t - 2).wait()
            cell_copy(t - 3).wait()

        retreat(t, even_s, odd_s)
        retreat(t - 1, odd_s, even_s)
        return 0

    lax.fori_loop(0, steps // 2, retreat_two, 0)


ROW_DEC = KK * 2 * C
ROW_COND = ROW_DEC + C
ROW_ENC = ROW_COND + 32
ROW_MASK = ROW_ENC + C
ROW_VECTOR = ROW_MASK + 16
ROWS = ROW_VECTOR + 16
PART = 64
SMALL = ROWS - ROW_DEC


def vector_places():
    place = np.zeros((7 * C + 4 * C + 64, 5 * LANES), np.float32)
    for line in range(7 * C):
        place[line, line] = 1.0
    for line in range(4 * C):
        place[7 * C + line, 7 * C + NK * KK + line % C] = 1.0
    for line in range(64):
        if line % 16 < NM:
            place[11 * C + line, 8 * C + NK * KK + line % 16] = 1.0
    return place


def logit_map_gradient(clip_group, hid_ref, sum_ref, out_ref, turned_s):
    logits = NK * KK
    groups, items, width = sum_ref.shape
    eye = one_hot_eye(width)
    for group in range(groups):
        turned_s[:, group * items : (group + 1) * items] = nt(
            eye, sum_ref[lax.rem(clip_group + groups - group, groups)]
        ).astype(BF)
    squares = jnp.zeros((1, LANES), F32)
    stride = 2 * WB * C // LANES
    for row in range(2):
        for start in range(0, WB * C, 2 * LANES):
            hid = jnp.concatenate(
                [hid_ref[group, row, :, start : start + 2 * LANES] for group in range(groups)], axis=0
            )
            grad = nn(turned_s[...], hid)[:logits]
            for one in range(2):
                part = grad[:, one * LANES : (one + 1) * LANES]
                squares = squares + jnp.sum(part * part, 0, keepdims=True)
                out_ref[pl.ds((start // LANES + one) * 2 + row, logits, stride=stride), :] = part
    return jnp.sum(squares, 1, keepdims=True) * (1.0 / groups)


def pack_kernel(
    half_ref, x_ref, enc_ref, hid_ref, keep_ref, denc_ref, lines_ref, head_ref, ddec_ref, dmask_ref, dcond_ref,
    dline_ref, sum_ref, we_ref, bias_ref, place_ref, encoder_ref, *rest,
):
    groups = sum_ref.shape[0]
    far_hids = rest[:groups]
    (block_ref, far_dfc_ref, win_even_s, win_odd_s, join_even_s, join_odd_s, dwe_s, sums_s, packed_s, every_s,
     dfc_s, turned_s, sems) = rest[groups:]
    hid_copies = [
        pltpu.make_async_copy(far_hid, every_s.at[group], sems.at[1 + group]) for group, far_hid in enumerate(far_hids)
    ]
    for copy in hid_copies:
        copy.start()
    own = keep_ref.shape[0] - 1
    base = half_ref[0] * own
    lanes = lane_places()
    dwe_s[...] = jnp.zeros_like(dwe_s)
    sums_s[...] = jnp.zeros_like(sums_s)
    packed_s[...] = jnp.zeros_like(packed_s)

    def gather(i, win_s, join_s):
        t = base + i
        earlier = jnp.maximum(t - 1, 0)
        started = jnp.where(t > 0, 1.0, 0.0)
        spread([enc_ref[t, tile].astype(F32) for tile in range(TILES)], lanes, 2, join_s, 2 * C, 0)
        spread(
            [hid_ref[earlier, tile].astype(F32) * started for tile in range(TILES)], lanes, 2, join_s, 2 * C, C
        )
        d_gates = jnp.concatenate([keep_ref[i, tile] for tile in range(TILES)], axis=1)
        joined = jnp.concatenate([stacked(join_s, 0, KS), stacked(join_s, 2, KS)], axis=1)
        packed_s[0:ROW_DEC] += nt(joined, d_gates)
        spread(image_tiles(x_ref, t), lanes, 1, win_s, 16, 0)
        for two in range(0, TILES, 2):
            window = stacked(win_s, two, 3)
            pre = nn(we_ref[...], window) + twice(bias_ref[0:C])
            centered = pre - jnp.mean(pre, 0, keepdims=True)
            scale = lax.rsqrt(jnp.mean(centered * centered, 0, keepdims=True) + NORM_EPS)
            normal = centered * scale
            gain = twice(bias_ref[C : 2 * C])
            value = normal * gain + twice(bias_ref[2 * C : 3 * C])
            gate = logistic(value)
            d_out = jnp.concatenate([denc_ref[i, two], denc_ref[i, two + 1]], axis=1)
            d_value = d_out * (gate * (1.0 + value * (1.0 - gate)))
            d_gain = d_value * normal
            d_normal = d_value * gain
            d_pre = scale * (
                d_normal
                - jnp.mean(d_normal, 0, keepdims=True)
                - normal * jnp.mean(d_normal * normal, 0, keepdims=True)
            )
            sums_s[0:C] += d_pre[:, :LANES] + d_pre[:, LANES:]
            sums_s[C : 2 * C] += d_gain[:, :LANES] + d_gain[:, LANES:]
            sums_s[2 * C : 3 * C] += d_value[:, :LANES] + d_value[:, LANES:]
            dwe_s[...] += nt(d_pre.astype(BF), window)

    def gather_two(pair, _):
        gather(2 * pair, win_even_s, join_even_s)
        gather(2 * pair + 1, win_odd_s, join_odd_s)
        return 0

    lax.fori_loop(0, own // 2, gather_two, 0)
    for copy in hid_copies:
        copy.wait()
    squares = logit_map_gradient(half_ref[1], every_s, sum_ref, dfc_s, turned_s)
    dfc_copy = pltpu.make_async_copy(dfc_s, far_dfc_ref, sems.at[0])
    dfc_copy.start()
    packed_s[ROW_DEC:ROW_COND] = ddec_ref[...]
    packed_s[ROW_COND:ROW_ENC] = dcond_ref[...]
    packed_s[ROW_ENC:ROW_MASK] = nn_exact(dwe_s[...], encoder_ref[...])
    packed_s[ROW_MASK:ROW_VECTOR] = dmask_ref[...]
    ones = jnp.ones((8, LANES), F32)
    sums_s[3 * C : 7 * C] = lines_ref[...]
    sums_s[7 * C : 11 * C + 64] = head_ref[0:192]
    line = nn_exact(nt_exact(ones, sums_s[...]), place_ref[...].astype(F32))[0:1]
    logit_line = jnp.concatenate([dline_ref[...], jnp.zeros((dline_ref.shape[0], 3 * LANES), F32)], axis=1)
    line = line + pltpu.roll(jnp.sum(logit_line, 0, keepdims=True), 7 * C, 1)
    packed_s[ROW_VECTOR : ROW_VECTOR + 8] = jnp.concatenate(
        [line[:, place * LANES : (place + 1) * LANES] for place in range(5)] + [jnp.zeros((3, LANES), F32)], axis=0
    )
    lost = jnp.sum(jnp.sum(head_ref[192:195], 0, keepdims=True), 1, keepdims=True)
    counted = jnp.sum(head_ref[195:196], 1, keepdims=True)
    lane = lax.broadcasted_iota(jnp.int32, (1, LANES), 1)
    value = jnp.where(lane == 0, lost, jnp.where(lane == 1, counted, jnp.where(lane == 2, squares, 0.0)))
    terms = []
    for _ in range(3):
        low = value.astype(BF).astype(F32)
        terms.append(low)
        value = value - low
    devices = block_ref.shape[0]
    large = ROW_DEC // devices
    small = SMALL // devices
    fill = jnp.zeros((PART - large - 2 * small - 3, LANES), F32)
    for device in range(devices):
        value = packed_s[ROW_DEC + device * small : ROW_DEC + (device + 1) * small]
        high = value.astype(BF).astype(F32)
        rows = [packed_s[device * large : (device + 1) * large], high, value - high] + terms + [fill]
        block_ref[device] = jnp.concatenate(rows, axis=0).astype(BF)
    dfc_copy.wait()


def total_kernel(got_ref, out_ref, scalar_ref):
    devices, rows, _ = got_ref.shape
    total = got_ref[0].astype(F32)
    for device in range(1, devices):
        total = total + got_ref[device].astype(F32)
    large = ROW_DEC // devices
    small = SMALL // devices
    end = large + 2 * small
    scalar_ref[...] = total[end : end + 1] + total[end + 1 : end + 2] + total[end + 2 : end + 3]
    value = total[large : large + small] + total[large + small : end]
    high = value.astype(BF).astype(F32)
    low = jnp.concatenate([total[:large], high, value - high, total[end:]], axis=0).astype(BF)
    for device in range(devices):
        out_ref[device] = low


def update(weight, grad, factor, first, second, rate):
    first = BETA_ONE * first + (factor * (1.0 - BETA_ONE)) * grad
    second = BETA_TWO * second + (factor * factor * (1.0 - BETA_TWO)) * (grad * grad)
    root = (second * lax.rsqrt(second)) * (1.0 - BETA_TWO**STEP_NO) ** -0.5 + ADAM_EPS
    turned = pl.reciprocal(root, approx=True)
    turned = turned * (2.0 - root * turned)
    step = first * turned * (rate / (1.0 - BETA_ONE**STEP_NO))
    return (weight * (1.0 - rate * DECAY) - step, first, second)


def update_kernel(rates, got_ref, scalar_ref, dfc_ref, *refs):
    weights, firsts, seconds = refs[0:7], refs[7:14], refs[14:21]
    norm_ref = refs[21]
    news = refs[22:29], refs[29:36], refs[36:43]
    packed_s, fc_s, lstm_s, sems, fc_in_s, lstm_in_s, in_sems = refs[43:]
    ins = []
    plan = ((2, fc_in_s, 5), (1, lstm_in_s, 2))
    for index, scratch, chunks in plan:
        sources = [weights[index], firsts[index], seconds[index]] + ([dfc_ref] if index == 2 else [])
        chunk = sources[0].shape[0] // chunks
        for at in range(chunks):
            for kind, source in enumerate(sources):
                here = pl.ds(at * chunk, chunk)
                copy = pltpu.make_async_copy(source.at[here], scratch.at[kind, here], in_sems.at[len(ins)])
                copy.start()
                ins.append(copy)
    devices = got_ref.shape[0]
    large = ROW_DEC // devices
    small = SMALL // devices
    for device in range(devices):
        rows = got_ref[device].astype(F32)
        packed_s[device * large : (device + 1) * large] = rows[:large]
        packed_s[ROW_DEC + device * small : ROW_DEC + (device + 1) * small] = (
            rows[large : large + small] + rows[large + small : large + 2 * small]
        )

    def add_rows(block, total):
        rows = packed_s[pl.ds(pl.multiple_of(block * 32, 32), 32)]
        return total + jnp.sum((rows * rows).reshape(4, 8, LANES), 0)

    squares = lax.fori_loop(0, ROWS // 32, add_rows, jnp.zeros((8, LANES), F32))
    terms = scalar_ref[...]
    squares = jnp.sum(jnp.sum(squares, 0, keepdims=True), 1, keepdims=True) + terms[:, 2:3]
    inv_count = 1.0 / terms[:, 1:2]
    norm = jnp.sqrt(squares) * inv_count
    factor = inv_count * (CLIP_NORM / jnp.maximum(norm, CLIP_NORM))
    norm_ref[...] = jnp.sum(norm)

    copies = []
    for (index, scratch, chunks), outs in zip(plan, (fc_s, lstm_s)):
        rows = scratch.shape[1]
        chunk = rows // chunks
        wide = chunk // 2
        for at in range(chunks):
            for _ in range(scratch.shape[0]):
                ins.pop(0).wait()

            def block(i, _):
                here = pl.ds(pl.multiple_of(at * chunk + i * wide, 8), wide)
                grad = scratch[3, here] if index == 2 else packed_s[here]
                new = update(scratch[0, here], grad, factor, scratch[1, here], scratch[2, here], rates[index])
                for kind in range(3):
                    outs[kind, here] = new[kind]
                return 0

            lax.fori_loop(0, 2, block, 0)
            for kind in range(3):
                here = pl.ds(at * chunk, chunk)
                copy = pltpu.make_async_copy(outs.at[kind, here], news[kind][index].at[here], sems.at[len(copies)])
                copy.start()
                copies.append(copy)

    def step(index, grad):
        new = update(weights[index][...], grad, factor, firsts[index][...], seconds[index][...], rates[index])
        for kind in range(3):
            news[kind][index][...] = new[kind]

    step(0, packed_s[ROW_ENC:ROW_MASK, : KK * 3])
    cond = jnp.concatenate([packed_s[ROW_COND : ROW_COND + 16], packed_s[ROW_COND + 16 : ROW_COND + 32]], axis=1)
    step(3, cond[:COND, : NK * KK])
    step(4, packed_s[ROW_DEC:ROW_COND])
    step(5, packed_s[ROW_MASK : ROW_MASK + NM, 0:C])
    line = jnp.concatenate([packed_s[ROW_VECTOR + place : ROW_VECTOR + place + 1] for place in range(5)], axis=1)
    width = weights[6].shape[0]
    new = update(
        weights[6][...].reshape(1, width), line[:, :width], factor, firsts[6][...].reshape(1, width),
        seconds[6][...].reshape(1, width), rates[6],
    )
    for kind in range(3):
        news[kind][6][...] = new[kind].reshape(width)
    for copy in copies:
        copy.wait()


SMEM_SPEC = pl.BlockSpec(memory_space=pltpu.SMEM)
VMEM_SPEC = pl.BlockSpec(memory_space=pltpu.VMEM)


def cost(micros):
    return pl.CostEstimate(flops=int(micros * 8e8), bytes_accessed=1024, transcendentals=0)


ANY_SPEC = pl.BlockSpec(memory_space=pl.ANY)


def call(kernel, micros, outs, scratch, half, *operands, far_in=(), far_out=()):
    def specs(count, far):
        return [ANY_SPEC if index in far else VMEM_SPEC for index in range(count)]

    return pl.pallas_call(
        kernel,
        cost_estimate=cost(micros),
        out_shape=[jax.ShapeDtypeStruct(shape, kind) for shape, kind in outs],
        in_specs=[SMEM_SPEC] + specs(len(operands), far_in),
        out_specs=specs(len(outs), far_out),
        scratch_shapes=[
            pltpu.SemaphoreType.DMA(kind) if shape is None else pltpu.VMEM(shape, kind) for shape, kind in scratch
        ],
        compiler_params=pltpu.CompilerParams(vmem_limit_bytes=VMEM_BYTES),
    )(half, *operands)


def columns(values):
    return jnp.broadcast_to(values[:, None], (values.shape[0], LANES))


def exchange(block, axes):
    return lax.all_to_all(block, axes, 0, 0, tiled=True)


def to_all(block, axes):
    count = lax.axis_size(axes)
    return exchange(jnp.broadcast_to(block[None], (count,) + block.shape), axes)


def strip_order():
    sent = np.arange(WB * C)
    natural = sent % WB * C + sent // WB % 4 * 8 + sent // LANES
    order = np.zeros((WB * C, WB * C), np.float32)
    order[sent, natural] = 1.0
    return order


def whole_clips(
    frames, valid, flags, actions, states, latent,
    w_enc, w_lstm, w_fc, w_cond, w_deconv, w_mask, vector,
    m_enc, m_lstm, m_fc, m_cond, m_deconv, m_mask, m_vector,
    v_enc, v_lstm, v_fc, v_cond, v_deconv, v_mask, v_vector,
):
    clips, shots, _, strip_rows, width = frames.shape
    steps = shots - 1
    own = steps // HALVES
    count = lax.axis_size("row")
    place = lax.axis_index("row")
    clip = place // HALVES
    half = place % HALVES
    half_1 = half.reshape(1).astype(jnp.int32)
    b_enc, g_enc, s_enc, b_lstm, b_fc, b_dec, b_mask = split_vector(vector)
    places, encoder = window_places()
    flagged = jnp.pad(valid.astype(BF), ((0, 0), (1, 0), (0, 0), (0, 0)))
    pieces = jnp.concatenate([frames, flagged[:, :, None]], axis=2).reshape(clips, shots, 4, 2, 2, width)
    pieces = jnp.transpose(pieces, (0, 1, 4, 2, 3, 5)).reshape(clips, shots * 8, LANES)
    pieces = jnp.pad(pieces, ((0, 0), (0, 8), (0, 0)))
    raw = exchange(jnp.repeat(pieces, HALVES, axis=0), "row")

    wide_enc = jnp.einsum(
        "rk,ko->or", jnp.asarray(encoder, BF), w_enc.astype(BF), preferred_element_type=F32
    ).astype(BF)
    bias = columns(
        jnp.concatenate([vector[: 7 * C], b_dec, jnp.pad(b_mask, (0, 16 - NM), constant_values=-1e30)])
    )
    cells = (steps, TILES, C, LANES)
    x, enc, hid, act, cell, strips_out = call(
        forward_kernel,
        20,
        [
            ((shots, TILES, 16, LANES), BF), ((shots,) + cells[1:], BF), (cells, BF),
            ((steps, TILES, 4 * C, LANES), F32),
            (cells, F32), ((count, own, 16, LANES), BF),
        ],
        [
            ((6, 48, LANES), BF), ((8, KS * C, LANES), BF), ((8, KS * C, LANES), BF), ((TILES, C, LANES), F32),
            ((KK * C, LANES), BF), ((4 * C, KK * C), BF), ((4 * C, KK * C), BF),
            ((TILES, 4 * C, LANES), F32), ((TILES, 4 * C, LANES), F32),
            ((steps, TILES, 4 * C, LANES), F32), (cells, F32), (None, (2, steps)),
        ],
        half_1, raw, wide_enc, w_lstm, bias, far_out=(3, 4),
    )
    items = clips * steps
    order = jnp.asarray(strip_order(), BF)
    k_fc = jnp.pad(w_fc.astype(BF), ((0, 0), (0, 2 * LANES - NK * KK), (0, 0)))
    k_fc = jnp.einsum("jnl,kl->jnk", k_fc, order, preferred_element_type=F32).astype(BF)
    strip_hid = exchange(strips_out, "row").reshape(items, 2, WB * C)
    parts = jnp.einsum("mjk,jnk->mn", strip_hid, k_fc, preferred_element_type=F32)
    strip_hid = jnp.einsum("mjk,kl->jml", strip_hid, order, preferred_element_type=F32).astype(BF)
    summed = jnp.sum(exchange(parts.reshape(count, own, 2 * LANES), "row"), 0)[:, : NK * KK]
    presence = flags.astype(F32)
    conditions = jnp.concatenate(
        [
            actions * presence[..., :1],
            states * presence[..., 1:],
            jnp.broadcast_to(latent[:, None, :], (clips, steps, latent.shape[1])),
        ],
        -1,
    )
    cond = lax.dynamic_slice(conditions, (clip, half * own, 0), (1, own, COND))[0]
    logits = summed + (jnp.dot(cond, w_cond, precision=HIGH) + b_fc)
    logits = jnp.pad(
        logits.reshape(own, NK, KK), ((0, 0), (1, 5), (0, 32 - KK)), constant_values=-1e30
    )
    both = ("clip", "row")
    devices = lax.axis_size(both)
    dec, d_logit, d_dec, d_mask, head_sums, sent, d_cond = call(
        head_kernel,
        30,
        [
            ((own, TILES, C, LANES), BF), ((own, 2 * LANES), F32), ((C, 4 * C), F32), ((16, LANES), F32),
            ((200, LANES), F32), ((devices, own, 2 * LANES), BF), ((32, LANES), F32),
        ],
        [
            ((6, 48, LANES), F32), ((6, 48, LANES), F32), ((C, 4 * C), BF), ((4 * C, C), BF), ((64, 12 * C), BF),
            ((4 * C, 192), BF), ((4 * C + 64, LANES), F32), ((64, 4 * C), F32),
            ((4 * WIN, 32), BF), ((32, 4 * WIN), BF), ((4 * WIN, TILES * LANES), BF),
            ((4 * WIN, TILES * LANES), BF), ((own, 64, 4 * WIN), F32),
            ((own, 16, 32), F32), ((own * 16, 32), F32),
        ],
        half_1, x, hid, logits, w_deconv, w_mask.T, bias,
        jnp.asarray(places, BF), jnp.asarray(places.transpose(0, 2, 1), BF), jnp.pad(cond.T, ((0, 16 - COND), (0, 0))),
    )
    groups = lax.axis_size("clip")
    routes = [[(i, (i + step) % groups) for i in range(groups)] for step in range(1, groups)]
    strip_hids = [strip_hid] + [lax.ppermute(strip_hid, "clip", route) for route in routes]
    every_sum = exchange(sent, both)
    every_sum, strip_hids[1] = lax.optimization_barrier((every_sum, strip_hids[1]))
    every_sum = every_sum.reshape(-1, items, 2 * LANES)
    d_sum = lax.dynamic_index_in_dim(every_sum, lax.axis_index("clip"), 0, False)
    back_fc = jnp.einsum("mn,jnk->mjk", d_sum, k_fc, preferred_element_type=F32).astype(BF)
    back_fc = exchange(back_fc.reshape(count, own, 16, LANES), "row")
    back_fc, strip_hids[3] = lax.optimization_barrier((back_fc, strip_hids[3]))
    swap = [(index, index ^ 1) for index in range(count)]

    keep, d_enc, lines = call(
        backward_kernel,
        0.1,
        [((own + 1, TILES, 4 * C, LANES), BF), ((own + 1, TILES, C, LANES), F32), ((4 * C, LANES), F32)],
        [
            ((8, 4 * C, LANES), BF), ((TILES, C, LANES), F32), ((TILES, C, LANES), F32),
            ((KS * 2 * C, KS * 4 * C), BF), ((TILES, 7 * C, LANES), F32), ((TILES, 7 * C, LANES), F32),
            ((steps, TILES, 4 * C, LANES), F32), (cells, F32), (None, (2, steps)),
        ],
        half_1, act, cell, dec, lax.ppermute(dec, "row", swap), back_fc, lax.ppermute(back_fc, "row", swap), w_lstm,
        far_in=(0, 1),
    )
    block, d_fc = call(
        pack_kernel,
        12,
        [((devices, PART, LANES), BF), ((w_fc.size // LANES, LANES), F32)],
        [
            ((6, 48, LANES), BF), ((6, 48, LANES), BF), ((8, KS * 2 * C, LANES), BF), ((8, KS * 2 * C, LANES), BF),
            ((C, WIN), F32), ((11 * C + 64, LANES), F32),
            ((ROWS, LANES), F32), ((groups,) + strip_hid.shape, BF), ((w_fc.size // LANES, LANES), F32),
            ((2 * LANES, groups * items), BF), (None, (1 + groups,)),
        ],
        jnp.stack([half, lax.axis_index("clip")]).astype(jnp.int32), x, enc, hid, keep, d_enc, lines, head_sums, d_dec, d_mask, d_cond, d_logit, every_sum,
        wide_enc, bias,
        jnp.asarray(vector_places(), BF), jnp.asarray(np.pad(encoder, ((0, 0), (0, LANES - KK * 3))), F32), *strip_hids,
        far_in=tuple(range(16, 16 + groups)), far_out=(1,),
    )
    sums, scalars = pl.pallas_call(
        total_kernel,
        out_shape=[jax.ShapeDtypeStruct(block.shape, BF), jax.ShapeDtypeStruct((1, LANES), F32)],
        in_specs=[VMEM_SPEC],
        out_specs=[VMEM_SPEC, VMEM_SPEC],
        compiler_params=pltpu.CompilerParams(vmem_limit_bytes=VMEM_BYTES),
    )(exchange(block, both))
    sums = exchange(sums, both)
    rates = learning_rates(w_fc.shape[0] * count)

    def shown(group):
        enc, lstm, fc, cond, dec, mask, line = group
        fc = fc.reshape(2, NK * KK, WB * C // LANES, LANES)
        fc = jnp.transpose(fc, (1, 2, 0, 3)).reshape(-1, LANES)
        return [enc.T, lstm, fc, cond, dec, mask.T, line]

    def back(group):
        enc, lstm, fc, cond, dec, mask, line = group
        fc = fc.reshape(NK * KK, WB * C // LANES, 2, LANES)
        fc = jnp.transpose(fc, (2, 0, 1, 3)).reshape(w_fc.shape)
        return [enc.T, lstm, fc, cond, dec, mask.T, line]

    weights = shown([w_enc, w_lstm, w_fc, w_cond, w_deconv, w_mask, vector])
    firsts = shown([m_enc, m_lstm, m_fc, m_cond, m_deconv, m_mask, m_vector])
    seconds = shown([v_enc, v_lstm, v_fc, v_cond, v_deconv, v_mask, v_vector])
    shapes = [jax.ShapeDtypeStruct(value.shape, F32) for value in weights]
    places_out = [VMEM_SPEC, ANY_SPEC, ANY_SPEC] + [VMEM_SPEC] * 4
    new = pl.pallas_call(
        functools.partial(update_kernel, rates),
        out_shape=[jax.ShapeDtypeStruct((), F32)] + shapes * 3,
        in_specs=[VMEM_SPEC, VMEM_SPEC, ANY_SPEC] + places_out * 3,
        out_specs=[SMEM_SPEC] + places_out * 3,
        scratch_shapes=[
            pltpu.VMEM((ROWS, LANES), F32), pltpu.VMEM((3,) + shapes[2].shape, F32),
            pltpu.VMEM((3,) + shapes[1].shape, F32), pltpu.SemaphoreType.DMA((21,)),
            pltpu.VMEM((4,) + shapes[2].shape, F32), pltpu.VMEM((3,) + shapes[1].shape, F32),
            pltpu.SemaphoreType.DMA((26,)),
        ],
        compiler_params=pltpu.CompilerParams(vmem_limit_bytes=VMEM_BYTES),
    )(sums, scalars, d_fc, *weights, *firsts, *seconds)
    outs = [scalars[0, 0], scalars[0, 1], new[0]]
    for kind in range(3):
        outs.extend(back(new[1 + 7 * kind : 8 + 7 * kind]))
    return tuple(outs)


def shards(frames, *rest):
    clips, _, _, strip_rows, width = frames.shape
    count = lax.axis_size("row")
    one_clip = strip_rows * count // 2 == TILES * BANDS and width // 2 == WB
    devices = lax.axis_size(("clip", "row"))
    even = ROW_DEC % devices == 0 and SMALL % devices == 0
    if one_clip and clips * HALVES == count and even and (ROW_DEC + 2 * SMALL) // devices + 3 <= PART:
        return whole_clips(frames, *rest)
    return strips(frames, *rest)


def solution(mesh):
    placed = (
        P("clip", None, None, "row", None),
        P("clip", None, "row", None),
        P("clip", None, None),
        P("clip", None, None),
        P("clip", None, None),
        P("clip", None),
        P(),
        P(),
        P("row", None, None),
        P(),
        P(),
        P(),
        P(),
        P(),
        P(),
        P("row", None, None),
        P(),
        P(),
        P(),
        P(),
        P(),
        P(),
        P("row", None, None),
        P(),
        P(),
        P(),
        P(),
    )
    return jax.shard_map(
        shards,
        mesh=mesh,
        in_specs=placed,
        out_specs=(
            P(),
            P(),
            P(),
            P(),
            P(),
            P("row", None, None),
            P(),
            P(),
            P(),
            P(),
            P(),
            P(),
            P("row", None, None),
            P(),
            P(),
            P(),
            P(),
            P(),
            P(),
            P("row", None, None),
            P(),
            P(),
            P(),
            P(),
        ),
        check_vma=False,
    )
```
